512 devices in a mesh: sample: 8 (over z), ctx: 16 (over y, core), head: 4 (over x).
Axes of the slice: x: 4, y: 8, z: 8, core: 2. Of those that a mesh axis runs over, the one named last changes fastest.
Arguments:
- prompt_query: bfloat16 [2048, 32, 128], P(('sample', 'ctx'), 'head'), may hold values from -1.5 to 1.5
- prompt_key: bfloat16 [2048, 32, 128], P(('sample', 'ctx'), 'head'), may hold values from -1.5 to 1.5
- prompt_value: bfloat16 [2048, 32, 128], P(('sample', 'ctx'), 'head'), may hold values from -1.5 to 1.5
- prompt_grad: bfloat16 [2048, 32, 128], P(('sample', 'ctx'), 'head'), may hold values from -6 to 6
- prompt_decay: float32 [32, 2048], P('head', ('sample', 'ctx')), may hold values from -1 to 0, as said below
- reply_query: bfloat16 [8, 2048, 32, 128], P('sample', 'ctx', 'head'), may hold values from -1.5 to 1.5
- reply_key: bfloat16 [8, 2048, 32, 128], P('sample', 'ctx', 'head'), may hold values from -1.5 to 1.5
- reply_value: bfloat16 [8, 2048, 32, 128], P('sample', 'ctx', 'head'), may hold values from -1.5 to 1.5
- reply_grad: bfloat16 [8, 2048, 32, 128], P('sample', 'ctx', 'head'), may hold values from -6 to 6
- reply_decay: float32 [8, 32, 2048], P('sample', 'head', 'ctx'), may hold values from -1 to 0, as said below
- reply_lengths: int32 [8], P('sample'), may hold values from 1 to 2048, 10240 in all
- norm_gain: bfloat16 [32, 128], P('head'), may hold values from 0.099609375 to 1.8984375
Outputs:
- prompt_query_grad: bfloat16 [2048, 32, 128], P(('sample', 'ctx'), 'head')
- prompt_key_grad: bfloat16 [2048, 32, 128], P(('sample', 'ctx'), 'head')
- prompt_value_grad: bfloat16 [2048, 32, 128], P(('sample', 'ctx'), 'head')
- reply_query_grad: bfloat16 [8, 2048, 32, 128], P('sample', 'ctx', 'head')
- reply_key_grad: bfloat16 [8, 2048, 32, 128], P('sample', 'ctx', 'head')
- reply_value_grad: bfloat16 [8, 2048, 32, 128], P('sample', 'ctx', 'head')
The draws below stay inside these ranges and needn't reach their ends.
Inputs may be any that keep to these rules, and one draw needn't show every extreme that they name: `reply_lengths`: each response's length in tokens; the longest is exactly 2048. `prompt_decay`: never positive. `reply_decay`: never positive.
All inputs are finite; a program needn't handle non-finite values. No bound on the sum of `reply_lengths` on one device may be relied on, other than what follows from the above.
Results may differ from the reference program's by a relative error of at most 0.0051.
Values sent between devices are 32-bit elements; how exact they have to be, the bound alone decides.
No kernel may reach another device: no remote copies, remote signals or barrier semaphores. Data moves between devices by JAX's collectives and lax.ppermute only.
A program may use at most 128 MiB of HBM per device.

```python
import math
import jax
import jax.numpy as jnp
import numpy as np
from jax import lax

DK = 128
H = 32
CH = 128
PR_DEV = 16
R = 8
LMAX = 2048
P_SIZE = 2048
N_SAMPLE = 8
N_CTX = 16


def head_rates(key, share):
    key = jax.random.fold_in(key, 101)
    pick_key, slow_key, fast_key = jax.random.split(key, 3)
    chain_length = float(P_SIZE + LMAX)
    slow_heads = jax.random.uniform(pick_key, (H,)) < share
    slow_rate = jax.random.uniform(slow_key, (H,), minval=0.1, maxval=0.6) / chain_length
    fast_rate = jnp.exp(jax.random.uniform(fast_key, (H,), minval=jnp.log(1.0 / 50.0), maxval=jnp.log(1.0 / 30.0)))
    return jnp.where(slow_heads, slow_rate, fast_rate)


def log_decay(key, decay_speeds, array_dimensions):
    dispersion_key, surge_random_key, level_random_key = jax.random.split(key, 3)
    chain_length = float(P_SIZE + LMAX)
    multipliers = jax.random.uniform(dispersion_key, array_dimensions, minval=0.4, maxval=1.6)
    surge_amounts = jax.random.uniform(surge_random_key, array_dimensions) < 3.0 / chain_length
    nesting_levels = -jnp.log1p(-jax.random.uniform(level_random_key, array_dimensions, minval=0.2, maxval=0.5))
    return (-decay_speeds * multipliers - jnp.where(surge_amounts, nesting_levels, 0.0)).astype(jnp.float32)


def draw_prompt_decay(key, part):
    share = 0.5
    decay_speeds = head_rates(key, share)
    key = jax.random.fold_in(key, 1)
    return log_decay(key, decay_speeds[:, None], (H, P_SIZE))


def draw_reply_decay(key, part):
    share = 0.5
    decay_speeds = head_rates(key, share)
    key = jax.random.fold_in(key, 2)
    return log_decay(key, decay_speeds[None, :, None], (R, H, LMAX))


def block_scale(rng, shape, cuts, smallest, largest):
    factor_of = 1.0
    for axis_at, shards_of in cuts:
        heights = jax.random.uniform(jax.random.fold_in(jax.random.fold_in(rng, 6), axis_at), (shards_of,), jnp.float32, smallest / len(cuts), largest / len(cuts))
        factor_of = factor_of * jnp.repeat(jnp.exp(heights), shape[axis_at] // shards_of).reshape((-1,) + (1,) * (len(shape) - 1 - axis_at))
    return factor_of


def profile(number_of, total, reach, slope):
    portions = [(1 << 20) // math.isqrt(standing ** slope) + 1 for standing in range(2, number_of + 1)]
    rest, holding = total - reach - (number_of - 1), [1] * (number_of - 1)
    while rest > 0:
        free = [i for i in range(number_of - 1) if holding[i] < reach]
        whole, budget = sum([portions[i] for i in free]), rest
        for i in free:
            extra = min(reach - holding[i], max(1, budget * portions[i] // whole), rest)
            holding[i] = holding[i] + extra
            rest = rest - extra
    return np.array([reach] + holding)


def ragged(own_key, count, total, reach, lean):
    if count == 2:
        one = jax.random.randint(own_key, (), max(1, total - reach), min(reach, total - 1) + 1)
        return jnp.stack([one, total - one])
    tallies = jnp.asarray(profile(count, total, reach, lean), jnp.int32)
    couples = (count - 1) // 2
    giver, sink = tallies[1:1 + 2 * couples:2], tallies[2:2 + 2 * couples:2]
    margin = jnp.minimum(giver - 1, reach - sink)
    passed = jax.random.randint(jax.random.fold_in(own_key, 1), (couples,), 0, 1 << 20) % (margin + 1)
    tallies = tallies.at[1:1 + 2 * couples:2].set(giver - passed).at[2:2 + 2 * couples:2].set(sink + passed)
    return tallies[jax.random.permutation(jax.random.fold_in(own_key, 2), count)]


def centred(rng, shape, scale, bound, shards=(), kind=jnp.bfloat16):
    entries = jax.random.normal(rng, shape, jnp.float32) * scale
    if len(shards) > 0:
        entries = block_scale(rng, shape, shards, -0.22, 0.18) * entries
    return jnp.clip(entries, min=-bound, max=bound).astype(kind)


def setup_inputs(seed: int = 0) -> dict:
    streams_of = jax.random.split(jax.random.key(seed), 13)
    prompt_query = centred(streams_of[0], (P_SIZE, H, DK), 0.25, 1.5, ((0, 128), (1, 4)))
    prompt_key = centred(streams_of[1], (P_SIZE, H, DK), 0.25, 1.5, ((0, 128), (1, 4)))
    prompt_value = centred(streams_of[2], (P_SIZE, H, DK), 0.25, 1.5, ((0, 128), (1, 4)))
    prompt_grad = centred(streams_of[3], (P_SIZE, H, DK), 1.0, 6.0, ((0, 128), (1, 4)))
    prompt_decay = draw_prompt_decay(jax.random.fold_in(streams_of[12], 71), 0)
    reply_query = centred(streams_of[5], (R, LMAX, H, DK), 0.25, 1.5, ((0, 8), (1, 16), (2, 4)))
    reply_key = centred(streams_of[6], (R, LMAX, H, DK), 0.25, 1.5, ((0, 8), (1, 16), (2, 4)))
    reply_value = centred(streams_of[7], (R, LMAX, H, DK), 0.25, 1.5, ((0, 8), (1, 16), (2, 4)))
    reply_grad = centred(streams_of[8], (R, LMAX, H, DK), 1.0, 6.0, ((0, 8), (1, 16), (2, 4)))
    reply_decay = draw_reply_decay(jax.random.fold_in(streams_of[12], 71), 0)
    reply_lengths = ragged(streams_of[10], R, R * LMAX * 5 // 8, LMAX, 2).astype(jnp.int32)
    norm_gain = jnp.clip(1.0 + 0.18 * jax.random.normal(streams_of[11], (H, DK), jnp.float32), 0.099609375, 1.8984375).astype(jnp.bfloat16)
    return dict(prompt_query=prompt_query, prompt_key=prompt_key, prompt_value=prompt_value, prompt_grad=prompt_grad, prompt_decay=prompt_decay, reply_query=reply_query, reply_key=reply_key, reply_value=reply_value, reply_grad=reply_grad, reply_decay=reply_decay, reply_lengths=reply_lengths, norm_gain=norm_gain)


HIGH = lax.Precision.HIGHEST
EPSILON = 1e-05

def as_float(array):
    return array.astype(jnp.float32)

def decay_mask(running):
    extent = running.shape[1]
    row_ids = lax.broadcasted_iota(jnp.int32, (extent, extent), 0)
    col_ids = lax.broadcasted_iota(jnp.int32, (extent, extent), 1)
    causal = (row_ids >= col_ids)[None]
    spread = running[:, :, None] - running[:, None, :]
    return jnp.where(causal, jnp.exp(jnp.where(causal, spread, 0.0)), 0.0)

def out_weights(queries, key_rows, running):
    masking = decay_mask(running)
    scores = jnp.einsum('thd,shd->hts', as_float(queries), as_float(key_rows), precision=HIGH)
    return (masking, (scores * masking).astype(jnp.bfloat16))

def grad_mix(out_grad, values, masking):
    inner = jnp.einsum('thd,shd->hts', as_float(out_grad), as_float(values), precision=HIGH)
    return (inner * masking).astype(jnp.bfloat16)

def front_pass(queries, key_rows, values, running, state_in):
    masking, weights = out_weights(queries, key_rows, running)
    carried = jnp.einsum('thd,hde->the', as_float(queries), state_in, precision=HIGH)
    local = jnp.einsum('hts,she->the', as_float(weights), as_float(values), precision=HIGH)
    return (masking, weights, local + jnp.exp(running).T[:, :, None] * carried)

def forward_summary(key_rows, values, running):
    to_end = jnp.exp(running[:, -1:] - running)
    weighted = as_float(key_rows) * to_end.T[:, :, None]
    summary = jnp.einsum('thd,the->hde', weighted, as_float(values), precision=HIGH)
    return (jnp.exp(running[:, -1]), summary)

def norm_back(outputs, upstream, squares, intersection, features):
    inverse = lax.rsqrt(squares / features + EPSILON)
    project = intersection * inverse * inverse / features
    return ((upstream - outputs * project[:, None, None]) * inverse[:, None, None]).astype(jnp.bfloat16)

def back_left(queries, key_rows, values, out_grad, running, masking, state_in):
    grad_weights = grad_mix(out_grad, values, masking)
    carried = jnp.einsum('the,hde->thd', as_float(out_grad), state_in, precision=HIGH)
    local = jnp.einsum('hts,shd->thd', as_float(grad_weights), as_float(key_rows), precision=HIGH)
    query_grad = (local + jnp.exp(running).T[:, :, None] * carried).astype(jnp.bfloat16)
    weighted = as_float(queries) * jnp.exp(running).T[:, :, None]
    back_state = jnp.einsum('thd,the->hde', weighted, as_float(out_grad), precision=HIGH)
    return (grad_weights, query_grad, back_state)

def back_right(queries, key_rows, values, out_grad, running, weights, grad_weights, adjoint):
    to_end = jnp.exp(running[:, -1:] - running).T[:, :, None]
    key_grad = jnp.einsum('hst,shd->thd', as_float(grad_weights), as_float(queries), precision=HIGH)
    key_grad = key_grad + to_end * jnp.einsum('the,hde->thd', as_float(values), adjoint, precision=HIGH)
    value_grad = jnp.einsum('hst,she->the', as_float(weights), as_float(out_grad), precision=HIGH)
    value_grad = value_grad + to_end * jnp.einsum('thd,hde->the', as_float(key_rows), adjoint, precision=HIGH)
    return (key_grad.astype(jnp.bfloat16), value_grad.astype(jnp.bfloat16))

def reference(prompt_query, prompt_key, prompt_value, prompt_grad, prompt_decay, reply_query, reply_key, reply_value, reply_grad, reply_decay, reply_lengths, norm_gain):
    blocks = N_SAMPLE * N_CTX
    features = float(H * DK)
    scale_gain = as_float(norm_gain)[None]

    def split_prompt(array):
        return array.reshape(blocks, PR_DEV, H, DK)
    prompt_items = (split_prompt(prompt_query), split_prompt(prompt_key), split_prompt(prompt_value), split_prompt(prompt_grad), prompt_decay.reshape(H, blocks, PR_DEV).transpose(1, 0, 2))

    def forward_step(state_in, item):
        queries, key_rows, values, upstream_raw, decay = item
        running = jnp.cumsum(decay, axis=1)
        masking, weights, outputs = front_pass(queries, key_rows, values, running, state_in)
        upstream = as_float(upstream_raw) * scale_gain
        out_grad = norm_back(outputs, upstream, lax.optimization_barrier(jnp.sum(outputs * outputs, axis=(1, 2))), lax.optimization_barrier(jnp.sum(upstream * outputs, axis=(1, 2))), features)
        grad_weights, query_grad, back_state = back_left(queries, key_rows, values, out_grad, running, masking, state_in)
        factor, summary = forward_summary(key_rows, values, running)
        return (factor[:, None, None] * state_in + summary, (query_grad, out_grad, factor, back_state))

    def backward_step(adjoint, item):
        queries, key_rows, values, out_grad, decay, factor, back_state = item
        running = jnp.cumsum(decay, axis=1)
        masking, weights = out_weights(queries, key_rows, running)
        grad_weights = grad_mix(out_grad, values, masking)
        key_grad, value_grad = back_right(queries, key_rows, values, out_grad, running, weights, grad_weights, adjoint)
        return (factor[:, None, None] * adjoint + back_state, (key_grad, value_grad))
    zero_state = jnp.zeros((H, DK, DK), jnp.float32)
    prompt_end, prompt_saved = lax.scan(forward_step, zero_state, prompt_items)
    prompt_qgrad, prompt_ograd, prompt_factor, prompt_back = prompt_saved

    def one_reply(item):
        queries, key_rows, values, upstream_raw, decay, length_one = item
        live = (jnp.arange(LMAX, dtype=jnp.int32) < length_one)[:, None, None]
        nothing = jnp.zeros((), jnp.bfloat16)

        def split_reply(array):
            return jnp.where(live, array, nothing).reshape(N_CTX, CH, H, DK)
        items = (split_reply(queries), split_reply(key_rows), split_reply(values), split_reply(upstream_raw), decay.reshape(H, N_CTX, CH).transpose(1, 0, 2))
        unused, saved = lax.scan(forward_step, prompt_end, items)
        query_grad, out_grad, factor, back_state = saved
        adjoint, grads = lax.scan(backward_step, zero_state, (items[0], items[1], items[2], out_grad, items[4], factor, back_state), reverse=True)
        return (query_grad.reshape(LMAX, H, DK), grads[0].reshape(LMAX, H, DK), grads[1].reshape(LMAX, H, DK), adjoint)
    reply_qgrad, reply_kgrad, reply_vgrad, adjoints = lax.map(one_reply, (reply_query, reply_key, reply_value, reply_grad, reply_decay, reply_lengths))
    total_adjoint = lax.optimization_barrier(jnp.sum(adjoints, axis=0))
    unused, prompt_grads = lax.scan(backward_step, total_adjoint, (prompt_items[0], prompt_items[1], prompt_items[2], prompt_ograd, prompt_items[4], prompt_factor, prompt_back), reverse=True)
    return (prompt_qgrad.reshape(P_SIZE, H, DK), prompt_grads[0].reshape(P_SIZE, H, DK), prompt_grads[1].reshape(P_SIZE, H, DK), reply_qgrad, reply_kgrad, reply_vgrad)
```

```python
import jax
import jax.numpy as jnp
from jax import lax
from jax.experimental import pallas as pl
from jax.experimental.pallas import tpu as pltpu
from jax.sharding import PartitionSpec as P

EPSILON = 1e-05
F32 = jnp.float32
BF16 = jnp.bfloat16
HEADS = 8
D = 128
HALF = D // 2
T = 128
PT = 16
CTX = 16
SAMPLE = 8
HEAD_AXIS = 4
ROW = CTX * PT
FEATURES = float(HEADS * HEAD_AXIS * D)


def iota(shape, axis):
    return lax.broadcasted_iota(jnp.int32, shape, axis)


def dot(a, b, ca, cb):
    return lax.dot_general(a, b, (((ca,), (cb,)), ((), ())), preferred_element_type=F32)


def split(x):
    high = x.astype(BF16)
    return high, (x - high.astype(F32)).astype(BF16)


def split3(x):
    high, rest = x.astype(BF16), None
    rest = x - high.astype(F32)
    mid = rest.astype(BF16)
    return high, mid, (rest - mid.astype(F32)).astype(BF16)


def dot_right(a, x, ca, cb):
    return sum(dot(a, part, ca, cb) for part in split(x))


def dot_left(x, b, ca, cb):
    return sum(dot(part, b, ca, cb) for part in split(x))


def low_lanes(rows):
    return iota((rows, D), 1) < HALF


def pack(x, half):
    top, bottom, low = x[0:8], x[8:16], low_lanes(8)
    if half == 0:
        return jnp.where(low, top, pltpu.roll(bottom, HALF, 1))
    return jnp.where(low, pltpu.roll(top, HALF, 1), bottom)


def unpack(first, second):
    low = low_lanes(8)
    top = jnp.where(low, first, pltpu.roll(second, HALF, 1))
    bottom = jnp.where(low, pltpu.roll(first, HALF, 1), second)
    return jnp.concatenate([top, bottom], axis=0)


def rows_of_half(x):
    both = jnp.stack([x[:, :, :HALF], x[:, :, HALF:]], axis=1)
    return both.reshape(ROW, HALF)


def packed_half(x):
    both = x.reshape(CTX, 2, 8, HALF)
    return jnp.concatenate([both[:, 0], both[:, 1]], axis=-1)


def running_rows(decay):
    upper = (iota((T, T), 0) <= iota((T, T), 1)).astype(BF16)
    return sum(dot(part, upper, 1, 0) for part in split3(decay))


def running_columns(decay):
    lower = (iota((T, T), 1) <= iota((T, T), 0)).astype(BF16)
    return sum(dot(lower, part, 1, 1) for part in split3(decay))


def masking(column, row):
    extent = row.shape[1]
    causal = iota((extent, extent), 0) >= iota((extent, extent), 1)
    return jnp.where(causal, jnp.exp(jnp.where(causal, column - row, 0.0)), 0.0)


def column_to_row(column):
    extent = column.shape[0]
    eye = iota((extent, max(extent, D)), 0) == iota((extent, max(extent, D)), 1)
    return jnp.sum(jnp.where(eye, column, 0.0), axis=0, keepdims=True)


def row_to_column(row, extent):
    eye = iota((extent, row.shape[1]), 0) == iota((extent, row.shape[1]), 1)
    return jnp.sum(jnp.where(eye, row, 0.0), axis=1, keepdims=True)


def live_tokens(lengths):
    return lax.axis_index("ctx") * T + iota((T, 1), 0) < lengths[0]


def prompt_send_kernel(key, value, decay, reply_decay, out, rows_k, rows_v):
    rows_k[...] = key[...].astype(F32).reshape(PT * HEADS, D)
    rows_v[...] = value[...].astype(F32).reshape(PT * HEADS, D)
    wide = jnp.concatenate([decay[...], jnp.zeros((HEADS, D - PT), F32)], axis=1)
    totals = jnp.sum(reply_decay[0], axis=1, keepdims=True)
    at = iota((8, D), 0)
    for h in range(HEADS):
        k = rows_k[pl.ds(h, PT, HEADS), :]
        v = rows_v[pl.ds(h, PT, HEADS), :]
        tail = jnp.where(at == 0, wide[h : h + 1], jnp.where(at == 1, totals[h : h + 1], 0.0))
        for half in range(2):
            out[2 * h + half, 0:16, :] = k
            out[2 * h + half, 16:24, :] = pack(v, half)
            out[2 * h + half, 24:32, :] = tail


def reply_send_kernel(lengths, key, value, decay, prompt_query, out, key_out, value_out, rows_k, rows_v, rows_q):
    rows_k[...] = key[0].astype(F32).reshape(T * HEADS, D)
    rows_v[...] = value[0].astype(F32).reshape(T * HEADS, D)
    rows_q[...] = prompt_query[...].astype(F32).reshape(PT * HEADS, D)
    live = live_tokens(lengths)
    columns = running_columns(decay[0])
    to_end = jnp.exp(columns[T - 1 : T, :] - columns)
    for h in range(HEADS):
        k = jnp.where(live, rows_k[pl.ds(h, T, HEADS), :], 0.0)
        v = jnp.where(live, rows_v[pl.ds(h, T, HEADS), :], 0.0).astype(BF16)
        key_out[h] = k.astype(BF16)
        value_out[h] = v
        state = dot_right(v, k * to_end[:, h : h + 1], 0, 0)
        q = rows_q[pl.ds(h, PT, HEADS), :]
        for half in range(2):
            out[2 * h + half, 0:64, :] = state[half * HALF : (half + 1) * HALF]
            out[2 * h + half, 64:80, :] = q


def reply_local_kernel(lengths, query, grad, key, value, decay, query_out, grad_out, weights_out, local_out, rows):
    live = live_tokens(lengths)
    lines = running_rows(decay[0])
    columns = running_columns(decay[0])
    rows[...] = query[0].astype(F32).reshape(T * HEADS, D)
    for h in range(HEADS):
        q = jnp.where(live, rows[pl.ds(h, T, HEADS), :], 0.0).astype(BF16)
        query_out[h] = q
        mask = masking(columns[:, h : h + 1], lines[h : h + 1])
        weights = (dot(q, key[h], 1, 1) * mask).astype(BF16)
        weights_out[h] = weights
        local_out[h] = dot(weights, value[h], 1, 0)
    rows[...] = grad[0].astype(F32).reshape(T * HEADS, D)
    for h in range(HEADS):
        grad_out[h] = jnp.where(live, rows[pl.ds(h, T, HEADS), :], 0.0).astype(BF16)


def prompt_row_kernel(received, out, key_out, value_out, column_out, line_out):
    k = received[:, 0:16, :].reshape(ROW, D)
    v = rows_of_half(received[:, 16:24, :]).astype(BF16)
    decay = received[:, 24, :]
    token_block, token_place = iota((ROW, CTX), 0) // PT, iota((ROW, D), 0) % PT
    block = iota((ROW, CTX), 1)
    parts = split3(decay)
    own = sum(dot((block == token_block).astype(BF16), part, 1, 0) for part in parts)
    before = sum(dot((block < token_block).astype(BF16), part, 1, 0) for part in parts)
    running = jnp.sum(before + jnp.where(iota((ROW, D), 1) <= token_place, own, 0.0), axis=1, keepdims=True)
    last = running[ROW - 1 : ROW]
    state = dot_right(v, k * jnp.exp(last - running), 0, 0)
    total = jnp.broadcast_to(last, (8, D))
    for s in range(SAMPLE):
        out[s, 0:64, :] = state
        out[s, 64:72, :] = total
    key_out[...] = k.astype(BF16)
    value_out[...] = v
    column_out[...] = jnp.broadcast_to(running, (ROW, D))
    line_out[...] = jnp.broadcast_to(column_to_row(running), (8, ROW))


def same_block():
    return iota((ROW, ROW), 0) // PT == iota((ROW, ROW), 1) // PT


def prompt_weights(q, k, mask):
    scores = dot(q, k, 1, 1) * mask
    high = scores.astype(BF16)
    low = jnp.where(same_block(), 0.0, scores - high.astype(F32)).astype(BF16)
    return high, low


def fold_kernel(rows_received, received, first, key, value, column, line, out, start_out, total_out, query_out):
    place = lax.axis_index("sample")
    end = jnp.zeros((HALF, D), F32)
    start = end
    for s in range(SAMPLE):
        start = jnp.where(place == s, end, start)
        total = rows_received[s, 64:65, :]
        total_out[s : s + 1, :] = total
        end = jnp.exp(total) * end + rows_received[s, 0:64, :]
    start_out[...] = start
    state = end
    for b in range(CTX):
        out[b, 0:64, :] = state
        state = jnp.exp(first[b, 25:26, :]) * state + received[b, 0:64, :]
    q = received[:, 64:80, :].reshape(ROW, D).astype(BF16)
    query_out[...] = q
    running = column[:, 0:1]
    weights = prompt_weights(q, key[...], masking(running, line[0:1, :]))
    v = value[...]
    outputs = sum(dot(part, v, 1, 0) for part in weights)
    outputs = outputs + jnp.exp(running) * dot_right(q, start, 1, 1)
    out[:, 64:72, :] = packed_half(outputs)


def output_kernel(received, query, local, grad, decay, gain, prompt_grad, out, output_out, prompt_out, rows):
    columns = jnp.exp(running_columns(decay[0]))
    scale = gain[...].astype(F32)
    rows[...] = prompt_grad[...].astype(F32).reshape(PT * HEADS, D)
    squares = jnp.zeros((T, D), F32)
    crossed = jnp.zeros((T, D), F32)
    prompt_squares = jnp.zeros((PT, D), F32)
    prompt_crossed = jnp.zeros((PT, D), F32)
    for h in range(HEADS):
        state = jnp.concatenate([received[2 * h, 0:64, :], received[2 * h + 1, 0:64, :]], axis=0)
        outputs = local[h] + columns[:, h : h + 1] * dot_right(query[h], state, 1, 1)
        output_out[h] = outputs
        upstream = grad[h].astype(F32) * scale[h : h + 1]
        squares = squares + outputs * outputs
        crossed = crossed + upstream * outputs
        outputs = unpack(received[2 * h, 64:72, :], received[2 * h + 1, 64:72, :])
        prompt_out[h] = outputs
        upstream = rows[pl.ds(h, PT, HEADS), :] * scale[h : h + 1]
        prompt_squares = prompt_squares + outputs * outputs
        prompt_crossed = prompt_crossed + upstream * outputs
    sums = [
        column_to_row(jnp.sum(part, axis=1, keepdims=True))
        for part in (squares, crossed, prompt_squares, prompt_crossed)
    ]
    at = iota((8, D), 0)
    tile = jnp.zeros((8, D), F32)
    for i, part in enumerate(sums):
        tile = jnp.where(at == i, part, tile)
    for x in range(HEAD_AXIS):
        out[x] = tile


def norm_terms(squares, crossed):
    inverse = lax.rsqrt(squares / FEATURES + EPSILON)
    return inverse, crossed * inverse * inverse / FEATURES


def grad_kernel(
    sums, outputs, prompt_outputs, query, grad, decay, gain, prompt_grad, out, grad_out, rows
):
    columns = jnp.exp(running_columns(decay[0]))
    scale = gain[...].astype(F32)
    rows[...] = prompt_grad[...].astype(F32).reshape(PT * HEADS, D)
    total = sums[0] + sums[1] + sums[2] + sums[3]
    inverse, project = norm_terms(row_to_column(total[0:1], T), row_to_column(total[1:2], T))
    prompt_inverse, prompt_project = norm_terms(row_to_column(total[2:3], PT), row_to_column(total[3:4], PT))
    for h in range(HEADS):
        upstream = grad[h].astype(F32) * scale[h : h + 1]
        out_grad = ((upstream - outputs[h] * project) * inverse).astype(BF16)
        grad_out[h] = out_grad
        back = dot_right(out_grad, query[h].astype(F32) * columns[:, h : h + 1], 0, 0)
        upstream = rows[pl.ds(h, PT, HEADS), :] * scale[h : h + 1]
        prompt_out_grad = ((upstream - prompt_outputs[h] * prompt_project) * prompt_inverse).astype(BF16).astype(F32)
        for half in range(2):
            out[2 * h + half, 0:64, :] = back[half * HALF : (half + 1) * HALF]
            out[2 * h + half, 64:72, :] = pack(prompt_out_grad, half)


def reply_back_kernel(
    received, out_grad, query, key, value, weights, decay, query_grad, key_local, value_local, rows
):
    lines = running_rows(decay[0])
    columns = running_columns(decay[0])
    scales = jnp.exp(columns)
    for h in range(HEADS):
        state = jnp.concatenate([received[2 * h, 0:64, :], received[2 * h + 1, 0:64, :]], axis=0)
        og = out_grad[h]
        mask = masking(columns[:, h : h + 1], lines[h : h + 1])
        mix = (dot(og, value[h], 1, 1) * mask).astype(BF16)
        rows[pl.ds(h, T, HEADS), :] = dot(mix, key[h], 1, 0) + scales[:, h : h + 1] * dot_right(og, state, 1, 0)
        key_local[h] = dot(mix, query[h], 0, 0)
        value_local[h] = dot(weights[h], og, 0, 0)
    query_grad[0] = rows[...].reshape(T, HEADS, D).astype(BF16)


def prompt_mix(og, v, mask):
    return split(dot(og, v, 1, 1) * mask)


def back_fold_kernel(
    received, first, start, totals, query, key, value, column, line, out, rows_out, grad_out
):
    adjoint = jnp.zeros((HALF, D), F32)
    for b in range(CTX - 1, -1, -1):
        out[b, 0:64, :] = adjoint
        adjoint = jnp.exp(first[b, 25:26, :]) * adjoint + received[b, 0:64, :]
    og = rows_of_half(received[:, 64:72, :]).astype(BF16)
    grad_out[...] = og
    running = column[:, 0:1]
    scale = jnp.exp(running)
    q = query[...]
    back = dot_right(og, q.astype(F32) * scale, 0, 0)
    place = lax.axis_index("sample")
    for s in range(SAMPLE):
        after = jnp.zeros((1, D), F32)
        between = after
        for other in range(s + 1, SAMPLE):
            after = after + totals[other : other + 1, :]
            between = between + jnp.where(other < place, totals[other : other + 1, :], 0.0)
        rows_out[s] = jnp.exp(after) * adjoint + jnp.where(place > s, jnp.exp(between), 0.0) * back
    mix = prompt_mix(og, value[...], masking(running, line[0:1, :]))
    k = key[...]
    query_grad = sum(dot(part, k, 1, 0) for part in mix) + scale * dot_right(og, start[...], 1, 0)
    out[:, 64:80, :] = query_grad.reshape(CTX, PT, D)


def prompt_back_kernel(rows_received, out_grad, query, key, value, column, line, out):
    adjoint = rows_received[0]
    for s in range(1, SAMPLE):
        adjoint = adjoint + rows_received[s]
    running = column[:, 0:1]
    to_end = jnp.exp(running[ROW - 1 : ROW] - running)
    mask = masking(running, line[0:1, :])
    q, k, v, og = query[...], key[...], value[...], out_grad[...]
    mix = prompt_mix(og, v, mask)
    key_grad = sum(dot(part, q, 0, 0) for part in mix) + to_end * dot_right(v, adjoint, 1, 0)
    weights = prompt_weights(q, k, mask)
    value_grad = sum(dot(part, og, 0, 0) for part in weights) + to_end * dot_right(k, adjoint, 1, 1)
    out[:, 0:16, :] = key_grad.reshape(CTX, PT, D)
    out[:, 16:24, :] = packed_half(value_grad)


def reply_end_kernel(received, key, value, key_local, value_local, decay, key_grad, value_grad, rows_k, rows_v):
    columns = running_columns(decay[0])
    to_end = jnp.exp(columns[T - 1 : T, :] - columns)
    for h in range(HEADS):
        adjoint = jnp.concatenate([received[2 * h, 0:64, :], received[2 * h + 1, 0:64, :]], axis=0)
        scale = to_end[:, h : h + 1]
        rows_k[pl.ds(h, T, HEADS), :] = key_local[h] + scale * dot_right(value[h], adjoint, 1, 0)
        rows_v[pl.ds(h, T, HEADS), :] = value_local[h] + scale * dot_right(key[h], adjoint, 1, 1)
    key_grad[0] = rows_k[...].reshape(T, HEADS, D).astype(BF16)
    value_grad[0] = rows_v[...].reshape(T, HEADS, D).astype(BF16)


def prompt_end_kernel(received, last, query_grad, key_grad, value_grad, rows_q, rows_k, rows_v):
    for h in range(HEADS):
        rows_q[pl.ds(h, PT, HEADS), :] = received[2 * h, 64:80, :] + received[2 * h + 1, 64:80, :]
        rows_k[pl.ds(h, PT, HEADS), :] = last[2 * h, 0:16, :] + last[2 * h + 1, 0:16, :]
        rows_v[pl.ds(h, PT, HEADS), :] = unpack(last[2 * h, 16:24, :], last[2 * h + 1, 16:24, :])
    query_grad[...] = rows_q[...].reshape(PT, HEADS, D).astype(BF16)
    key_grad[...] = rows_k[...].reshape(PT, HEADS, D).astype(BF16)
    value_grad[...] = rows_v[...].reshape(PT, HEADS, D).astype(BF16)


VMEM = pl.BlockSpec(memory_space=pltpu.VMEM)
SMEM = pl.BlockSpec(memory_space=pltpu.SMEM)
REPLY_ROWS = pltpu.VMEM((T * HEADS, D), F32)
PROMPT_ROWS = pltpu.VMEM((PT * HEADS, D), F32)
BY_HEAD = ((HEADS, T, D), BF16)
BY_HEAD_WIDE = ((HEADS, T, D), F32)
REPLY = ((1, T, HEADS, D), BF16)
PROMPT = ((PT, HEADS, D), BF16)


def run(kernel, outs, scratch, *operands, flops=0):
    specs = [SMEM if operand.dtype == jnp.int32 else VMEM for operand in operands]
    moved = sum(operand.size * operand.dtype.itemsize for operand in operands)
    return pl.pallas_call(
        kernel,
        out_shape=[jax.ShapeDtypeStruct(shape, kind) for shape, kind in outs],
        in_specs=specs,
        out_specs=[VMEM] * len(outs),
        scratch_shapes=scratch,
        compiler_params=pltpu.CompilerParams(vmem_limit_bytes=24 * 1024 * 1024),
        cost_estimate=pl.CostEstimate(flops=flops, bytes_accessed=2 * moved, transcendentals=0),
        name=kernel.__name__,
    )(*operands)


def exchange(x, axis):
    return lax.all_to_all(x, axis, 0, 0, tiled=True)


def shards(
    prompt_query,
    prompt_key,
    prompt_value,
    prompt_grad,
    prompt_decay,
    reply_query,
    reply_key,
    reply_value,
    reply_grad,
    reply_decay,
    reply_lengths,
    norm_gain,
):
    work = 8 * 2 * T * D * D
    (sent,) = run(
        prompt_send_kernel,
        [((CTX, 32, D), F32)],
        [PROMPT_ROWS, PROMPT_ROWS],
        prompt_key,
        prompt_value,
        prompt_decay,
        reply_decay,
    )
    first = exchange(sent, "ctx")
    sent, key, value = run(
        reply_send_kernel,
        [((CTX, 80, D), F32), BY_HEAD, BY_HEAD],
        [REPLY_ROWS, REPLY_ROWS, PROMPT_ROWS],
        reply_lengths,
        reply_key,
        reply_value,
        reply_decay,
        prompt_query,
        flops=2 * work,
    )
    blocks = exchange(sent, "ctx")
    sent, row_key, row_value, column, line = run(
        prompt_row_kernel,
        [
            ((SAMPLE, 72, D), F32),
            ((ROW, D), BF16),
            ((ROW, HALF), BF16),
            ((ROW, D), F32),
            ((8, ROW), F32),
        ],
        [],
        first,
    )
    rows = exchange(sent, "sample")
    query, grad, weights, local = run(
        reply_local_kernel,
        [BY_HEAD, BY_HEAD, BY_HEAD, BY_HEAD_WIDE],
        [REPLY_ROWS],
        reply_lengths,
        reply_query,
        reply_grad,
        key,
        value,
        reply_decay,
        flops=2 * work,
    )
    sent, start, totals, row_query = run(
        fold_kernel,
        [((CTX, 72, D), F32), ((HALF, D), F32), ((SAMPLE, D), F32), ((ROW, D), BF16)],
        [],
        rows,
        blocks,
        first,
        row_key,
        row_value,
        column,
        line,
    )
    states = exchange(sent, "ctx")
    sent, outputs, prompt_outputs = run(
        output_kernel,
        [((HEAD_AXIS, 8, D), F32), BY_HEAD_WIDE, ((HEADS, PT, D), F32)],
        [PROMPT_ROWS],
        states,
        query,
        local,
        grad,
        reply_decay,
        norm_gain,
        prompt_grad,
        flops=2 * work,
    )
    sums = exchange(sent, "head")
    sent, out_grad = run(
        grad_kernel,
        [((CTX, 72, D), F32), BY_HEAD],
        [PROMPT_ROWS],
        sums,
        outputs,
        prompt_outputs,
        query,
        grad,
        reply_decay,
        norm_gain,
        prompt_grad,
        flops=2 * work,
    )
    backs = exchange(sent, "ctx")
    reply_query_grad, key_local, value_local = run(
        reply_back_kernel,
        [REPLY, BY_HEAD_WIDE, BY_HEAD_WIDE],
        [REPLY_ROWS],
        states,
        out_grad,
        query,
        key,
        value,
        weights,
        reply_decay,
        flops=6 * work,
    )
    sent, sent_rows, row_grad = run(
        back_fold_kernel,
        [((CTX, 80, D), F32), ((SAMPLE, HALF, D), F32), ((ROW, HALF), BF16)],
        [],
        backs,
        first,
        start,
        totals,
        row_query,
        row_key,
        row_value,
        column,
        line,
    )
    rows = exchange(sent_rows, "sample")
    adjoints = exchange(sent, "ctx")
    (sent,) = run(
        prompt_back_kernel,
        [((CTX, 24, D), F32)],
        [],
        rows,
        row_grad,
        row_query,
        row_key,
        row_value,
        column,
        line,
    )
    last = exchange(sent, "ctx")
    reply_key_grad, reply_value_grad = run(
        reply_end_kernel,
        [REPLY, REPLY],
        [REPLY_ROWS, REPLY_ROWS],
        adjoints,
        key,
        value,
        key_local,
        value_local,
        reply_decay,
        flops=4 * work,
    )
    prompt_query_grad, prompt_key_grad, prompt_value_grad = run(
        prompt_end_kernel, [PROMPT, PROMPT, PROMPT], [PROMPT_ROWS] * 3, adjoints, last
    )
    return (
        prompt_query_grad,
        prompt_key_grad,
        prompt_value_grad,
        reply_query_grad,
        reply_key_grad,
        reply_value_grad,
    )


def solution(mesh):
    prompt = P(("sample", "ctx"), "head", None)
    reply = P("sample", "ctx", "head", None)
    in_specs = (
        (prompt,) * 4
        + (P("head", ("sample", "ctx")),)
        + (reply,) * 4
        + (P("sample", "head", "ctx"), P("sample"), P("head", None))
    )
    out_specs = (prompt,) * 3 + (reply,) * 3
    return jax.shard_map(shards, mesh=mesh, in_specs=in_specs, out_specs=out_specs, check_vma=False)
```

```python
import jax
import jax.numpy as jnp
from jax import lax
from jax.experimental import pallas as pl
from jax.experimental.pallas import tpu as pltpu
from jax.sharding import PartitionSpec as P

EPSILON = 1e-05
F32 = jnp.float32
BF16 = jnp.bfloat16
HEADS = 8
D = 128
HALF = D // 2
T = 128
PT = 16
CTX = 16
SAMPLE = 8
HEAD_AXIS = 4
ROW = CTX * PT
FEATURES = float(HEADS * HEAD_AXIS * D)


def iota(shape, axis):
    return lax.broadcasted_iota(jnp.int32, shape, axis)


def dot(a, b, ca, cb):
    return lax.dot_general(a, b, (((ca,), (cb,)), ((), ())), preferred_element_type=F32)


def split(x):
    high = x.astype(BF16)
    return high, (x - high.astype(F32)).astype(BF16)


def split3(x):
    high, rest = x.astype(BF16), None
    rest = x - high.astype(F32)
    mid = rest.astype(BF16)
    return high, mid, (rest - mid.astype(F32)).astype(BF16)


def dot_right(a, x, ca, cb):
    return sum(dot(a, part, ca, cb) for part in split(x))


def dot_left(x, b, ca, cb):
    return sum(dot(part, b, ca, cb) for part in split(x))


def low_lanes(rows):
    return iota((rows, D), 1) < HALF


def pack(x, half):
    top, bottom, low = x[0:8], x[8:16], low_lanes(8)
    if half == 0:
        return jnp.where(low, top, pltpu.roll(bottom, HALF, 1))
    return jnp.where(low, pltpu.roll(top, HALF, 1), bottom)


def unpack(first, second):
    low = low_lanes(8)
    top = jnp.where(low, first, pltpu.roll(second, HALF, 1))
    bottom = jnp.where(low, pltpu.roll(first, HALF, 1), second)
    return jnp.concatenate([top, bottom], axis=0)


def rows_of_half(x):
    both = jnp.stack([x[:, :, :HALF], x[:, :, HALF:]], axis=1)
    return both.reshape(ROW, HALF)


def packed_half(x):
    both = x.reshape(CTX, 2, 8, HALF)
    return jnp.concatenate([both[:, 0], both[:, 1]], axis=-1)


def running_rows(decay):
    upper = (iota((T, T), 0) <= iota((T, T), 1)).astype(BF16)
    return sum(dot(part, upper, 1, 0) for part in split3(decay))


def running_columns(decay):
    lower = (iota((T, T), 1) <= iota((T, T), 0)).astype(BF16)
    return sum(dot(lower, part, 1, 1) for part in split3(decay))


def masking(column, row):
    extent = row.shape[1]
    causal = iota((extent, extent), 0) >= iota((extent, extent), 1)
    return jnp.where(causal, jnp.exp(jnp.where(causal, column - row, 0.0)), 0.0)


def column_to_row(column):
    extent = column.shape[0]
    eye = iota((extent, max(extent, D)), 0) == iota((extent, max(extent, D)), 1)
    return jnp.sum(jnp.where(eye, column, 0.0), axis=0, keepdims=True)


def row_to_column(row, extent):
    eye = iota((extent, row.shape[1]), 0) == iota((extent, row.shape[1]), 1)
    return jnp.sum(jnp.where(eye, row, 0.0), axis=1, keepdims=True)


def live_tokens(lengths):
    return lax.axis_index("ctx") * T + iota((T, 1), 0) < lengths[0]


def send_kernel(
    lengths, key, value, decay, prompt_query, prompt_key, prompt_value, prompt_decay, out, key_out, value_out,
    rows_k, rows_v, prompt_q, prompt_k, prompt_v,
):
    rows_k[...] = key[0].astype(F32).reshape(T * HEADS, D)
    rows_v[...] = value[0].astype(F32).reshape(T * HEADS, D)
    prompt_q[...] = prompt_query[...].astype(F32).reshape(PT * HEADS, D)
    prompt_k[...] = prompt_key[...].astype(F32).reshape(PT * HEADS, D)
    prompt_v[...] = prompt_value[...].astype(F32).reshape(PT * HEADS, D)
    live = live_tokens(lengths)
    columns = running_columns(decay[0])
    to_end = jnp.exp(columns[T - 1 : T, :] - columns)
    wide = jnp.concatenate([prompt_decay[...], jnp.zeros((HEADS, D - PT), F32)], axis=1)
    totals = jnp.sum(decay[0], axis=1, keepdims=True)
    at = iota((8, D), 0)
    for h in range(HEADS):
        k = jnp.where(live, rows_k[pl.ds(h, T, HEADS), :], 0.0)
        v = jnp.where(live, rows_v[pl.ds(h, T, HEADS), :], 0.0).astype(BF16)
        key_out[h] = k.astype(BF16)
        value_out[h] = v
        state = dot_right(v, k * to_end[:, h : h + 1], 0, 0)
        tail = jnp.where(at == 0, wide[h : h + 1], jnp.where(at == 1, totals[h : h + 1], 0.0))
        q = prompt_q[pl.ds(h, PT, HEADS), :]
        k = prompt_k[pl.ds(h, PT, HEADS), :]
        v = prompt_v[pl.ds(h, PT, HEADS), :]
        for half in range(2):
            out[2 * h + half, 0:64, :] = state[half * HALF : (half + 1) * HALF]
            out[2 * h + half, 64:80, :] = k
            out[2 * h + half, 80:88, :] = pack(v, half)
            out[2 * h + half, 88:96, :] = tail
            out[2 * h + half, 96:104, :] = q[8 * half : 8 * half + 8]


def reply_local_kernel(lengths, query, grad, key, value, decay, query_out, grad_out, weights_out, local_out, rows):
    live = live_tokens(lengths)
    lines = running_rows(decay[0])
    columns = running_columns(decay[0])
    rows[...] = query[0].astype(F32).reshape(T * HEADS, D)
    for h in range(HEADS):
        q = jnp.where(live, rows[pl.ds(h, T, HEADS), :], 0.0).astype(BF16)
        query_out[h] = q
        mask = masking(columns[:, h : h + 1], lines[h : h + 1])
        weights = (dot(q, key[h], 1, 1) * mask).astype(BF16)
        weights_out[h] = weights
        local_out[h] = dot(weights, value[h], 1, 0)
    rows[...] = grad[0].astype(F32).reshape(T * HEADS, D)
    for h in range(HEADS):
        grad_out[h] = jnp.where(live, rows[pl.ds(h, T, HEADS), :], 0.0).astype(BF16)


def prompt_row_kernel(received, out, key_out, value_out, column_out, line_out, query_out):
    k = received[:, 64:80, :].reshape(ROW, D)
    v = rows_of_half(received[:, 80:88, :]).astype(BF16)
    decay = received[:, 88, :]
    token_block, token_place = iota((ROW, CTX), 0) // PT, iota((ROW, D), 0) % PT
    block = iota((ROW, CTX), 1)
    parts = split3(decay)
    own = sum(dot((block == token_block).astype(BF16), part, 1, 0) for part in parts)
    before = sum(dot((block < token_block).astype(BF16), part, 1, 0) for part in parts)
    running = jnp.sum(before + jnp.where(iota((ROW, D), 1) <= token_place, own, 0.0), axis=1, keepdims=True)
    last = running[ROW - 1 : ROW]
    state = dot_right(v, k * jnp.exp(last - running), 0, 0)
    total = jnp.broadcast_to(last, (8, D))
    for s in range(SAMPLE):
        out[s, 0:64, :] = state
        out[s, 64:72, :] = total
    key_out[...] = k.astype(BF16)
    value_out[...] = v
    column_out[...] = jnp.broadcast_to(running, (ROW, D))
    line_out[...] = jnp.broadcast_to(column_to_row(running), (8, ROW))
    query_out[...] = received[:, 96:104, :]


def same_block():
    return iota((ROW, ROW), 0) // PT == iota((ROW, ROW), 1) // PT


def prompt_weights(q, k, mask):
    scores = dot(q, k, 1, 1) * mask
    high = scores.astype(BF16)
    low = jnp.where(same_block(), 0.0, scores - high.astype(F32)).astype(BF16)
    return high, low


def second_core():
    return lax.axis_index("ctx") % 2 == 1


def prompt_local_kernel(own, other, key, value, column, line, query_out, local_out, high_out, low_out):
    second = second_core()
    first_half = jnp.where(second, other[...], own[...])
    second_half = jnp.where(second, own[...], other[...])
    q = jnp.concatenate([first_half, second_half], axis=1).reshape(ROW, D).astype(BF16)
    query_out[...] = q
    weights = prompt_weights(q, key[...], masking(column[:, 0:1], line[0:1, :]))
    v = value[...]
    local_out[...] = sum(dot(part, v, 1, 0) for part in weights)
    high_out[...], low_out[...] = weights


def fold_kernel(rows_received, received, query, local, column, out, start_out, total_out):
    place = lax.axis_index("sample")
    end = jnp.zeros((HALF, D), F32)
    start = end
    for s in range(SAMPLE):
        start = jnp.where(place == s, end, start)
        total = rows_received[s, 64:65, :]
        total_out[s : s + 1, :] = total
        end = jnp.exp(total) * end + rows_received[s, 0:64, :]
    start_out[...] = start
    state = end
    for b in range(CTX):
        out[b, 0:64, :] = state
        state = jnp.exp(received[b, 89:90, :]) * state + received[b, 0:64, :]
    outputs = local[...] + jnp.exp(column[:, 0:1]) * dot_right(query[...], start, 1, 1)
    out[:, 64:72, :] = packed_half(outputs)


def output_kernel(received, query, local, grad, decay, gain, prompt_grad, out, output_out, prompt_out, rows):
    columns = jnp.exp(running_columns(decay[0]))
    scale = gain[...].astype(F32)
    rows[...] = prompt_grad[...].astype(F32).reshape(PT * HEADS, D)
    squares = jnp.zeros((T, D), F32)
    crossed = jnp.zeros((T, D), F32)
    prompt_squares = jnp.zeros((PT, D), F32)
    prompt_crossed = jnp.zeros((PT, D), F32)
    for h in range(HEADS):
        state = jnp.concatenate([received[2 * h, 0:64, :], received[2 * h + 1, 0:64, :]], axis=0)
        outputs = local[h] + columns[:, h : h + 1] * dot_right(query[h], state, 1, 1)
        output_out[h] = outputs
        upstream = grad[h].astype(F32) * scale[h : h + 1]
        squares = squares + outputs * outputs
        crossed = crossed + upstream * outputs
        outputs = unpack(received[2 * h, 64:72, :], received[2 * h + 1, 64:72, :])
        prompt_out[h] = outputs
        upstream = rows[pl.ds(h, PT, HEADS), :] * scale[h : h + 1]
        prompt_squares = prompt_squares + outputs * outputs
        prompt_crossed = prompt_crossed + upstream * outputs
    sums = [
        column_to_row(jnp.sum(part, axis=1, keepdims=True))
        for part in (squares, crossed, prompt_squares, prompt_crossed)
    ]
    at = iota((8, D), 0)
    tile = jnp.zeros((8, D), F32)
    for i, part in enumerate(sums):
        tile = jnp.where(at == i, part, tile)
    for x in range(HEAD_AXIS):
        out[x] = tile


def norm_terms(squares, crossed):
    inverse = lax.rsqrt(squares / FEATURES + EPSILON)
    return inverse, crossed * inverse * inverse / FEATURES


def grad_kernel(sums, outputs, prompt_outputs, query, grad, decay, gain, prompt_grad, out, grad_out, rows):
    columns = jnp.exp(running_columns(decay[0]))
    scale = gain[...].astype(F32)
    rows[...] = prompt_grad[...].astype(F32).reshape(PT * HEADS, D)
    total = sums[0] + sums[1] + sums[2] + sums[3]
    inverse, project = norm_terms(row_to_column(total[0:1], T), row_to_column(total[1:2], T))
    prompt_inverse, prompt_project = norm_terms(row_to_column(total[2:3], PT), row_to_column(total[3:4], PT))
    for h in range(HEADS):
        upstream = grad[h].astype(F32) * scale[h : h + 1]
        out_grad = ((upstream - outputs[h] * project) * inverse).astype(BF16)
        grad_out[h] = out_grad
        back = dot_right(out_grad, query[h].astype(F32) * columns[:, h : h + 1], 0, 0)
        upstream = rows[pl.ds(h, PT, HEADS), :] * scale[h : h + 1]
        prompt_out_grad = ((upstream - prompt_outputs[h] * prompt_project) * prompt_inverse).astype(BF16).astype(F32)
        for half in range(2):
            out[2 * h + half, 0:64, :] = back[half * HALF : (half + 1) * HALF]
            out[2 * h + half, 64:72, :] = pack(prompt_out_grad, half)


def reply_back_kernel(
    received, out_grad, query, key, value, weights, decay, query_grad, key_local, value_local, rows
):
    lines = running_rows(decay[0])
    columns = running_columns(decay[0])
    scales = jnp.exp(columns)
    for h in range(HEADS):
        state = jnp.concatenate([received[2 * h, 0:64, :], received[2 * h + 1, 0:64, :]], axis=0)
        og = out_grad[h]
        mask = masking(columns[:, h : h + 1], lines[h : h + 1])
        mix = (dot(og, value[h], 1, 1) * mask).astype(BF16)
        rows[pl.ds(h, T, HEADS), :] = dot(mix, key[h], 1, 0) + scales[:, h : h + 1] * dot_right(og, state, 1, 0)
        key_local[h] = dot(mix, query[h], 0, 0)
        value_local[h] = dot(weights[h], og, 0, 0)
    query_grad[0] = rows[...].reshape(T, HEADS, D).astype(BF16)


def back_fold_kernel(received, first, totals, query, column, rows_out):
    adjoint = jnp.zeros((HALF, D), F32)
    for b in range(CTX - 1, -1, -1):
        adjoint = jnp.exp(first[b, 89:90, :]) * adjoint + received[b, 0:64, :]
    og = rows_of_half(received[:, 64:72, :]).astype(BF16)
    back = dot_right(og, query[...].astype(F32) * jnp.exp(column[:, 0:1]), 0, 0)
    place = lax.axis_index("sample")
    for s in range(SAMPLE):
        after = jnp.zeros((1, D), F32)
        between = after
        for other in range(s + 1, SAMPLE):
            after = after + totals[other : other + 1, :]
            between = between + jnp.where(other < place, totals[other : other + 1, :], 0.0)
        rows_out[s] = jnp.exp(after) * adjoint + jnp.where(place > s, jnp.exp(between), 0.0) * back


def prompt_mid_kernel(
    received, first, start, query, key, value, high, low, column, line,
    out, keep_out, swap_out, key_local, value_local,
):
    adjoint = jnp.zeros((HALF, D), F32)
    for b in range(CTX - 1, -1, -1):
        out[b] = adjoint
        adjoint = jnp.exp(first[b, 89:90, :]) * adjoint + received[b, 0:64, :]
    og = rows_of_half(received[:, 64:72, :]).astype(BF16)
    running = column[:, 0:1]
    mix = split(dot(og, value[...], 1, 1) * masking(running, line[0:1, :]))
    k, q = key[...], query[...]
    query_grad = sum(dot(part, k, 1, 0) for part in mix) + jnp.exp(running) * dot_right(og, start[...], 1, 0)
    query_grad = query_grad.reshape(CTX, PT, D)
    second = second_core()
    keep_out[...] = jnp.where(second, query_grad[:, 8:16], query_grad[:, 0:8])
    swap_out[...] = jnp.where(second, query_grad[:, 0:8], query_grad[:, 8:16])
    key_local[...] = sum(dot(part, q, 0, 0) for part in mix)
    value_local[...] = dot(high[...], og, 0, 0) + dot(low[...], og, 0, 0)


def prompt_back_kernel(rows_received, adjoints, keep, swapped, key_local, value_local, key, value, column, out):
    adjoint = rows_received[0]
    for s in range(1, SAMPLE):
        adjoint = adjoint + rows_received[s]
    running = column[:, 0:1]
    to_end = jnp.exp(running[ROW - 1 : ROW] - running)
    key_grad = key_local[...] + to_end * dot_right(value[...], adjoint, 1, 0)
    value_grad = value_local[...] + to_end * dot_right(key[...], adjoint, 1, 1)
    out[:, 0:64, :] = adjoints[...]
    out[:, 64:80, :] = key_grad.reshape(CTX, PT, D)
    out[:, 80:88, :] = packed_half(value_grad)
    out[:, 88:96, :] = keep[...] + swapped[...]


def end_kernel(
    received, key, value, key_local, value_local, decay,
    key_grad, value_grad, prompt_query_grad, prompt_key_grad, prompt_value_grad,
    rows_k, rows_v, prompt_q, prompt_k, prompt_v,
):
    columns = running_columns(decay[0])
    to_end = jnp.exp(columns[T - 1 : T, :] - columns)
    for h in range(HEADS):
        low, high = received[2 * h], received[2 * h + 1]
        adjoint = jnp.concatenate([low[0:64], high[0:64]], axis=0)
        scale = to_end[:, h : h + 1]
        rows_k[pl.ds(h, T, HEADS), :] = key_local[h] + scale * dot_right(value[h], adjoint, 1, 0)
        rows_v[pl.ds(h, T, HEADS), :] = value_local[h] + scale * dot_right(key[h], adjoint, 1, 1)
        prompt_k[pl.ds(h, PT, HEADS), :] = low[64:80] + high[64:80]
        prompt_v[pl.ds(h, PT, HEADS), :] = unpack(low[80:88], high[80:88])
        prompt_q[pl.ds(h, PT, HEADS), :] = jnp.concatenate([low[88:96], high[88:96]], axis=0)
    key_grad[0] = rows_k[...].reshape(T, HEADS, D).astype(BF16)
    value_grad[0] = rows_v[...].reshape(T, HEADS, D).astype(BF16)
    prompt_query_grad[...] = prompt_q[...].reshape(PT, HEADS, D).astype(BF16)
    prompt_key_grad[...] = prompt_k[...].reshape(PT, HEADS, D).astype(BF16)
    prompt_value_grad[...] = prompt_v[...].reshape(PT, HEADS, D).astype(BF16)


VMEM = pl.BlockSpec(memory_space=pltpu.VMEM)
SMEM = pl.BlockSpec(memory_space=pltpu.SMEM)
REPLY_ROWS = pltpu.VMEM((T * HEADS, D), F32)
PROMPT_ROWS = pltpu.VMEM((PT * HEADS, D), F32)
BY_HEAD = ((HEADS, T, D), BF16)
BY_HEAD_WIDE = ((HEADS, T, D), F32)
REPLY = ((1, T, HEADS, D), BF16)
PROMPT = ((PT, HEADS, D), BF16)


def run(kernel, outs, scratch, *operands, flops=0):
    specs = [SMEM if operand.dtype == jnp.int32 else VMEM for operand in operands]
    moved = sum(operand.size * operand.dtype.itemsize for operand in operands)
    return pl.pallas_call(
        kernel,
        out_shape=[jax.ShapeDtypeStruct(shape, kind) for shape, kind in outs],
        in_specs=specs,
        out_specs=[VMEM] * len(outs),
        scratch_shapes=scratch,
        compiler_params=pltpu.CompilerParams(vmem_limit_bytes=8 * 1024 * 1024),
        cost_estimate=pl.CostEstimate(flops=flops, bytes_accessed=2 * moved, transcendentals=0),
        name=kernel.__name__,
    )(*operands)


def exchange(x, axis):
    return lax.all_to_all(x, axis, 0, 0, tiled=True)


def swap_cores(x):
    return lax.ppermute(x, "ctx", [(i, i ^ 1) for i in range(CTX)])


def shards(
    prompt_query,
    prompt_key,
    prompt_value,
    prompt_grad,
    prompt_decay,
    reply_query,
    reply_key,
    reply_value,
    reply_grad,
    reply_decay,
    reply_lengths,
    norm_gain,
):
    work = 8 * 2 * T * D * D
    sent, key, value = run(
        send_kernel,
        [((CTX, 104, D), F32), BY_HEAD, BY_HEAD],
        [REPLY_ROWS] * 2 + [PROMPT_ROWS] * 3,
        reply_lengths,
        reply_key,
        reply_value,
        reply_decay,
        prompt_query,
        prompt_key,
        prompt_value,
        prompt_decay,
        flops=2 * work,
    )
    first = exchange(sent, "ctx")
    sent, row_key, row_value, column, line, half_query = run(
        prompt_row_kernel,
        [
            ((SAMPLE, 72, D), F32),
            ((ROW, D), BF16),
            ((ROW, HALF), BF16),
            ((ROW, D), F32),
            ((8, ROW), F32),
            ((CTX, 8, D), F32),
        ],
        [],
        first,
    )
    rows = exchange(sent, "sample")
    query, grad, weights, local = run(
        reply_local_kernel,
        [BY_HEAD, BY_HEAD, BY_HEAD, BY_HEAD_WIDE],
        [REPLY_ROWS],
        reply_lengths,
        reply_query,
        reply_grad,
        key,
        value,
        reply_decay,
        flops=2 * work,
    )
    row_query, row_local, row_high, row_low = run(
        prompt_local_kernel,
        [((ROW, D), BF16), ((ROW, HALF), F32), ((ROW, ROW), BF16), ((ROW, ROW), BF16)],
        [],
        half_query,
        swap_cores(half_query),
        row_key,
        row_value,
        column,
        line,
        flops=work,
    )
    sent, start, totals = run(
        fold_kernel,
        [((CTX, 72, D), F32), ((HALF, D), F32), ((SAMPLE, D), F32)],
        [],
        rows,
        first,
        row_query,
        row_local,
        column,
    )
    states = exchange(sent, "ctx")
    sent, outputs, prompt_outputs = run(
        output_kernel,
        [((HEAD_AXIS, 8, D), F32), BY_HEAD_WIDE, ((HEADS, PT, D), F32)],
        [PROMPT_ROWS],
        states,
        query,
        local,
        grad,
        reply_decay,
        norm_gain,
        prompt_grad,
        flops=2 * work,
    )
    sums = exchange(sent, "head")
    sent, out_grad = run(
        grad_kernel,
        [((CTX, 72, D), F32), BY_HEAD],
        [PROMPT_ROWS],
        sums,
        outputs,
        prompt_outputs,
        query,
        grad,
        reply_decay,
        norm_gain,
        prompt_grad,
        flops=2 * work,
    )
    backs = exchange(sent, "ctx")
    reply_query_grad, key_local, value_local = run(
        reply_back_kernel,
        [REPLY, BY_HEAD_WIDE, BY_HEAD_WIDE],
        [REPLY_ROWS],
        states,
        out_grad,
        query,
        key,
        value,
        weights,
        reply_decay,
        flops=6 * work,
    )
    (sent,) = run(back_fold_kernel, [((SAMPLE, HALF, D), F32)], [], backs, first, totals, row_query, column)
    rows = exchange(sent, "sample")
    adjoints, keep, swap, row_key_local, row_value_local = run(
        prompt_mid_kernel,
        [
            ((CTX, HALF, D), F32),
            ((CTX, 8, D), F32),
            ((CTX, 8, D), F32),
            ((ROW, D), F32),
            ((ROW, HALF), F32),
        ],
        [],
        backs,
        first,
        start,
        row_query,
        row_key,
        row_value,
        row_high,
        row_low,
        column,
        line,
        flops=work,
    )
    (sent,) = run(
        prompt_back_kernel,
        [((CTX, 96, D), F32)],
        [],
        rows,
        adjoints,
        keep,
        swap_cores(swap),
        row_key_local,
        row_value_local,
        row_key,
        row_value,
        column,
    )
    received = exchange(sent, "ctx")
    reply_key_grad, reply_value_grad, prompt_query_grad, prompt_key_grad, prompt_value_grad = run(
        end_kernel,
        [REPLY, REPLY, PROMPT, PROMPT, PROMPT],
        [REPLY_ROWS] * 2 + [PROMPT_ROWS] * 3,
        received,
        key,
        value,
        key_local,
        value_local,
        reply_decay,
        flops=4 * work,
    )
    return (
        prompt_query_grad,
        prompt_key_grad,
        prompt_value_grad,
        reply_query_grad,
        reply_key_grad,
        reply_value_grad,
    )


def solution(mesh):
    prompt = P(("sample", "ctx"), "head", None)
    reply = P("sample", "ctx", "head", None)
    in_specs = (
        (prompt,) * 4
        + (P("head", ("sample", "ctx")),)
        + (reply,) * 4
        + (P("sample", "head", "ctx"), P("sample"), P("head", None))
    )
    out_specs = (prompt,) * 3 + (reply,) * 3
    return jax.shard_map(shards, mesh=mesh, in_specs=in_specs, out_specs=out_specs, check_vma=False)
```

```python
import jax
import jax.numpy as jnp
from jax import lax
from jax.experimental import pallas as pl
from jax.experimental.pallas import tpu as pltpu
from jax.sharding import PartitionSpec as P

EPSILON = 1e-05
F32 = jnp.float32
BF16 = jnp.bfloat16
HEADS = 8
D = 128
HALF = D // 2
T = 128
PT = 16
CTX = 16
SAMPLE = 8
HEAD_AXIS = 4
ROW = CTX * PT
FEATURES = float(HEADS * HEAD_AXIS * D)


def iota(shape, axis):
    return lax.broadcasted_iota(jnp.int32, shape, axis)


def dot(a, b, ca, cb):
    return lax.dot_general(a, b, (((ca,), (cb,)), ((), ())), preferred_element_type=F32)


def split(x):
    high = x.astype(BF16)
    return high, (x - high.astype(F32)).astype(BF16)


def split3(x):
    high, rest = x.astype(BF16), None
    rest = x - high.astype(F32)
    mid = rest.astype(BF16)
    return high, mid, (rest - mid.astype(F32)).astype(BF16)


def dot_right(a, x, ca, cb):
    return sum(dot(a, part, ca, cb) for part in split(x))


def dot_left(x, b, ca, cb):
    return sum(dot(part, b, ca, cb) for part in split(x))


def low_lanes(rows):
    return iota((rows, D), 1) < HALF


def pack(x, half):
    top, bottom, low = x[0:8], x[8:16], low_lanes(8)
    if half == 0:
        return jnp.where(low, top, pltpu.roll(bottom, HALF, 1))
    return jnp.where(low, pltpu.roll(top, HALF, 1), bottom)


def unpack(first, second):
    low = low_lanes(8)
    top = jnp.where(low, first, pltpu.roll(second, HALF, 1))
    bottom = jnp.where(low, pltpu.roll(first, HALF, 1), second)
    return jnp.concatenate([top, bottom], axis=0)


def rows_of_half(x):
    both = jnp.stack([x[:, :, :HALF], x[:, :, HALF:]], axis=1)
    return both.reshape(ROW, HALF)


def packed_half(x):
    both = x.reshape(CTX, 2, 8, HALF)
    return jnp.concatenate([both[:, 0], both[:, 1]], axis=-1)


def running_rows(decay):
    upper = (iota((T, T), 0) <= iota((T, T), 1)).astype(BF16)
    return sum(dot(part, upper, 1, 0) for part in split3(decay))


def running_columns(decay):
    lower = (iota((T, T), 1) <= iota((T, T), 0)).astype(BF16)
    return sum(dot(lower, part, 1, 1) for part in split3(decay))


def masking(column, row):
    extent = row.shape[1]
    causal = iota((extent, extent), 0) >= iota((extent, extent), 1)
    return jnp.where(causal, jnp.exp(jnp.where(causal, column - row, 0.0)), 0.0)


def column_to_row(column):
    extent = column.shape[0]
    eye = iota((extent, max(extent, D)), 0) == iota((extent, max(extent, D)), 1)
    return jnp.sum(jnp.where(eye, column, 0.0), axis=0, keepdims=True)


def row_to_column(row, extent):
    eye = iota((extent, row.shape[1]), 0) == iota((extent, row.shape[1]), 1)
    return jnp.sum(jnp.where(eye, row, 0.0), axis=1, keepdims=True)


def live_tokens(lengths):
    return lax.axis_index("ctx") * T + iota((T, 1), 0) < lengths[0]


def start_copies(pairs, sems):
    copies = [pltpu.make_async_copy(source, target, sems.at[i]) for i, (source, target) in enumerate(pairs)]
    for copy in copies:
        copy.start()
    return copies


def send_kernel(
    lengths, key, value, decay, prompt_query, prompt_key, prompt_value, prompt_decay, out, key_out, value_out,
    key_in, value_in, decay_in, query_in, prompt_key_in, prompt_value_in, prompt_decay_in,
    rows_k, rows_v, prompt_q, prompt_k, prompt_v, sems,
):
    copies = start_copies(
        [
            (decay, decay_in),
            (prompt_decay, prompt_decay_in),
            (prompt_query, query_in),
            (prompt_key, prompt_key_in),
            (prompt_value, prompt_value_in),
            (value, value_in),
            (key, key_in),
        ],
        sems,
    )
    live = live_tokens(lengths)
    for copy in copies[:5]:
        copy.wait()
    columns = running_columns(decay_in[0])
    to_end = jnp.exp(columns[T - 1 : T, :] - columns)
    wide = jnp.concatenate([prompt_decay_in[...], jnp.zeros((HEADS, D - PT), F32)], axis=1)
    totals = jnp.sum(decay_in[0], axis=1, keepdims=True)
    at = iota((8, D), 0)
    prompt_q[...] = query_in[...].astype(F32).reshape(PT * HEADS, D)
    prompt_k[...] = prompt_key_in[...].astype(F32).reshape(PT * HEADS, D)
    prompt_v[...] = prompt_value_in[...].astype(F32).reshape(PT * HEADS, D)
    for h in range(HEADS):
        tail = jnp.where(at == 0, wide[h : h + 1], jnp.where(at == 1, totals[h : h + 1], 0.0))
        q = prompt_q[pl.ds(h, PT, HEADS), :]
        k = prompt_k[pl.ds(h, PT, HEADS), :]
        v = prompt_v[pl.ds(h, PT, HEADS), :]
        for half in range(2):
            out[2 * h + half, 64:80, :] = k
            out[2 * h + half, 80:88, :] = pack(v, half)
            out[2 * h + half, 88:96, :] = tail
            out[2 * h + half, 96:104, :] = q[8 * half : 8 * half + 8]
    for copy in copies[5:]:
        copy.wait()
    rows_v[...] = value_in[0].astype(F32).reshape(T * HEADS, D)
    rows_k[...] = key_in[0].astype(F32).reshape(T * HEADS, D)
    for h in range(HEADS):
        k = jnp.where(live, rows_k[pl.ds(h, T, HEADS), :], 0.0)
        v = jnp.where(live, rows_v[pl.ds(h, T, HEADS), :], 0.0).astype(BF16)
        key_out[h] = k.astype(BF16)
        value_out[h] = v
        state = dot_right(v, k * to_end[:, h : h + 1], 0, 0)
        for half in range(2):
            out[2 * h + half, 0:64, :] = state[half * HALF : (half + 1) * HALF]


def wide_columns(columns):
    return jnp.concatenate([columns, jnp.zeros((T, D - HEADS), F32)], axis=1)


def reply_local_kernel(
    lengths, query, grad, key, decay, gain, prompt_grad,
    query_out, grad_out, weights_out, growth_out, scale_out, upstream_out,
    query_in, grad_in, rows, rows_g, prompt_rows, sems,
):
    copies = start_copies([(query, query_in), (grad, grad_in)], sems)
    live = live_tokens(lengths)
    lines = running_rows(decay[0])
    columns = running_columns(decay[0])
    growth_out[...] = wide_columns(jnp.exp(columns))
    scale = gain[...].astype(F32)
    scale_out[...] = scale
    prompt_rows[...] = prompt_grad[...].astype(F32).reshape(PT * HEADS, D)
    for h in range(HEADS):
        upstream_out[h] = prompt_rows[pl.ds(h, PT, HEADS), :] * scale[h : h + 1]
    for copy in copies:
        copy.wait()
    rows[...] = query_in[0].astype(F32).reshape(T * HEADS, D)
    rows_g[...] = grad_in[0].astype(F32).reshape(T * HEADS, D)
    for h in range(HEADS):
        q = jnp.where(live, rows[pl.ds(h, T, HEADS), :], 0.0).astype(BF16)
        query_out[h] = q
        mask = masking(columns[:, h : h + 1], lines[h : h + 1])
        weights_out[h] = (dot(q, key[h], 1, 1) * mask).astype(BF16)
        grad_out[h] = jnp.where(live, rows_g[pl.ds(h, T, HEADS), :], 0.0).astype(BF16)


def prompt_row_kernel(received, out, column_out, query_out, blocks_out):
    decay = received[:, 88, :]
    token_block, token_place = iota((ROW, CTX), 0) // PT, iota((ROW, D), 0) % PT
    block = iota((ROW, CTX), 1)
    parts = split3(decay)
    own = sum(dot((block == token_block).astype(BF16), part, 1, 0) for part in parts)
    before = sum(dot((block < token_block).astype(BF16), part, 1, 0) for part in parts)
    running = jnp.sum(before + jnp.where(iota((ROW, D), 1) <= token_place, own, 0.0), axis=1, keepdims=True)
    last = running[ROW - 1 : ROW]
    k = received[:, 64:80, :].reshape(ROW, D)
    v = rows_of_half(received[:, 80:88, :]).astype(BF16)
    state = dot_right(v, k * jnp.exp(last - running), 0, 0)
    total = jnp.broadcast_to(last, (8, D))
    for s in range(SAMPLE):
        out[s, 0:64, :] = state
        out[s, 64:72, :] = total
    column_out[...] = jnp.broadcast_to(running, (ROW, D))
    query_out[...] = received[:, 96:104, :]
    blocks_out[...] = received[:, 89, :]


def same_block():
    return iota((ROW, ROW), 0) // PT == iota((ROW, ROW), 1) // PT


def prompt_weights(q, k, mask):
    scores = dot(q, k, 1, 1) * mask
    high = scores.astype(BF16)
    low = jnp.where(same_block(), 0.0, scores - high.astype(F32)).astype(BF16)
    return high, low


def second_core():
    return lax.axis_index("ctx") % 2 == 1


def prompt_local_kernel(
    received, other, column, query_out, key_out, value_out, line_out, local_out
):
    own = received[:, 96:104, :]
    second = second_core()
    first_half = jnp.where(second, other[...], own)
    second_half = jnp.where(second, own, other[...])
    q = jnp.concatenate([first_half, second_half], axis=1).reshape(ROW, D).astype(BF16)
    k = received[:, 64:80, :].reshape(ROW, D).astype(BF16)
    v = rows_of_half(received[:, 80:88, :]).astype(BF16)
    running = column[:, 0:1]
    line = column_to_row(running)
    query_out[...] = q
    key_out[...] = k
    value_out[...] = v
    line_out[...] = jnp.broadcast_to(line, (8, ROW))
    weights = prompt_weights(q, k, masking(running, line))
    local_out[...] = sum(dot(part, v, 1, 0) for part in weights)


def fold_kernel(rows_received, received, query, local, column, out, start_out, total_out):
    place = lax.axis_index("sample")
    end = jnp.zeros((HALF, D), F32)
    start = end
    for s in range(SAMPLE):
        start = jnp.where(place == s, end, start)
        total = rows_received[s, 64:65, :]
        total_out[s : s + 1, :] = total
        end = jnp.exp(total) * end + rows_received[s, 0:64, :]
    start_out[...] = start
    state = end
    for b in range(CTX):
        out[b, 0:64, :] = state
        state = jnp.exp(received[b, 89:90, :]) * state + received[b, 0:64, :]
    outputs = local[...] + jnp.exp(column[:, 0:1]) * dot_right(query[...], start, 1, 1)
    out[:, 64:72, :] = packed_half(outputs)


def output_kernel(
    received, query, weights, value, grad, growth, scale, prompt_upstream, out, output_out, prompt_out
):
    squares = jnp.zeros((T, D), F32)
    crossed = jnp.zeros((T, D), F32)
    prompt_squares = jnp.zeros((PT, D), F32)
    prompt_crossed = jnp.zeros((PT, D), F32)
    for h in range(HEADS):
        state = jnp.concatenate([received[2 * h, 0:64, :], received[2 * h + 1, 0:64, :]], axis=0)
        outputs = dot(weights[h], value[h], 1, 0) + growth[:, h : h + 1] * dot_right(query[h], state, 1, 1)
        output_out[h] = outputs
        upstream = grad[h].astype(F32) * scale[h : h + 1, :]
        squares = squares + outputs * outputs
        crossed = crossed + upstream * outputs
        outputs = unpack(received[2 * h, 64:72, :], received[2 * h + 1, 64:72, :])
        prompt_out[h] = outputs
        prompt_squares = prompt_squares + outputs * outputs
        prompt_crossed = prompt_crossed + prompt_upstream[h] * outputs
    sums = [
        column_to_row(jnp.sum(part, axis=1, keepdims=True))
        for part in (squares, crossed, prompt_squares, prompt_crossed)
    ]
    at = iota((8, D), 0)
    tile = jnp.zeros((8, D), F32)
    for i, part in enumerate(sums):
        tile = jnp.where(at == i, part, tile)
    for x in range(HEAD_AXIS):
        out[x] = tile


def norm_terms(squares, crossed):
    inverse = lax.rsqrt(squares / FEATURES + EPSILON)
    return inverse, crossed * inverse * inverse / FEATURES


def grad_kernel(
    sums, outputs, prompt_outputs, query, grad, growth, scale, prompt_upstream, out, grad_out
):
    total = sums[0] + sums[1] + sums[2] + sums[3]
    inverse, project = norm_terms(row_to_column(total[0:1], T), row_to_column(total[1:2], T))
    prompt_inverse, prompt_project = norm_terms(row_to_column(total[2:3], PT), row_to_column(total[3:4], PT))
    for h in range(HEADS):
        upstream = grad[h].astype(F32) * scale[h : h + 1, :]
        out_grad = ((upstream - outputs[h] * project) * inverse).astype(BF16)
        grad_out[h] = out_grad
        back = dot_right(out_grad, query[h].astype(F32) * growth[:, h : h + 1], 0, 0)
        prompt_out_grad = (prompt_upstream[h] - prompt_outputs[h] * prompt_project) * prompt_inverse
        prompt_out_grad = prompt_out_grad.astype(BF16).astype(F32)
        for half in range(2):
            out[2 * h + half, 0:64, :] = back[half * HALF : (half + 1) * HALF]
            out[2 * h + half, 64:72, :] = pack(prompt_out_grad, half)


def reply_back_kernel(
    received, out_grad, query, key, value, weights, decay, totals,
    query_grad, key_local, value_local, to_end_out, factors_out, rows,
):
    lines = running_rows(decay[0])
    columns = running_columns(decay[0])
    scales = jnp.exp(columns)
    to_end_out[...] = wide_columns(jnp.exp(columns[T - 1 : T, :] - columns))
    place = lax.axis_index("sample")
    for s in range(SAMPLE):
        after = jnp.zeros((1, D), F32)
        between = after
        for other in range(s + 1, SAMPLE):
            after = after + totals[other : other + 1, :]
            between = between + jnp.where(other < place, totals[other : other + 1, :], 0.0)
        factors_out[s : s + 1, :] = jnp.exp(after)
        factors_out[SAMPLE + s : SAMPLE + s + 1, :] = jnp.where(place > s, jnp.exp(between), 0.0)
    for h in range(HEADS):
        state = jnp.concatenate([received[2 * h, 0:64, :], received[2 * h + 1, 0:64, :]], axis=0)
        og = out_grad[h]
        mask = masking(columns[:, h : h + 1], lines[h : h + 1])
        mix = (dot(og, value[h], 1, 1) * mask).astype(BF16)
        rows[pl.ds(h, T, HEADS), :] = dot(mix, key[h], 1, 0) + scales[:, h : h + 1] * dot_right(og, state, 1, 0)
        key_local[h] = dot(mix, query[h], 0, 0)
        value_local[h] = dot(weights[h], og, 0, 0)
    query_grad[0] = rows[...].reshape(T, HEADS, D).astype(BF16)


def back_fold_kernel(received, blocks, factors, query, column, rows_out):
    adjoint = jnp.zeros((HALF, D), F32)
    for b in range(CTX - 1, -1, -1):
        adjoint = jnp.exp(blocks[b : b + 1, :]) * adjoint + received[b, 0:64, :]
    og = rows_of_half(received[:, 64:72, :]).astype(BF16)
    back = dot_right(og, query[...].astype(F32) * jnp.exp(column[:, 0:1]), 0, 0)
    for s in range(SAMPLE):
        rows_out[s] = factors[s : s + 1, :] * adjoint + factors[SAMPLE + s : SAMPLE + s + 1, :] * back


def prompt_mid_kernel(received, blocks, start, query, key, value, column, line, out, swap_out):
    adjoint = jnp.zeros((HALF, D), F32)
    for b in range(CTX - 1, -1, -1):
        out[b, 0:64, :] = adjoint
        adjoint = jnp.exp(blocks[b : b + 1, :]) * adjoint + received[b, 0:64, :]
    og = rows_of_half(received[:, 64:72, :]).astype(BF16)
    running = column[:, 0:1]
    mask = masking(running, line[0:1, :])
    mix = split(dot(og, value[...], 1, 1) * mask)
    k, q = key[...], query[...]
    query_grad = sum(dot(part, k, 1, 0) for part in mix) + jnp.exp(running) * dot_right(og, start[...], 1, 0)
    query_grad = query_grad.reshape(CTX, PT, D)
    second = second_core()
    swap_out[...] = jnp.where(second, query_grad[:, 0:8], query_grad[:, 8:16])
    key_local = sum(dot(part, q, 0, 0) for part in mix)
    value_local = sum(dot(part, og, 0, 0) for part in prompt_weights(q, k, mask))
    out[:, 64:80, :] = key_local.reshape(CTX, PT, D)
    out[:, 80:88, :] = packed_half(value_local)
    out[:, 88:96, :] = jnp.where(second, query_grad[:, 8:16], query_grad[:, 0:8])


def prompt_back_kernel(rows_received, swapped, key, value, column, message, out, part, sems):
    arrive = pltpu.make_async_copy(message.at[:, 64:96, :], part, sems.at[0])
    arrive.start()
    adjoint = rows_received[0]
    for s in range(1, SAMPLE):
        adjoint = adjoint + rows_received[s]
    running = column[:, 0:1]
    to_end = jnp.exp(running[ROW - 1 : ROW] - running)
    key_grad = to_end * dot_right(value[...], adjoint, 1, 0)
    value_grad = to_end * dot_right(key[...], adjoint, 1, 1)
    arrive.wait()
    part[:, 0:16, :] += key_grad.reshape(CTX, PT, D)
    part[:, 16:24, :] += packed_half(value_grad)
    part[:, 24:32, :] += swapped[...]
    leave = pltpu.make_async_copy(part, out.at[:, 64:96, :], sems.at[1])
    leave.start()
    leave.wait()


def end_kernel(
    received, key, value, key_local, value_local, to_end,
    key_grad, value_grad, prompt_query_grad, prompt_key_grad, prompt_value_grad,
    rows_k, rows_v, prompt_q, prompt_k, prompt_v,
):
    for h in range(HEADS):
        low, high = received[2 * h], received[2 * h + 1]
        adjoint = jnp.concatenate([low[0:64], high[0:64]], axis=0)
        scale = to_end[:, h : h + 1]
        rows_k[pl.ds(h, T, HEADS), :] = key_local[h] + scale * dot_right(value[h], adjoint, 1, 0)
        rows_v[pl.ds(h, T, HEADS), :] = value_local[h] + scale * dot_right(key[h], adjoint, 1, 1)
        prompt_k[pl.ds(h, PT, HEADS), :] = low[64:80] + high[64:80]
        prompt_v[pl.ds(h, PT, HEADS), :] = unpack(low[80:88], high[80:88])
        prompt_q[pl.ds(h, PT, HEADS), :] = jnp.concatenate([low[88:96], high[88:96]], axis=0)
    key_grad[0] = rows_k[...].reshape(T, HEADS, D).astype(BF16)
    value_grad[0] = rows_v[...].reshape(T, HEADS, D).astype(BF16)
    prompt_query_grad[...] = prompt_q[...].reshape(PT, HEADS, D).astype(BF16)
    prompt_key_grad[...] = prompt_k[...].reshape(PT, HEADS, D).astype(BF16)
    prompt_value_grad[...] = prompt_v[...].reshape(PT, HEADS, D).astype(BF16)


VMEM = pl.BlockSpec(memory_space=pltpu.VMEM)
SMEM = pl.BlockSpec(memory_space=pltpu.SMEM)
HBM = pl.BlockSpec(memory_space=pltpu.HBM)
REPLY_ROWS = pltpu.VMEM((T * HEADS, D), F32)
PROMPT_ROWS = pltpu.VMEM((PT * HEADS, D), F32)
BY_HEAD = ((HEADS, T, D), BF16)
BY_HEAD_WIDE = ((HEADS, T, D), F32)
REPLY = ((1, T, HEADS, D), BF16)
PROMPT = ((PT, HEADS, D), BF16)


def run(kernel, outs, scratch, *operands, hbm=(), hbm_outs=(), kept=(), far=(), aliases=None, flops=0):
    operands = [
        pltpu.with_memory_space_constraint(operand, pltpu.HBM) if i in hbm else operand
        for i, operand in enumerate(operands)
    ]
    specs = [
        SMEM if operand.dtype == jnp.int32 else HBM if i in hbm else VMEM for i, operand in enumerate(operands)
    ]
    moved = sum(operand.size * operand.dtype.itemsize for operand in operands)
    return pl.pallas_call(
        kernel,
        out_shape=[
            pltpu.VMEM(shape, kind)
            if i in kept
            else pltpu.HBM(shape, kind)
            if i in far
            else jax.ShapeDtypeStruct(shape, kind)
            for i, (shape, kind) in enumerate(outs)
        ],
        in_specs=specs,
        out_specs=[HBM if i in hbm_outs else VMEM for i in range(len(outs))],
        scratch_shapes=scratch,
        input_output_aliases=aliases or {},
        compiler_params=pltpu.CompilerParams(vmem_limit_bytes=8 * 1024 * 1024),
        cost_estimate=pl.CostEstimate(flops=flops, bytes_accessed=2 * moved, transcendentals=0),
        name=kernel.__name__,
    )(*operands)


def exchange(x, axis):
    return lax.all_to_all(x, axis, 0, 0, tiled=True)


def swap_cores(x):
    return lax.ppermute(x, "ctx", [(i, i ^ 1) for i in range(CTX)])


def shards(
    prompt_query,
    prompt_key,
    prompt_value,
    prompt_grad,
    prompt_decay,
    reply_query,
    reply_key,
    reply_value,
    reply_grad,
    reply_decay,
    reply_lengths,
    norm_gain,
):
    work = 8 * 2 * T * D * D
    reply_in, prompt_in = pltpu.VMEM(*REPLY), pltpu.VMEM(*PROMPT)
    sent, key, value = run(
        send_kernel,
        [((CTX, 104, D), F32), BY_HEAD, BY_HEAD],
        [reply_in, reply_in, pltpu.VMEM((1, HEADS, T), F32)]
        + [prompt_in] * 3
        + [pltpu.VMEM((HEADS, PT), F32)]
        + [REPLY_ROWS] * 2
        + [PROMPT_ROWS] * 3
        + [pltpu.SemaphoreType.DMA((7,))],
        reply_lengths,
        reply_key,
        reply_value,
        reply_decay,
        prompt_query,
        prompt_key,
        prompt_value,
        prompt_decay,
        hbm=range(1, 8),
        flops=2 * work,
        kept=(1, 2),
    )
    first = exchange(sent, "ctx")
    sent, column, half_query, blocks = run(
        prompt_row_kernel,
        [((SAMPLE, 72, D), F32), ((ROW, D), F32), ((CTX, 8, D), F32), ((CTX, D), F32)],
        [],
        first,
        kept=(1, 3),
    )
    rows = exchange(sent, "sample")
    query, grad, weights, growth, scale, prompt_upstream = run(
        reply_local_kernel,
        [BY_HEAD, BY_HEAD, BY_HEAD, ((T, D), F32), ((HEADS, D), F32), ((HEADS, PT, D), F32)],
        [reply_in, reply_in, REPLY_ROWS, REPLY_ROWS, PROMPT_ROWS, pltpu.SemaphoreType.DMA((2,))],
        reply_lengths,
        reply_query,
        reply_grad,
        key,
        reply_decay,
        norm_gain,
        prompt_grad,
        hbm=(1, 2),
        flops=2 * work,
        kept=range(6),
    )
    row_query, row_key, row_value, line, row_local = run(
        prompt_local_kernel,
        [
            ((ROW, D), BF16),
            ((ROW, D), BF16),
            ((ROW, HALF), BF16),
            ((8, ROW), F32),
            ((ROW, HALF), F32),
        ],
        [],
        first,
        swap_cores(half_query),
        column,
        flops=work,
        kept=range(5),
    )
    sent, start, totals = run(
        fold_kernel,
        [((CTX, 72, D), F32), ((HALF, D), F32), ((SAMPLE, D), F32)],
        [],
        rows,
        first,
        row_query,
        row_local,
        column,
        far=(1, 2),
    )
    states = exchange(sent, "ctx")
    sent, outputs, prompt_outputs = run(
        output_kernel,
        [((HEAD_AXIS, 8, D), F32), BY_HEAD_WIDE, ((HEADS, PT, D), F32)],
        [],
        states,
        query,
        weights,
        value,
        grad,
        growth,
        scale,
        prompt_upstream,
        flops=2 * work,
        kept=(1, 2),
    )
    sums = exchange(sent, "head")
    sent, out_grad = run(
        grad_kernel,
        [((CTX, 72, D), F32), BY_HEAD],
        [],
        sums,
        outputs,
        prompt_outputs,
        query,
        grad,
        growth,
        scale,
        prompt_upstream,
        flops=2 * work,
        far=(1,),
    )
    backs = exchange(sent, "ctx")
    reply_query_grad, key_local, value_local, to_end, factors = run(
        reply_back_kernel,
        [REPLY, BY_HEAD_WIDE, BY_HEAD_WIDE, ((T, D), F32), ((2 * SAMPLE, D), F32)],
        [REPLY_ROWS],
        states,
        out_grad,
        query,
        key,
        value,
        weights,
        reply_decay,
        totals,
        flops=6 * work,
        kept=(1, 2, 3, 4),
    )
    (sent,) = run(
        back_fold_kernel, [((SAMPLE, HALF, D), F32)], [], backs, blocks, factors, row_query, column
    )
    rows = exchange(sent, "sample")
    message, swap = run(
        prompt_mid_kernel,
        [((CTX, 96, D), F32), ((CTX, 8, D), F32)],
        [],
        backs,
        blocks,
        start,
        row_query,
        row_key,
        row_value,
        column,
        line,
        flops=work,
    )
    (sent,) = run(
        prompt_back_kernel,
        [((CTX, 96, D), F32)],
        [pltpu.VMEM((CTX, 32, D), F32), pltpu.SemaphoreType.DMA((2,))],
        rows,
        swap_cores(swap),
        row_key,
        row_value,
        column,
        message,
        hbm=(5,),
        hbm_outs=(0,),
        aliases={5: 0},
    )
    received = exchange(sent, "ctx")
    reply_key_grad, reply_value_grad, prompt_query_grad, prompt_key_grad, prompt_value_grad = run(
        end_kernel,
        [REPLY, REPLY, PROMPT, PROMPT, PROMPT],
        [REPLY_ROWS] * 2 + [PROMPT_ROWS] * 3,
        received,
        key,
        value,
        key_local,
        value_local,
        to_end,
        flops=4 * work,
    )
    return (
        prompt_query_grad,
        prompt_key_grad,
        prompt_value_grad,
        reply_query_grad,
        reply_key_grad,
        reply_value_grad,
    )


def solution(mesh):
    prompt = P(("sample", "ctx"), "head", None)
    reply = P("sample", "ctx", "head", None)
    in_specs = (
        (prompt,) * 4
        + (P("head", ("sample", "ctx")),)
        + (reply,) * 4
        + (P("sample", "head", "ctx"), P("sample"), P("head", None))
    )
    out_specs = (prompt,) * 3 + (reply,) * 3
    return jax.shard_map(shards, mesh=mesh, in_specs=in_specs, out_specs=out_specs, check_vma=False)
```

```python
import jax
import jax.numpy as jnp
from jax import lax
from jax.experimental import pallas as pl
from jax.experimental.pallas import tpu as pltpu
from jax.sharding import PartitionSpec as P

EPSILON = 1e-05
F32 = jnp.float32
BF16 = jnp.bfloat16
HEADS = 8
D = 128
HALF = D // 2
T = 128
PT = 16
CTX = 16
SAMPLE = 8
HEAD_AXIS = 4
ROW = CTX * PT
FEATURES = float(HEADS * HEAD_AXIS * D)


def iota(shape, axis):
    return lax.broadcasted_iota(jnp.int32, shape, axis)


def dot(a, b, ca, cb):
    return lax.dot_general(a, b, (((ca,), (cb,)), ((), ())), preferred_element_type=F32)


def split(x):
    high = x.astype(BF16)
    return high, (x - high.astype(F32)).astype(BF16)


def split3(x):
    high, rest = x.astype(BF16), None
    rest = x - high.astype(F32)
    mid = rest.astype(BF16)
    return high, mid, (rest - mid.astype(F32)).astype(BF16)


def dot_right(a, x, ca, cb):
    return sum(dot(a, part, ca, cb) for part in split(x))


def dot_left(x, b, ca, cb):
    return sum(dot(part, b, ca, cb) for part in split(x))


def low_lanes(rows):
    return iota((rows, D), 1) < HALF


def pack(x, half):
    top, bottom, low = x[0:8], x[8:16], low_lanes(8)
    if half == 0:
        return jnp.where(low, top, pltpu.roll(bottom, HALF, 1))
    return jnp.where(low, pltpu.roll(top, HALF, 1), bottom)


def unpack(first, second):
    low = low_lanes(8)
    top = jnp.where(low, first, pltpu.roll(second, HALF, 1))
    bottom = jnp.where(low, pltpu.roll(first, HALF, 1), second)
    return jnp.concatenate([top, bottom], axis=0)


def rows_of_half(x):
    both = jnp.stack([x[:, :, :HALF], x[:, :, HALF:]], axis=1)
    return both.reshape(ROW, HALF)


def packed_half(x):
    both = x.reshape(CTX, 2, 8, HALF)
    return jnp.concatenate([both[:, 0], both[:, 1]], axis=-1)


def running_rows(decay):
    upper = (iota((T, T), 0) <= iota((T, T), 1)).astype(BF16)
    return sum(dot(part, upper, 1, 0) for part in split3(decay))


def running_columns(decay):
    lower = (iota((T, T), 1) <= iota((T, T), 0)).astype(BF16)
    return sum(dot(lower, part, 1, 1) for part in split3(decay))


def masking(column, row):
    extent = row.shape[1]
    causal = iota((extent, extent), 0) >= iota((extent, extent), 1)
    return jnp.where(causal, jnp.exp(jnp.where(causal, column - row, 0.0)), 0.0)


def column_to_row(column):
    extent = column.shape[0]
    eye = iota((extent, max(extent, D)), 0) == iota((extent, max(extent, D)), 1)
    return jnp.sum(jnp.where(eye, column, 0.0), axis=0, keepdims=True)


def row_to_column(row, extent):
    eye = iota((extent, row.shape[1]), 0) == iota((extent, row.shape[1]), 1)
    return jnp.sum(jnp.where(eye, row, 0.0), axis=1, keepdims=True)


def live_tokens(lengths):
    return lax.axis_index("ctx") * T + iota((T, 1), 0) < lengths[0]


def start_copies(pairs, sems):
    copies = [pltpu.make_async_copy(source, target, sems.at[i]) for i, (source, target) in enumerate(pairs)]
    for copy in copies:
        copy.start()
    return copies


def send_kernel(
    lengths, key, value, decay, prompt_query, prompt_key, prompt_value, prompt_decay, out, key_out, value_out,
    key_in, value_in, decay_in, query_in, prompt_key_in, prompt_value_in, prompt_decay_in,
    rows_k, rows_v, prompt_q, prompt_k, prompt_v, sems,
):
    copies = start_copies(
        [
            (decay, decay_in),
            (prompt_decay, prompt_decay_in),
            (prompt_query, query_in),
            (prompt_key, prompt_key_in),
            (prompt_value, prompt_value_in),
            (value, value_in),
            (key, key_in),
        ],
        sems,
    )
    live = live_tokens(lengths)
    for copy in copies[:5]:
        copy.wait()
    columns = running_columns(decay_in[0])
    to_end = jnp.exp(columns[T - 1 : T, :] - columns)
    wide = jnp.concatenate([prompt_decay_in[...], jnp.zeros((HEADS, D - PT), F32)], axis=1)
    totals = jnp.sum(decay_in[0], axis=1, keepdims=True)
    at = iota((8, D), 0)
    prompt_q[...] = query_in[...].astype(F32).reshape(PT * HEADS, D)
    prompt_k[...] = prompt_key_in[...].astype(F32).reshape(PT * HEADS, D)
    prompt_v[...] = prompt_value_in[...].astype(F32).reshape(PT * HEADS, D)
    for h in range(HEADS):
        tail = jnp.where(at == 0, wide[h : h + 1], jnp.where(at == 1, totals[h : h + 1], 0.0))
        q = prompt_q[pl.ds(h, PT, HEADS), :]
        k = prompt_k[pl.ds(h, PT, HEADS), :]
        v = prompt_v[pl.ds(h, PT, HEADS), :]
        for half in range(2):
            out[2 * h + half, 64:80, :] = k
            out[2 * h + half, 80:88, :] = pack(v, half)
            out[2 * h + half, 88:96, :] = tail
            out[2 * h + half, 96:104, :] = q[8 * half : 8 * half + 8]
    for copy in copies[5:]:
        copy.wait()
    rows_v[...] = value_in[0].astype(F32).reshape(T * HEADS, D)
    rows_k[...] = key_in[0].astype(F32).reshape(T * HEADS, D)
    for h in range(HEADS):
        k = jnp.where(live, rows_k[pl.ds(h, T, HEADS), :], 0.0)
        v = jnp.where(live, rows_v[pl.ds(h, T, HEADS), :], 0.0).astype(BF16)
        key_out[h] = k.astype(BF16)
        value_out[h] = v
        state = dot_right(v, k * to_end[:, h : h + 1], 0, 0)
        for half in range(2):
            out[2 * h + half, 0:64, :] = state[half * HALF : (half + 1) * HALF]


def wide_columns(columns):
    return jnp.concatenate([columns, jnp.zeros((T, D - HEADS), F32)], axis=1)


def reply_local_kernel(
    lengths, query, grad, key, decay, gain, prompt_grad,
    query_out, grad_out, weights_out, growth_out, scale_out, upstream_out,
    query_in, grad_in, rows, rows_g, prompt_rows, sems,
):
    copies = start_copies([(query, query_in), (grad, grad_in)], sems)
    live = live_tokens(lengths)
    lines = running_rows(decay[0])
    columns = running_columns(decay[0])
    growth_out[...] = wide_columns(jnp.exp(columns))
    scale = gain[...].astype(F32)
    scale_out[...] = scale
    prompt_rows[...] = prompt_grad[...].astype(F32).reshape(PT * HEADS, D)
    for h in range(HEADS):
        upstream_out[h] = prompt_rows[pl.ds(h, PT, HEADS), :] * scale[h : h + 1]
    for copy in copies:
        copy.wait()
    rows[...] = query_in[0].astype(F32).reshape(T * HEADS, D)
    rows_g[...] = grad_in[0].astype(F32).reshape(T * HEADS, D)
    for h in range(HEADS):
        q = jnp.where(live, rows[pl.ds(h, T, HEADS), :], 0.0).astype(BF16)
        query_out[h] = q
        mask = masking(columns[:, h : h + 1], lines[h : h + 1])
        weights_out[h] = (dot(q, key[h], 1, 1) * mask).astype(BF16)
        grad_out[h] = jnp.where(live, rows_g[pl.ds(h, T, HEADS), :], 0.0).astype(BF16)


def prompt_row_kernel(received, out, column_out, query_out, blocks_out):
    decay = received[:, 88, :]
    token_block, token_place = iota((ROW, CTX), 0) // PT, iota((ROW, D), 0) % PT
    block = iota((ROW, CTX), 1)
    parts = split3(decay)
    own = sum(dot((block == token_block).astype(BF16), part, 1, 0) for part in parts)
    before = sum(dot((block < token_block).astype(BF16), part, 1, 0) for part in parts)
    running = jnp.sum(before + jnp.where(iota((ROW, D), 1) <= token_place, own, 0.0), axis=1, keepdims=True)
    last = running[ROW - 1 : ROW]
    k = received[:, 64:80, :].reshape(ROW, D)
    v = rows_of_half(received[:, 80:88, :]).astype(BF16)
    state = dot_right(v, k * jnp.exp(last - running), 0, 0)
    total = jnp.broadcast_to(last, (8, D))
    for s in range(SAMPLE):
        out[s, 0:64, :] = state
        out[s, 64:72, :] = total
    column_out[...] = jnp.broadcast_to(running, (ROW, D))
    query_out[...] = received[:, 96:104, :]
    blocks_out[...] = received[:, 89, :]


def same_block():
    return iota((ROW, ROW), 0) // PT == iota((ROW, ROW), 1) // PT


def prompt_weights(q, k, mask):
    scores = dot(q, k, 1, 1) * mask
    high = scores.astype(BF16)
    low = jnp.where(same_block(), 0.0, scores - high.astype(F32)).astype(BF16)
    return high, low


def second_core():
    return lax.axis_index("ctx") % 2 == 1


def prompt_local_kernel(
    received, other, column, query_out, key_out, value_out, line_out, local_out
):
    own = received[:, 96:104, :]
    second = second_core()
    first_half = jnp.where(second, other[...], own)
    second_half = jnp.where(second, own, other[...])
    q = jnp.concatenate([first_half, second_half], axis=1).reshape(ROW, D).astype(BF16)
    k = received[:, 64:80, :].reshape(ROW, D).astype(BF16)
    v = rows_of_half(received[:, 80:88, :]).astype(BF16)
    running = column[:, 0:1]
    line = column_to_row(running)
    query_out[...] = q
    key_out[...] = k
    value_out[...] = v
    line_out[...] = jnp.broadcast_to(line, (8, ROW))
    weights = prompt_weights(q, k, masking(running, line))
    local_out[...] = sum(dot(part, v, 1, 0) for part in weights)


def fold_kernel(rows_received, received, query, local, column, after_reply, out, start_out, factors_out):
    del after_reply
    place = lax.axis_index("sample")
    totals = [rows_received[s, 64:65, :] for s in range(SAMPLE)]
    end = jnp.zeros((HALF, D), F32)
    start = end
    for s in range(SAMPLE):
        start = jnp.where(place == s, end, start)
        end = jnp.exp(totals[s]) * end + rows_received[s, 0:64, :]
    start_out[...] = start
    state = end
    for b in range(CTX):
        out[b, 0:64, :] = state
        state = jnp.exp(received[b, 89:90, :]) * state + received[b, 0:64, :]
    outputs = local[...] + jnp.exp(column[:, 0:1]) * dot_right(query[...], start, 1, 1)
    out[:, 64:72, :] = packed_half(outputs)
    for s in range(SAMPLE):
        after = jnp.zeros((1, D), F32)
        between = after
        for other in range(s + 1, SAMPLE):
            after = after + totals[other]
            between = between + jnp.where(other < place, totals[other], 0.0)
        factors_out[s : s + 1, :] = jnp.exp(after)
        factors_out[SAMPLE + s : SAMPLE + s + 1, :] = jnp.where(place > s, jnp.exp(between), 0.0)


def output_kernel(
    received, query, weights, value, grad, growth, scale, prompt_upstream, out, output_out, prompt_out
):
    squares = jnp.zeros((T, D), F32)
    crossed = jnp.zeros((T, D), F32)
    prompt_squares = jnp.zeros((PT, D), F32)
    prompt_crossed = jnp.zeros((PT, D), F32)
    for h in range(HEADS):
        state = jnp.concatenate([received[2 * h, 0:64, :], received[2 * h + 1, 0:64, :]], axis=0)
        outputs = dot(weights[h], value[h], 1, 0) + growth[:, h : h + 1] * dot_right(query[h], state, 1, 1)
        output_out[h] = outputs
        upstream = grad[h].astype(F32) * scale[h : h + 1, :]
        squares = squares + outputs * outputs
        crossed = crossed + upstream * outputs
        outputs = unpack(received[2 * h, 64:72, :], received[2 * h + 1, 64:72, :])
        prompt_out[h] = outputs
        prompt_squares = prompt_squares + outputs * outputs
        prompt_crossed = prompt_crossed + prompt_upstream[h] * outputs
    sums = [
        column_to_row(jnp.sum(part, axis=1, keepdims=True))
        for part in (squares, crossed, prompt_squares, prompt_crossed)
    ]
    at = iota((8, D), 0)
    tile = jnp.zeros((8, D), F32)
    for i, part in enumerate(sums):
        tile = jnp.where(at == i, part, tile)
    for x in range(HEAD_AXIS):
        out[x] = tile


def norm_terms(squares, crossed):
    inverse = lax.rsqrt(squares / FEATURES + EPSILON)
    return inverse, crossed * inverse * inverse / FEATURES


def grad_kernel(
    sums, outputs, prompt_outputs, query, grad, growth, scale, prompt_upstream, out, grad_out
):
    total = sums[0] + sums[1] + sums[2] + sums[3]
    inverse, project = norm_terms(row_to_column(total[0:1], T), row_to_column(total[1:2], T))
    prompt_inverse, prompt_project = norm_terms(row_to_column(total[2:3], PT), row_to_column(total[3:4], PT))
    for h in range(HEADS):
        upstream = grad[h].astype(F32) * scale[h : h + 1, :]
        out_grad = ((upstream - outputs[h] * project) * inverse).astype(BF16)
        grad_out[h] = out_grad
        back = dot_right(out_grad, query[h].astype(F32) * growth[:, h : h + 1], 0, 0)
        prompt_out_grad = (prompt_upstream[h] - prompt_outputs[h] * prompt_project) * prompt_inverse
        prompt_out_grad = prompt_out_grad.astype(BF16).astype(F32)
        for half in range(2):
            out[2 * h + half, 0:64, :] = back[half * HALF : (half + 1) * HALF]
            out[2 * h + half, 64:72, :] = pack(prompt_out_grad, half)


def reply_back_kernel(
    received, out_grad, query, key, value, weights, decay, after_fold,
    query_grad, key_local, value_local, to_end_out, rows,
):
    del after_fold
    lines = running_rows(decay[0])
    columns = running_columns(decay[0])
    scales = jnp.exp(columns)
    to_end_out[...] = wide_columns(jnp.exp(columns[T - 1 : T, :] - columns))
    for h in range(HEADS):
        state = jnp.concatenate([received[2 * h, 0:64, :], received[2 * h + 1, 0:64, :]], axis=0)
        og = out_grad[h]
        mask = masking(columns[:, h : h + 1], lines[h : h + 1])
        mix = (dot(og, value[h], 1, 1) * mask).astype(BF16)
        rows[pl.ds(h, T, HEADS), :] = dot(mix, key[h], 1, 0) + scales[:, h : h + 1] * dot_right(og, state, 1, 0)
        key_local[h] = dot(mix, query[h], 0, 0)
        value_local[h] = dot(weights[h], og, 0, 0)
    query_grad[0] = rows[...].reshape(T, HEADS, D).astype(BF16)


def back_fold_kernel(received, blocks, factors, query, column, rows_out, ready_out):
    adjoint = jnp.zeros((HALF, D), F32)
    for b in range(CTX - 1, -1, -1):
        adjoint = jnp.exp(blocks[b : b + 1, :]) * adjoint + received[b, 0:64, :]
    og = rows_of_half(received[:, 64:72, :]).astype(BF16)
    back = dot_right(og, query[...].astype(F32) * jnp.exp(column[:, 0:1]), 0, 0)
    for s in range(SAMPLE):
        rows_out[s] = factors[s : s + 1, :] * adjoint + factors[SAMPLE + s : SAMPLE + s + 1, :] * back
    ready_out[...] = adjoint[0:8]


def prompt_mid_kernel(received, blocks, start, query, key, value, column, line, out, swap_out):
    adjoint = jnp.zeros((HALF, D), F32)
    for b in range(CTX - 1, -1, -1):
        out[b, 0:64, :] = adjoint
        adjoint = jnp.exp(blocks[b : b + 1, :]) * adjoint + received[b, 0:64, :]
    og = rows_of_half(received[:, 64:72, :]).astype(BF16)
    running = column[:, 0:1]
    mask = masking(running, line[0:1, :])
    mix = split(dot(og, value[...], 1, 1) * mask)
    k, q = key[...], query[...]
    query_grad = sum(dot(part, k, 1, 0) for part in mix) + jnp.exp(running) * dot_right(og, start[...], 1, 0)
    query_grad = query_grad.reshape(CTX, PT, D)
    second = second_core()
    swap_out[...] = jnp.where(second, query_grad[:, 0:8], query_grad[:, 8:16])
    key_local = sum(dot(part, q, 0, 0) for part in mix)
    value_local = sum(dot(part, og, 0, 0) for part in prompt_weights(q, k, mask))
    out[:, 64:80, :] = key_local.reshape(CTX, PT, D)
    out[:, 80:88, :] = packed_half(value_local)
    out[:, 88:96, :] = jnp.where(second, query_grad[:, 8:16], query_grad[:, 0:8])


def prompt_back_kernel(rows_received, swapped, key, value, column, message, after_reply, out):
    del after_reply
    adjoint = rows_received[0]
    for s in range(1, SAMPLE):
        adjoint = adjoint + rows_received[s]
    running = column[:, 0:1]
    to_end = jnp.exp(running[ROW - 1 : ROW] - running)
    key_grad = to_end * dot_right(value[...], adjoint, 1, 0)
    value_grad = to_end * dot_right(key[...], adjoint, 1, 1)
    out[:, 0:64, :] = message[:, 0:64, :]
    out[:, 64:80, :] = message[:, 64:80, :] + key_grad.reshape(CTX, PT, D)
    out[:, 80:88, :] = message[:, 80:88, :] + packed_half(value_grad)
    out[:, 88:96, :] = message[:, 88:96, :] + swapped[...]


def end_kernel(
    received, key, value, key_local, value_local, to_end,
    key_grad, value_grad, prompt_query_grad, prompt_key_grad, prompt_value_grad,
    rows_k, rows_v, prompt_q, prompt_k, prompt_v,
):
    for h in range(HEADS):
        low, high = received[2 * h], received[2 * h + 1]
        adjoint = jnp.concatenate([low[0:64], high[0:64]], axis=0)
        scale = to_end[:, h : h + 1]
        rows_k[pl.ds(h, T, HEADS), :] = key_local[h] + scale * dot_right(value[h], adjoint, 1, 0)
        rows_v[pl.ds(h, T, HEADS), :] = value_local[h] + scale * dot_right(key[h], adjoint, 1, 1)
        prompt_k[pl.ds(h, PT, HEADS), :] = low[64:80] + high[64:80]
        prompt_v[pl.ds(h, PT, HEADS), :] = unpack(low[80:88], high[80:88])
        prompt_q[pl.ds(h, PT, HEADS), :] = jnp.concatenate([low[88:96], high[88:96]], axis=0)
    key_grad[0] = rows_k[...].reshape(T, HEADS, D).astype(BF16)
    value_grad[0] = rows_v[...].reshape(T, HEADS, D).astype(BF16)
    prompt_query_grad[...] = prompt_q[...].reshape(PT, HEADS, D).astype(BF16)
    prompt_key_grad[...] = prompt_k[...].reshape(PT, HEADS, D).astype(BF16)
    prompt_value_grad[...] = prompt_v[...].reshape(PT, HEADS, D).astype(BF16)


VMEM = pl.BlockSpec(memory_space=pltpu.VMEM)
SMEM = pl.BlockSpec(memory_space=pltpu.SMEM)
HBM = pl.BlockSpec(memory_space=pltpu.HBM)
REPLY_ROWS = pltpu.VMEM((T * HEADS, D), F32)
PROMPT_ROWS = pltpu.VMEM((PT * HEADS, D), F32)
BY_HEAD = ((HEADS, T, D), BF16)
BY_HEAD_WIDE = ((HEADS, T, D), F32)
REPLY = ((1, T, HEADS, D), BF16)
PROMPT = ((PT, HEADS, D), BF16)


def run(kernel, outs, scratch, *operands, hbm=(), kept=(), flops=0):
    operands = [
        pltpu.with_memory_space_constraint(operand, pltpu.HBM) if i in hbm else operand
        for i, operand in enumerate(operands)
    ]
    specs = [
        SMEM if operand.dtype == jnp.int32 else HBM if i in hbm else VMEM for i, operand in enumerate(operands)
    ]
    moved = sum(operand.size * operand.dtype.itemsize for operand in operands)
    return pl.pallas_call(
        kernel,
        out_shape=[
            pltpu.VMEM(shape, kind) if i in kept else jax.ShapeDtypeStruct(shape, kind)
            for i, (shape, kind) in enumerate(outs)
        ],
        in_specs=specs,
        out_specs=[VMEM] * len(outs),
        scratch_shapes=scratch,
        compiler_params=pltpu.CompilerParams(vmem_limit_bytes=8 * 1024 * 1024),
        cost_estimate=pl.CostEstimate(flops=flops, bytes_accessed=2 * moved, transcendentals=0),
        name=kernel.__name__,
    )(*operands)


def exchange(x, axis):
    return lax.all_to_all(x, axis, 0, 0, tiled=True)


def swap_cores(x):
    return lax.ppermute(x, "ctx", [(i, i ^ 1) for i in range(CTX)])


def shards(
    prompt_query,
    prompt_key,
    prompt_value,
    prompt_grad,
    prompt_decay,
    reply_query,
    reply_key,
    reply_value,
    reply_grad,
    reply_decay,
    reply_lengths,
    norm_gain,
):
    work = 8 * 2 * T * D * D
    reply_in, prompt_in = pltpu.VMEM(*REPLY), pltpu.VMEM(*PROMPT)
    sent, key, value = run(
        send_kernel,
        [((CTX, 104, D), F32), BY_HEAD, BY_HEAD],
        [reply_in, reply_in, pltpu.VMEM((1, HEADS, T), F32)]
        + [prompt_in] * 3
        + [pltpu.VMEM((HEADS, PT), F32)]
        + [REPLY_ROWS] * 2
        + [PROMPT_ROWS] * 3
        + [pltpu.SemaphoreType.DMA((7,))],
        reply_lengths,
        reply_key,
        reply_value,
        reply_decay,
        prompt_query,
        prompt_key,
        prompt_value,
        prompt_decay,
        hbm=range(1, 8),
        flops=2 * work,
        kept=(1, 2),
    )
    first = exchange(sent, "ctx")
    sent, column, half_query, blocks = run(
        prompt_row_kernel,
        [((SAMPLE, 72, D), F32), ((ROW, D), F32), ((CTX, 8, D), F32), ((CTX, D), F32)],
        [],
        first,
        kept=(1, 3),
    )
    rows = exchange(sent, "sample")
    query, grad, weights, growth, scale, prompt_upstream = run(
        reply_local_kernel,
        [BY_HEAD, BY_HEAD, BY_HEAD, ((T, D), F32), ((HEADS, D), F32), ((HEADS, PT, D), F32)],
        [reply_in, reply_in, REPLY_ROWS, REPLY_ROWS, PROMPT_ROWS, pltpu.SemaphoreType.DMA((2,))],
        reply_lengths,
        reply_query,
        reply_grad,
        key,
        reply_decay,
        norm_gain,
        prompt_grad,
        hbm=(1, 2),
        flops=2 * work,
        kept=range(6),
    )
    row_query, row_key, row_value, line, row_local = run(
        prompt_local_kernel,
        [
            ((ROW, D), BF16),
            ((ROW, D), BF16),
            ((ROW, HALF), BF16),
            ((8, ROW), F32),
            ((ROW, HALF), F32),
        ],
        [],
        first,
        swap_cores(half_query),
        column,
        flops=work,
        kept=range(5),
    )
    sent, start, factors = run(
        fold_kernel,
        [((CTX, 72, D), F32), ((HALF, D), F32), ((2 * SAMPLE, D), F32)],
        [],
        rows,
        first,
        row_query,
        row_local,
        column,
        scale,
        kept=(1, 2),
    )
    states = exchange(sent, "ctx")
    sent, outputs, prompt_outputs = run(
        output_kernel,
        [((HEAD_AXIS, 8, D), F32), BY_HEAD_WIDE, ((HEADS, PT, D), F32)],
        [],
        states,
        query,
        weights,
        value,
        grad,
        growth,
        scale,
        prompt_upstream,
        flops=2 * work,
        kept=(1, 2),
    )
    sums = exchange(sent, "head")
    sent, out_grad = run(
        grad_kernel,
        [((CTX, 72, D), F32), BY_HEAD],
        [],
        sums,
        outputs,
        prompt_outputs,
        query,
        grad,
        growth,
        scale,
        prompt_upstream,
        flops=2 * work,
        kept=(1,),
    )
    backs = exchange(sent, "ctx")
    sent, ready = run(
        back_fold_kernel,
        [((SAMPLE, HALF, D), F32), ((8, D), F32)],
        [],
        backs,
        blocks,
        factors,
        row_query,
        column,
        kept=(1,),
    )
    rows = exchange(sent, "sample")
    reply_query_grad, key_local, value_local, to_end = run(
        reply_back_kernel,
        [REPLY, BY_HEAD_WIDE, BY_HEAD_WIDE, ((T, D), F32)],
        [REPLY_ROWS],
        states,
        out_grad,
        query,
        key,
        value,
        weights,
        reply_decay,
        ready,
        flops=6 * work,
        kept=(1, 2, 3),
    )
    message, swap = run(
        prompt_mid_kernel,
        [((CTX, 96, D), F32), ((CTX, 8, D), F32)],
        [],
        backs,
        blocks,
        start,
        row_query,
        row_key,
        row_value,
        column,
        line,
        flops=work,
        kept=(0,),
    )
    (sent,) = run(
        prompt_back_kernel,
        [((CTX, 96, D), F32)],
        [],
        rows,
        swap_cores(swap),
        row_key,
        row_value,
        column,
        message,
        to_end,
    )
    received = exchange(sent, "ctx")
    reply_key_grad, reply_value_grad, prompt_query_grad, prompt_key_grad, prompt_value_grad = run(
        end_kernel,
        [REPLY, REPLY, PROMPT, PROMPT, PROMPT],
        [REPLY_ROWS] * 2 + [PROMPT_ROWS] * 3,
        received,
        key,
        value,
        key_local,
        value_local,
        to_end,
        flops=4 * work,
    )
    return (
        prompt_query_grad,
        prompt_key_grad,
        prompt_value_grad,
        reply_query_grad,
        reply_key_grad,
        reply_value_grad,
    )


def solution(mesh):
    prompt = P(("sample", "ctx"), "head", None)
    reply = P("sample", "ctx", "head", None)
    in_specs = (
        (prompt,) * 4
        + (P("head", ("sample", "ctx")),)
        + (reply,) * 4
        + (P("sample", "head", "ctx"), P("sample"), P("head", None))
    )
    out_specs = (prompt,) * 3 + (reply,) * 3
    return jax.shard_map(shards, mesh=mesh, in_specs=in_specs, out_specs=out_specs, check_vma=False)
```

```python
import jax
import jax.numpy as jnp
from jax import lax
from jax.experimental import pallas as pl
from jax.experimental.pallas import tpu as pltpu
from jax.sharding import PartitionSpec as P

EPSILON = 1e-05
F32 = jnp.float32
BF16 = jnp.bfloat16
HEADS = 8
D = 128
HALF = D // 2
T = 128
PT = 16
CTX = 16
CHIPS = 8
SAMPLE = 8
HEAD_AXIS = 4
ROW = CTX * PT
FEATURES = float(HEADS * HEAD_AXIS * D)


def iota(shape, axis):
    return lax.broadcasted_iota(jnp.int32, shape, axis)


def dot(a, b, ca, cb):
    return lax.dot_general(a, b, (((ca,), (cb,)), ((), ())), preferred_element_type=F32)


def split(x):
    high = x.astype(BF16)
    return high, (x - high.astype(F32)).astype(BF16)


def split3(x):
    high, rest = x.astype(BF16), None
    rest = x - high.astype(F32)
    mid = rest.astype(BF16)
    return high, mid, (rest - mid.astype(F32)).astype(BF16)


def dot_right(a, x, ca, cb):
    return sum(dot(a, part, ca, cb) for part in split(x))


def dot_left(x, b, ca, cb):
    return sum(dot(part, b, ca, cb) for part in split(x))


def low_lanes(rows):
    return iota((rows, D), 1) < HALF


def pack(x, half):
    top, bottom, low = x[0:8], x[8:16], low_lanes(8)
    if half == 0:
        return jnp.where(low, top, pltpu.roll(bottom, HALF, 1))
    return jnp.where(low, pltpu.roll(top, HALF, 1), bottom)


def unpack(first, second):
    low = low_lanes(8)
    top = jnp.where(low, first, pltpu.roll(second, HALF, 1))
    bottom = jnp.where(low, pltpu.roll(first, HALF, 1), second)
    return jnp.concatenate([top, bottom], axis=0)


def rows_of_half(x):
    both = jnp.stack([x[:, :, :HALF], x[:, :, HALF:]], axis=1)
    return both.reshape(ROW, HALF)


def packed_half(x):
    both = x.reshape(CTX, 2, 8, HALF)
    return jnp.concatenate([both[:, 0], both[:, 1]], axis=-1)


def running_rows(decay):
    upper = (iota((T, T), 0) <= iota((T, T), 1)).astype(BF16)
    return sum(dot(part, upper, 1, 0) for part in split3(decay))


def running_columns(decay):
    lower = (iota((T, T), 1) <= iota((T, T), 0)).astype(BF16)
    return sum(dot(lower, part, 1, 1) for part in split3(decay))


def masking(column, row):
    extent = row.shape[1]
    causal = iota((extent, extent), 0) >= iota((extent, extent), 1)
    return jnp.where(causal, jnp.exp(jnp.where(causal, column - row, 0.0)), 0.0)


def column_to_row(column):
    extent = column.shape[0]
    eye = iota((extent, max(extent, D)), 0) == iota((extent, max(extent, D)), 1)
    return jnp.sum(jnp.where(eye, column, 0.0), axis=0, keepdims=True)


def row_to_column(row, extent):
    eye = iota((extent, row.shape[1]), 0) == iota((extent, row.shape[1]), 1)
    return jnp.sum(jnp.where(eye, row, 0.0), axis=1, keepdims=True)


def live_tokens(lengths):
    return lax.axis_index("ctx") * T + iota((T, 1), 0) < lengths[0]


def second_core():
    return lax.axis_index("ctx") % 2 == 1


def in_order(mine, other):
    second = second_core()
    return jnp.where(second, other, mine), jnp.where(second, mine, other)


def choose(first, last):
    return in_order(first, last)


def start_copies(pairs, sems):
    copies = [pltpu.make_async_copy(source, target, sems.at[i]) for i, (source, target) in enumerate(pairs)]
    for copy in copies:
        copy.start()
    return copies


def send_kernel(
    lengths, key, value, decay, prompt_query, prompt_key, prompt_value, prompt_decay,
    mine, theirs, query_out, key_out, value_out,
    key_in, value_in, decay_in, query_in, prompt_key_in, prompt_value_in, prompt_decay_in,
    rows_k, rows_v, prompt_q, prompt_k, prompt_v, sems,
):
    copies = start_copies(
        [
            (decay, decay_in),
            (prompt_decay, prompt_decay_in),
            (prompt_query, query_in),
            (prompt_key, prompt_key_in),
            (prompt_value, prompt_value_in),
            (value, value_in),
            (key, key_in),
        ],
        sems,
    )
    live = live_tokens(lengths)
    for copy in copies[:5]:
        copy.wait()
    columns = running_columns(decay_in[0])
    to_end = jnp.exp(columns[T - 1 : T, :] - columns)
    wide = jnp.concatenate([prompt_decay_in[...], jnp.zeros((HEADS, D - PT), F32)], axis=1)
    totals = jnp.sum(decay_in[0], axis=1, keepdims=True)
    at = iota((8, D), 0)
    prompt_q[...] = query_in[...].astype(F32).reshape(PT * HEADS, D)
    prompt_k[...] = prompt_key_in[...].astype(F32).reshape(PT * HEADS, D)
    prompt_v[...] = prompt_value_in[...].astype(F32).reshape(PT * HEADS, D)
    for h in range(HEADS):
        tail = jnp.where(at == 0, wide[h : h + 1], jnp.where(at == 1, totals[h : h + 1], 0.0))
        query_out[h] = prompt_q[pl.ds(h, PT, HEADS), :]
        k = prompt_k[pl.ds(h, PT, HEADS), :]
        v = prompt_v[pl.ds(h, PT, HEADS), :]
        for ref, half in zip((mine, theirs), choose(pack(v, 0), pack(v, 1))):
            ref[h, 64:80, :] = k
            ref[h, 80:88, :] = half
            ref[h, 88:96, :] = tail
    for copy in copies[5:]:
        copy.wait()
    rows_v[...] = value_in[0].astype(F32).reshape(T * HEADS, D)
    rows_k[...] = key_in[0].astype(F32).reshape(T * HEADS, D)
    for h in range(HEADS):
        k = jnp.where(live, rows_k[pl.ds(h, T, HEADS), :], 0.0)
        v = jnp.where(live, rows_v[pl.ds(h, T, HEADS), :], 0.0).astype(BF16)
        key_out[h] = k.astype(BF16)
        value_out[h] = v
        state = dot_right(v, k * to_end[:, h : h + 1], 0, 0)
        for ref, half in zip((mine, theirs), choose(state[0:64], state[64:128])):
            ref[h, 0:64, :] = half


def merge_kernel(mine, other, query, out, first_out, totals_out):
    at = iota((8, D), 0)
    for h in range(HEADS):
        first, last = in_order(mine[h], other[h])
        totals_out[h : h + 1, :] = first[89:90]
        totals_out[HEADS + h : HEADS + h + 1, :] = last[89:90]
        first_out[h] = first[0:64]
        out[h, 0:64, :] = jnp.exp(last[89:90]) * first[0:64] + last[0:64]
        out[h, 64:80, :] = first[64:80]
        out[h, 80:96, :] = last[64:80]
        out[h, 96:104, :] = first[80:88]
        out[h, 104:112, :] = last[80:88]
        tile = jnp.where(at == 0, first[88:89], jnp.where(at == 1, first[89:90], 0.0))
        out[h, 112:120, :] = jnp.where(at == 2, last[88:89], jnp.where(at == 3, last[89:90], tile))
        out[h, 120:136, :] = query[h]


def wide_columns(columns):
    return jnp.concatenate([columns, jnp.zeros((T, D - HEADS), F32)], axis=1)


def reply_local_kernel(
    lengths, query, grad, key, decay, gain, prompt_grad,
    query_out, grad_out, weights_out, growth_out, scale_out, upstream_out,
    query_in, grad_in, rows, rows_g, prompt_rows, sems,
):
    copies = start_copies([(query, query_in), (grad, grad_in)], sems)
    live = live_tokens(lengths)
    lines = running_rows(decay[0])
    columns = running_columns(decay[0])
    growth_out[...] = wide_columns(jnp.exp(columns))
    scale = gain[...].astype(F32)
    scale_out[...] = scale
    prompt_rows[...] = prompt_grad[...].astype(F32).reshape(PT * HEADS, D)
    for h in range(HEADS):
        upstream_out[h] = prompt_rows[pl.ds(h, PT, HEADS), :] * scale[h : h + 1]
    for copy in copies:
        copy.wait()
    rows[...] = query_in[0].astype(F32).reshape(T * HEADS, D)
    rows_g[...] = grad_in[0].astype(F32).reshape(T * HEADS, D)
    for h in range(HEADS):
        q = jnp.where(live, rows[pl.ds(h, T, HEADS), :], 0.0).astype(BF16)
        query_out[h] = q
        mask = masking(columns[:, h : h + 1], lines[h : h + 1])
        weights_out[h] = (dot(q, key[h], 1, 1) * mask).astype(BF16)
        grad_out[h] = jnp.where(live, rows_g[pl.ds(h, T, HEADS), :], 0.0).astype(BF16)


def prompt_row_kernel(received, out, column_out, query_out, blocks_out):
    decay = jnp.concatenate([received[:, 112, :], received[:, 114, :]], axis=0)
    token_block, token_place = iota((ROW, CTX), 0) // PT, iota((ROW, D), 0) % PT
    at = iota((ROW, CTX), 1)
    block = jnp.where(at < CHIPS, 2 * at, 2 * (at - CHIPS) + 1)
    parts = split3(decay)
    own = sum(dot((block == token_block).astype(BF16), part, 1, 0) for part in parts)
    before = sum(dot((block < token_block).astype(BF16), part, 1, 0) for part in parts)
    running = jnp.sum(before + jnp.where(iota((ROW, D), 1) <= token_place, own, 0.0), axis=1, keepdims=True)
    last = running[ROW - 1 : ROW]
    k = received[:, 64:96, :].reshape(ROW, D)
    v = rows_of_half(received[:, 96:112, :].reshape(CTX, 8, D)).astype(BF16)
    state = dot_right(v, k * jnp.exp(last - running), 0, 0)
    total = jnp.broadcast_to(last, (8, D))
    for s in range(SAMPLE):
        out[s, 0:64, :] = state
        out[s, 64:72, :] = total
    column_out[...] = jnp.broadcast_to(running, (ROW, D))
    query_out[...] = received[:, 120:136, :]
    blocks_out[...] = received[:, 113, :] + received[:, 115, :]


def same_block():
    return iota((ROW, ROW), 0) // PT == iota((ROW, ROW), 1) // PT


def prompt_weights(q, k, mask):
    scores = dot(q, k, 1, 1) * mask
    high = scores.astype(BF16)
    low = jnp.where(same_block(), 0.0, scores - high.astype(F32)).astype(BF16)
    return high, low


def prompt_local_kernel(
    received, other, column, query_out, key_out, value_out, line_out, local_out
):
    both = in_order(received[:, 120:136, :], other[...])
    q = jnp.concatenate(both, axis=1).reshape(ROW, D).astype(BF16)
    k = received[:, 64:96, :].reshape(ROW, D).astype(BF16)
    v = rows_of_half(received[:, 96:112, :].reshape(CTX, 8, D)).astype(BF16)
    running = column[:, 0:1]
    line = column_to_row(running)
    query_out[...] = q
    key_out[...] = k
    value_out[...] = v
    line_out[...] = jnp.broadcast_to(line, (8, ROW))
    weights = prompt_weights(q, k, masking(running, line))
    local_out[...] = sum(dot(part, v, 1, 0) for part in weights)


def fold_kernel(
    rows_received, received, blocks, query, local, column, after_reply, out, start_out, factors_out
):
    del after_reply
    place = lax.axis_index("sample")
    totals = [rows_received[s, 64:65, :] for s in range(SAMPLE)]
    end = jnp.zeros((HALF, D), F32)
    start = end
    for s in range(SAMPLE):
        start = jnp.where(place == s, end, start)
        end = jnp.exp(totals[s]) * end + rows_received[s, 0:64, :]
    start_out[...] = start
    state = end
    for y in range(CHIPS):
        out[y, 0:64, :] = state
        state = jnp.exp(blocks[y : y + 1, :]) * state + received[y, 0:64, :]
    outputs = local[...] + jnp.exp(column[:, 0:1]) * dot_right(query[...], start, 1, 1)
    out[:, 64:80, :] = packed_half(outputs).reshape(CHIPS, PT, D)
    for s in range(SAMPLE):
        after = jnp.zeros((1, D), F32)
        between = after
        for other in range(s + 1, SAMPLE):
            after = after + totals[other]
            between = between + jnp.where(other < place, totals[other], 0.0)
        factors_out[s : s + 1, :] = jnp.exp(after)
        factors_out[SAMPLE + s : SAMPLE + s + 1, :] = jnp.where(place > s, jnp.exp(between), 0.0)


def spread_kernel(received, first_state, totals, mine, theirs):
    for h in range(HEADS):
        before = received[h, 0:64, :]
        after = jnp.exp(totals[h : h + 1, :]) * before + first_state[h]
        mine[h, 0:64, :], theirs[h, 0:64, :] = choose(before, after)
        mine[h, 64:72, :], theirs[h, 64:72, :] = choose(received[h, 64:72, :], received[h, 72:80, :])


def output_kernel(
    mine, other, query, weights, value, grad, growth, scale, prompt_upstream, out, output_out, prompt_out
):
    squares = jnp.zeros((T, D), F32)
    crossed = jnp.zeros((T, D), F32)
    prompt_squares = jnp.zeros((PT, D), F32)
    prompt_crossed = jnp.zeros((PT, D), F32)
    for h in range(HEADS):
        low, high = in_order(mine[h], other[h])
        state = jnp.concatenate([low[0:64], high[0:64]], axis=0)
        outputs = dot(weights[h], value[h], 1, 0) + growth[:, h : h + 1] * dot_right(query[h], state, 1, 1)
        output_out[h] = outputs
        upstream = grad[h].astype(F32) * scale[h : h + 1, :]
        squares = squares + outputs * outputs
        crossed = crossed + upstream * outputs
        outputs = unpack(low[64:72], high[64:72])
        prompt_out[h] = outputs
        prompt_squares = prompt_squares + outputs * outputs
        prompt_crossed = prompt_crossed + prompt_upstream[h] * outputs
    sums = [
        column_to_row(jnp.sum(part, axis=1, keepdims=True))
        for part in (squares, crossed, prompt_squares, prompt_crossed)
    ]
    at = iota((8, D), 0)
    tile = jnp.zeros((8, D), F32)
    for i, part in enumerate(sums):
        tile = jnp.where(at == i, part, tile)
    for x in range(HEAD_AXIS):
        out[x] = tile


def norm_terms(squares, crossed):
    inverse = lax.rsqrt(squares / FEATURES + EPSILON)
    return inverse, crossed * inverse * inverse / FEATURES


def grad_kernel(
    sums, outputs, prompt_outputs, query, grad, growth, scale, prompt_upstream, mine, theirs, grad_out
):
    total = sums[0] + sums[1] + sums[2] + sums[3]
    inverse, project = norm_terms(row_to_column(total[0:1], T), row_to_column(total[1:2], T))
    prompt_inverse, prompt_project = norm_terms(row_to_column(total[2:3], PT), row_to_column(total[3:4], PT))
    for h in range(HEADS):
        upstream = grad[h].astype(F32) * scale[h : h + 1, :]
        out_grad = ((upstream - outputs[h] * project) * inverse).astype(BF16)
        grad_out[h] = out_grad
        back = dot_right(out_grad, query[h].astype(F32) * growth[:, h : h + 1], 0, 0)
        prompt_out_grad = (prompt_upstream[h] - prompt_outputs[h] * prompt_project) * prompt_inverse
        prompt_out_grad = prompt_out_grad.astype(BF16).astype(F32)
        mine[h, 0:64, :], theirs[h, 0:64, :] = choose(back[0:64], back[64:128])
        mine[h, 64:72, :], theirs[h, 64:72, :] = choose(pack(prompt_out_grad, 0), pack(prompt_out_grad, 1))


def back_merge_kernel(mine, other, totals, out, last_out):
    for h in range(HEADS):
        first, last = in_order(mine[h], other[h])
        last_out[h] = last[0:64]
        out[h, 0:64, :] = first[0:64] + jnp.exp(totals[h : h + 1, :]) * last[0:64]
        out[h, 64:72, :] = first[64:72]
        out[h, 72:80, :] = last[64:72]


def reply_back_kernel(
    mine, other, out_grad, query, key, value, weights, decay, after_fold,
    query_grad, key_local, value_local, to_end_out, rows,
):
    del after_fold
    lines = running_rows(decay[0])
    columns = running_columns(decay[0])
    scales = jnp.exp(columns)
    to_end_out[...] = wide_columns(jnp.exp(columns[T - 1 : T, :] - columns))
    for h in range(HEADS):
        state = jnp.concatenate(in_order(mine[h, 0:64, :], other[h, 0:64, :]), axis=0)
        og = out_grad[h]
        mask = masking(columns[:, h : h + 1], lines[h : h + 1])
        mix = (dot(og, value[h], 1, 1) * mask).astype(BF16)
        rows[pl.ds(h, T, HEADS), :] = dot(mix, key[h], 1, 0) + scales[:, h : h + 1] * dot_right(og, state, 1, 0)
        key_local[h] = dot(mix, query[h], 0, 0)
        value_local[h] = dot(weights[h], og, 0, 0)
    query_grad[0] = rows[...].reshape(T, HEADS, D).astype(BF16)


def back_fold_kernel(received, blocks, factors, query, column, rows_out, ready_out):
    adjoint = jnp.zeros((HALF, D), F32)
    for y in range(CHIPS - 1, -1, -1):
        adjoint = jnp.exp(blocks[y : y + 1, :]) * adjoint + received[y, 0:64, :]
    og = rows_of_half(received[:, 64:80, :].reshape(CTX, 8, D)).astype(BF16)
    back = dot_right(og, query[...].astype(F32) * jnp.exp(column[:, 0:1]), 0, 0)
    for s in range(SAMPLE):
        rows_out[s] = factors[s : s + 1, :] * adjoint + factors[SAMPLE + s : SAMPLE + s + 1, :] * back
    ready_out[...] = adjoint[0:8]


def prompt_mid_kernel(received, blocks, start, query, key, value, column, line, out, swap_out):
    adjoint = jnp.zeros((HALF, D), F32)
    for y in range(CHIPS - 1, -1, -1):
        out[y, 0:64, :] = adjoint
        adjoint = jnp.exp(blocks[y : y + 1, :]) * adjoint + received[y, 0:64, :]
    og = rows_of_half(received[:, 64:80, :].reshape(CTX, 8, D)).astype(BF16)
    running = column[:, 0:1]
    mask = masking(running, line[0:1, :])
    mix = split(dot(og, value[...], 1, 1) * mask)
    k, q = key[...], query[...]
    query_grad = sum(dot(part, k, 1, 0) for part in mix) + jnp.exp(running) * dot_right(og, start[...], 1, 0)
    query_grad = query_grad.reshape(CHIPS, 2 * PT, D)
    key_local = sum(dot(part, q, 0, 0) for part in mix)
    value_local = sum(dot(part, og, 0, 0) for part in prompt_weights(q, k, mask))
    out[:, 64:96, :] = key_local.reshape(CHIPS, 2 * PT, D)
    out[:, 96:112, :] = packed_half(value_local).reshape(CHIPS, PT, D)
    out[:, 112:128, :], swap_out[...] = choose(query_grad[:, 0:PT], query_grad[:, PT:])


def prompt_back_kernel(rows_received, swapped, key, value, column, message, after_reply, out):
    del after_reply
    adjoint = rows_received[0]
    for s in range(1, SAMPLE):
        adjoint = adjoint + rows_received[s]
    running = column[:, 0:1]
    to_end = jnp.exp(running[ROW - 1 : ROW] - running)
    key_grad = to_end * dot_right(value[...], adjoint, 1, 0)
    value_grad = to_end * dot_right(key[...], adjoint, 1, 1)
    out[:, 0:64, :] = message[:, 0:64, :]
    out[:, 64:96, :] = message[:, 64:96, :] + key_grad.reshape(CHIPS, 2 * PT, D)
    out[:, 96:112, :] = message[:, 96:112, :] + packed_half(value_grad).reshape(CHIPS, PT, D)
    out[:, 112:128, :] = message[:, 112:128, :] + swapped[...]


def back_spread_kernel(received, last_back, totals, mine, theirs):
    for h in range(HEADS):
        after = received[h, 0:64, :]
        before = jnp.exp(totals[HEADS + h : HEADS + h + 1, :]) * after + last_back[h]
        mine[h, 0:64, :], theirs[h, 0:64, :] = choose(before, after)
        mine[h, 64:80, :], theirs[h, 64:80, :] = choose(received[h, 64:80, :], received[h, 80:96, :])
        mine[h, 80:88, :], theirs[h, 80:88, :] = choose(received[h, 96:104, :], received[h, 104:112, :])


def end_kernel(
    received, mine, other, key, value, key_local, value_local, to_end,
    key_grad, value_grad, prompt_query_grad, prompt_key_grad, prompt_value_grad,
    rows_k, rows_v, prompt_q, prompt_k, prompt_v,
):
    for h in range(HEADS):
        low, high = in_order(mine[h], other[h])
        adjoint = jnp.concatenate([low[0:64], high[0:64]], axis=0)
        scale = to_end[:, h : h + 1]
        rows_k[pl.ds(h, T, HEADS), :] = key_local[h] + scale * dot_right(value[h], adjoint, 1, 0)
        rows_v[pl.ds(h, T, HEADS), :] = value_local[h] + scale * dot_right(key[h], adjoint, 1, 1)
        prompt_k[pl.ds(h, PT, HEADS), :] = low[64:80] + high[64:80]
        prompt_v[pl.ds(h, PT, HEADS), :] = unpack(low[80:88], high[80:88])
        prompt_q[pl.ds(h, PT, HEADS), :] = received[h, 112:128, :]
    key_grad[0] = rows_k[...].reshape(T, HEADS, D).astype(BF16)
    value_grad[0] = rows_v[...].reshape(T, HEADS, D).astype(BF16)
    prompt_query_grad[...] = prompt_q[...].reshape(PT, HEADS, D).astype(BF16)
    prompt_key_grad[...] = prompt_k[...].reshape(PT, HEADS, D).astype(BF16)
    prompt_value_grad[...] = prompt_v[...].reshape(PT, HEADS, D).astype(BF16)


VMEM = pl.BlockSpec(memory_space=pltpu.VMEM)
SMEM = pl.BlockSpec(memory_space=pltpu.SMEM)
HBM = pl.BlockSpec(memory_space=pltpu.HBM)
REPLY_ROWS = pltpu.VMEM((T * HEADS, D), F32)
PROMPT_ROWS = pltpu.VMEM((PT * HEADS, D), F32)
BY_HEAD = ((HEADS, T, D), BF16)
BY_HEAD_WIDE = ((HEADS, T, D), F32)
REPLY = ((1, T, HEADS, D), BF16)
PROMPT = ((PT, HEADS, D), BF16)


def run(kernel, outs, scratch, *operands, hbm=(), kept=(), flops=0):
    operands = [
        pltpu.with_memory_space_constraint(operand, pltpu.HBM) if i in hbm else operand
        for i, operand in enumerate(operands)
    ]
    specs = [
        SMEM if operand.dtype == jnp.int32 else HBM if i in hbm else VMEM for i, operand in enumerate(operands)
    ]
    moved = sum(operand.size * operand.dtype.itemsize for operand in operands)
    return pl.pallas_call(
        kernel,
        out_shape=[
            pltpu.VMEM(shape, kind) if i in kept else jax.ShapeDtypeStruct(shape, kind)
            for i, (shape, kind) in enumerate(outs)
        ],
        in_specs=specs,
        out_specs=[VMEM] * len(outs),
        scratch_shapes=scratch,
        compiler_params=pltpu.CompilerParams(vmem_limit_bytes=8 * 1024 * 1024),
        cost_estimate=pl.CostEstimate(flops=flops, bytes_accessed=2 * moved, transcendentals=0),
        name=kernel.__name__,
    )(*operands)


def exchange(x, axis):
    return lax.all_to_all(x, axis, 0, 0, tiled=True)


def exchange_chips(x):
    groups = [[2 * chip + core for chip in range(CHIPS)] for core in range(2)]
    return lax.all_to_all(x, "ctx", 0, 0, axis_index_groups=groups, tiled=True)


def swap_cores(x):
    return lax.ppermute(x, "ctx", [(i, i ^ 1) for i in range(CTX)])


def shards(
    prompt_query,
    prompt_key,
    prompt_value,
    prompt_grad,
    prompt_decay,
    reply_query,
    reply_key,
    reply_value,
    reply_grad,
    reply_decay,
    reply_lengths,
    norm_gain,
):
    work = 8 * 2 * T * D * D
    reply_in, prompt_in = pltpu.VMEM(*REPLY), pltpu.VMEM(*PROMPT)
    mine, theirs, own_query, key, value = run(
        send_kernel,
        [((HEADS, 96, D), F32), ((HEADS, 96, D), F32), ((HEADS, PT, D), F32), BY_HEAD, BY_HEAD],
        [reply_in, reply_in, pltpu.VMEM((1, HEADS, T), F32)]
        + [prompt_in] * 3
        + [pltpu.VMEM((HEADS, PT), F32)]
        + [REPLY_ROWS] * 2
        + [PROMPT_ROWS] * 3
        + [pltpu.SemaphoreType.DMA((7,))],
        reply_lengths,
        reply_key,
        reply_value,
        reply_decay,
        prompt_query,
        prompt_key,
        prompt_value,
        prompt_decay,
        hbm=range(1, 8),
        flops=2 * work,
        kept=(0, 2, 3, 4),
    )
    sent, first_state, block_totals = run(
        merge_kernel,
        [((HEADS, 136, D), F32), ((HEADS, HALF, D), F32), ((2 * HEADS, D), F32)],
        [],
        mine,
        swap_cores(theirs),
        own_query,
        kept=(1, 2),
    )
    first = exchange_chips(sent)
    sent, column, half_query, blocks = run(
        prompt_row_kernel,
        [((SAMPLE, 72, D), F32), ((ROW, D), F32), ((CHIPS, PT, D), F32), ((CHIPS, D), F32)],
        [],
        first,
        kept=(1, 3),
    )
    rows = exchange(sent, "sample")
    query, grad, weights, growth, scale, prompt_upstream = run(
        reply_local_kernel,
        [BY_HEAD, BY_HEAD, BY_HEAD, ((T, D), F32), ((HEADS, D), F32), ((HEADS, PT, D), F32)],
        [reply_in, reply_in, REPLY_ROWS, REPLY_ROWS, PROMPT_ROWS, pltpu.SemaphoreType.DMA((2,))],
        reply_lengths,
        reply_query,
        reply_grad,
        key,
        reply_decay,
        norm_gain,
        prompt_grad,
        hbm=(1, 2),
        flops=2 * work,
        kept=range(6),
    )
    row_query, row_key, row_value, line, row_local = run(
        prompt_local_kernel,
        [
            ((ROW, D), BF16),
            ((ROW, D), BF16),
            ((ROW, HALF), BF16),
            ((8, ROW), F32),
            ((ROW, HALF), F32),
        ],
        [],
        first,
        swap_cores(half_query),
        column,
        flops=work,
        kept=range(5),
    )
    sent, start, factors = run(
        fold_kernel,
        [((CHIPS, 80, D), F32), ((HALF, D), F32), ((2 * SAMPLE, D), F32)],
        [],
        rows,
        first,
        blocks,
        row_query,
        row_local,
        column,
        scale,
        kept=(1, 2),
    )
    mine, theirs = run(
        spread_kernel,
        [((HEADS, 72, D), F32), ((HEADS, 72, D), F32)],
        [],
        exchange_chips(sent),
        first_state,
        block_totals,
        kept=(0,),
    )
    other = swap_cores(theirs)
    sent, outputs, prompt_outputs = run(
        output_kernel,
        [((HEAD_AXIS, 8, D), F32), BY_HEAD_WIDE, ((HEADS, PT, D), F32)],
        [],
        mine,
        other,
        query,
        weights,
        value,
        grad,
        growth,
        scale,
        prompt_upstream,
        flops=2 * work,
        kept=(1, 2),
    )
    sums = exchange(sent, "head")
    back_mine, back_theirs, out_grad = run(
        grad_kernel,
        [((HEADS, 72, D), F32), ((HEADS, 72, D), F32), BY_HEAD],
        [],
        sums,
        outputs,
        prompt_outputs,
        query,
        grad,
        growth,
        scale,
        prompt_upstream,
        flops=2 * work,
        kept=(0, 2),
    )
    sent, last_back = run(
        back_merge_kernel,
        [((HEADS, 80, D), F32), ((HEADS, HALF, D), F32)],
        [],
        back_mine,
        swap_cores(back_theirs),
        block_totals,
        kept=(1,),
    )
    backs = exchange_chips(sent)
    sent, ready = run(
        back_fold_kernel,
        [((SAMPLE, HALF, D), F32), ((8, D), F32)],
        [],
        backs,
        blocks,
        factors,
        row_query,
        column,
        kept=(1,),
    )
    rows = exchange(sent, "sample")
    reply_query_grad, key_local, value_local, to_end = run(
        reply_back_kernel,
        [REPLY, BY_HEAD_WIDE, BY_HEAD_WIDE, ((T, D), F32)],
        [REPLY_ROWS],
        mine,
        other,
        out_grad,
        query,
        key,
        value,
        weights,
        reply_decay,
        ready,
        flops=6 * work,
        kept=(1, 2, 3),
    )
    message, swap = run(
        prompt_mid_kernel,
        [((CHIPS, 128, D), F32), ((CHIPS, PT, D), F32)],
        [],
        backs,
        blocks,
        start,
        row_query,
        row_key,
        row_value,
        column,
        line,
        flops=work,
        kept=(0,),
    )
    (sent,) = run(
        prompt_back_kernel,
        [((CHIPS, 128, D), F32)],
        [],
        rows,
        swap_cores(swap),
        row_key,
        row_value,
        column,
        message,
        to_end,
    )
    received = exchange_chips(sent)
    end_mine, end_theirs = run(
        back_spread_kernel,
        [((HEADS, 88, D), F32), ((HEADS, 88, D), F32)],
        [],
        received,
        last_back,
        block_totals,
        kept=(0,),
    )
    reply_key_grad, reply_value_grad, prompt_query_grad, prompt_key_grad, prompt_value_grad = run(
        end_kernel,
        [REPLY, REPLY, PROMPT, PROMPT, PROMPT],
        [REPLY_ROWS] * 2 + [PROMPT_ROWS] * 3,
        received,
        end_mine,
        swap_cores(end_theirs),
        key,
        value,
        key_local,
        value_local,
        to_end,
        flops=4 * work,
    )
    return (
        prompt_query_grad,
        prompt_key_grad,
        prompt_value_grad,
        reply_query_grad,
        reply_key_grad,
        reply_value_grad,
    )


def solution(mesh):
    prompt = P(("sample", "ctx"), "head", None)
    reply = P("sample", "ctx", "head", None)
    in_specs = (
        (prompt,) * 4
        + (P("head", ("sample", "ctx")),)
        + (reply,) * 4
        + (P("sample", "head", "ctx"), P("sample"), P("head", None))
    )
    out_specs = (prompt,) * 3 + (reply,) * 3
    return jax.shard_map(shards, mesh=mesh, in_specs=in_specs, out_specs=out_specs, check_vma=False)
```

```python
import jax
import jax.numpy as jnp
from jax import lax
from jax.experimental import pallas as pl
from jax.experimental.pallas import tpu as pltpu
from jax.sharding import PartitionSpec as P

EPSILON = 1e-05
F32 = jnp.float32
BF16 = jnp.bfloat16
HEADS = 8
D = 128
HALF = D // 2
T = 128
PT = 16
CTX = 16
CHIPS = 8
SAMPLE = 8
HEAD_AXIS = 4
ROW = CTX * PT
FEATURES = float(HEADS * HEAD_AXIS * D)


def iota(shape, axis):
    return lax.broadcasted_iota(jnp.int32, shape, axis)


def dot(a, b, ca, cb):
    return lax.dot_general(a, b, (((ca,), (cb,)), ((), ())), preferred_element_type=F32)


def split(x):
    high = x.astype(BF16)
    return high, (x - high.astype(F32)).astype(BF16)


def split3(x):
    high, rest = x.astype(BF16), None
    rest = x - high.astype(F32)
    mid = rest.astype(BF16)
    return high, mid, (rest - mid.astype(F32)).astype(BF16)


def dot_right(a, x, ca, cb):
    return sum(dot(a, part, ca, cb) for part in split(x))


def dot_left(x, b, ca, cb):
    return sum(dot(part, b, ca, cb) for part in split(x))


def low_lanes(rows):
    return iota((rows, D), 1) < HALF


def pack(x, half):
    top, bottom, low = x[0:8], x[8:16], low_lanes(8)
    if half == 0:
        return jnp.where(low, top, pltpu.roll(bottom, HALF, 1))
    return jnp.where(low, pltpu.roll(top, HALF, 1), bottom)


def unpack(first, second):
    low = low_lanes(8)
    top = jnp.where(low, first, pltpu.roll(second, HALF, 1))
    bottom = jnp.where(low, pltpu.roll(first, HALF, 1), second)
    return jnp.concatenate([top, bottom], axis=0)


def rows_of_half(x):
    both = jnp.stack([x[:, :, :HALF], x[:, :, HALF:]], axis=1)
    return both.reshape(ROW, HALF)


def packed_half(x):
    both = x.reshape(CTX, 2, 8, HALF)
    return jnp.concatenate([both[:, 0], both[:, 1]], axis=-1)


def running_rows(decay):
    upper = (iota((T, T), 0) <= iota((T, T), 1)).astype(BF16)
    return sum(dot(part, upper, 1, 0) for part in split3(decay))


def running_columns(decay):
    lower = (iota((T, T), 1) <= iota((T, T), 0)).astype(BF16)
    return sum(dot(lower, part, 1, 1) for part in split3(decay))


def masking(column, row):
    extent = row.shape[1]
    causal = iota((extent, extent), 0) >= iota((extent, extent), 1)
    return jnp.where(causal, jnp.exp(jnp.where(causal, column - row, 0.0)), 0.0)


def column_to_row(column):
    extent = column.shape[0]
    eye = iota((extent, max(extent, D)), 0) == iota((extent, max(extent, D)), 1)
    return jnp.sum(jnp.where(eye, column, 0.0), axis=0, keepdims=True)


def row_to_column(row, extent):
    eye = iota((extent, row.shape[1]), 0) == iota((extent, row.shape[1]), 1)
    return jnp.sum(jnp.where(eye, row, 0.0), axis=1, keepdims=True)


def live_tokens(lengths):
    return lax.axis_index("ctx") * T + iota((T, 1), 0) < lengths[0]


def second_core():
    return lax.axis_index("ctx") % 2 == 1


def in_order(mine, other):
    second = second_core()
    return jnp.where(second, other, mine), jnp.where(second, mine, other)


def choose(first, last):
    return in_order(first, last)


def start_copies(pairs, sems):
    copies = [pltpu.make_async_copy(source, target, sems.at[i]) for i, (source, target) in enumerate(pairs)]
    for copy in copies:
        copy.start()
    return copies


def send_kernel(
    lengths, key, value, decay, prompt_query, prompt_key, prompt_value, prompt_decay,
    mine, theirs, query_out, key_out, value_out,
    key_in, value_in, decay_in, query_in, prompt_key_in, prompt_value_in, prompt_decay_in,
    rows_k, rows_v, prompt_q, prompt_k, prompt_v, sems,
):
    copies = start_copies(
        [
            (decay, decay_in),
            (prompt_decay, prompt_decay_in),
            (prompt_query, query_in),
            (prompt_key, prompt_key_in),
            (prompt_value, prompt_value_in),
            (value, value_in),
            (key, key_in),
        ],
        sems,
    )
    live = live_tokens(lengths)
    for copy in copies[:5]:
        copy.wait()
    columns = running_columns(decay_in[0])
    to_end = jnp.exp(columns[T - 1 : T, :] - columns)
    wide = jnp.concatenate([prompt_decay_in[...], jnp.zeros((HEADS, D - PT), F32)], axis=1)
    totals = jnp.sum(decay_in[0], axis=1, keepdims=True)
    at = iota((8, D), 0)
    prompt_q[...] = query_in[...].astype(F32).reshape(PT * HEADS, D)
    prompt_k[...] = prompt_key_in[...].astype(F32).reshape(PT * HEADS, D)
    prompt_v[...] = prompt_value_in[...].astype(F32).reshape(PT * HEADS, D)
    for h in range(HEADS):
        tail = jnp.where(at == 0, wide[h : h + 1], jnp.where(at == 1, totals[h : h + 1], 0.0))
        query_out[h] = prompt_q[pl.ds(h, PT, HEADS), :]
        k = prompt_k[pl.ds(h, PT, HEADS), :]
        v = prompt_v[pl.ds(h, PT, HEADS), :]
        for ref, half in zip((mine, theirs), choose(pack(v, 0), pack(v, 1))):
            ref[h, 64:80, :] = k
            ref[h, 80:88, :] = half
            ref[h, 88:96, :] = tail
    for copy in copies[5:]:
        copy.wait()
    rows_v[...] = value_in[0].astype(F32).reshape(T * HEADS, D)
    rows_k[...] = key_in[0].astype(F32).reshape(T * HEADS, D)
    for h in range(HEADS):
        k = jnp.where(live, rows_k[pl.ds(h, T, HEADS), :], 0.0)
        v = jnp.where(live, rows_v[pl.ds(h, T, HEADS), :], 0.0).astype(BF16)
        key_out[h] = k.astype(BF16)
        value_out[h] = v
        state = dot_right(v, k * to_end[:, h : h + 1], 0, 0)
        for ref, half in zip((mine, theirs), choose(state[0:64], state[64:128])):
            ref[h, 0:64, :] = half


def merge_kernel(mine, other, query, out, first_out, totals_out):
    at = iota((8, D), 0)
    for h in range(HEADS):
        first, last = in_order(mine[h], other[h])
        totals_out[h : h + 1, :] = first[89:90]
        totals_out[HEADS + h : HEADS + h + 1, :] = last[89:90]
        first_out[h] = first[0:64]
        out[h, 0:64, :] = jnp.exp(last[89:90]) * first[0:64] + last[0:64]
        out[h, 64:80, :] = first[64:80]
        out[h, 80:96, :] = last[64:80]
        out[h, 96:104, :] = first[80:88]
        out[h, 104:112, :] = last[80:88]
        tile = jnp.where(at == 0, first[88:89], jnp.where(at == 1, first[89:90], 0.0))
        out[h, 112:120, :] = jnp.where(at == 2, last[88:89], jnp.where(at == 3, last[89:90], tile))
        out[h, 120:136, :] = query[h]


def wide_columns(columns):
    return jnp.concatenate([columns, jnp.zeros((T, D - HEADS), F32)], axis=1)


def reply_local_kernel(
    lengths, query, grad, key, decay, gain, prompt_grad,
    query_out, grad_out, weights_out, growth_out, scale_out, upstream_out,
    query_in, grad_in, rows, rows_g, prompt_rows, sems,
):
    copies = start_copies([(query, query_in), (grad, grad_in)], sems)
    live = live_tokens(lengths)
    lines = running_rows(decay[0])
    columns = running_columns(decay[0])
    growth_out[...] = wide_columns(jnp.exp(columns))
    scale = gain[...].astype(F32)
    scale_out[...] = scale
    prompt_rows[...] = prompt_grad[...].astype(F32).reshape(PT * HEADS, D)
    for h in range(HEADS):
        upstream_out[h] = prompt_rows[pl.ds(h, PT, HEADS), :] * scale[h : h + 1]
    for copy in copies:
        copy.wait()
    rows[...] = query_in[0].astype(F32).reshape(T * HEADS, D)
    rows_g[...] = grad_in[0].astype(F32).reshape(T * HEADS, D)
    for h in range(HEADS):
        q = jnp.where(live, rows[pl.ds(h, T, HEADS), :], 0.0).astype(BF16)
        query_out[h] = q
        mask = masking(columns[:, h : h + 1], lines[h : h + 1])
        weights_out[h] = (dot(q, key[h], 1, 1) * mask).astype(BF16)
        grad_out[h] = jnp.where(live, rows_g[pl.ds(h, T, HEADS), :], 0.0).astype(BF16)


def prompt_row_kernel(received, out, column_out, query_out, blocks_out):
    decay = jnp.concatenate([received[:, 112, :], received[:, 114, :]], axis=0)
    token_block, token_place = iota((ROW, CTX), 0) // PT, iota((ROW, D), 0) % PT
    at = iota((ROW, CTX), 1)
    block = jnp.where(at < CHIPS, 2 * at, 2 * (at - CHIPS) + 1)
    parts = split3(decay)
    own = sum(dot((block == token_block).astype(BF16), part, 1, 0) for part in parts)
    before = sum(dot((block < token_block).astype(BF16), part, 1, 0) for part in parts)
    running = jnp.sum(before + jnp.where(iota((ROW, D), 1) <= token_place, own, 0.0), axis=1, keepdims=True)
    last = running[ROW - 1 : ROW]
    k = received[:, 64:96, :].reshape(ROW, D)
    v = rows_of_half(received[:, 96:112, :].reshape(CTX, 8, D)).astype(BF16)
    state = dot_right(v, k * jnp.exp(last - running), 0, 0)
    total = jnp.broadcast_to(last, (8, D))
    for s in range(SAMPLE):
        out[s, 0:64, :] = state
        out[s, 64:72, :] = total
    column_out[...] = jnp.broadcast_to(running, (ROW, D))
    query_out[...] = received[:, 120:136, :]
    blocks_out[...] = received[:, 113, :] + received[:, 115, :]


def same_block():
    return iota((ROW, ROW), 0) // PT == iota((ROW, ROW), 1) // PT


def prompt_weights(q, k, mask):
    scores = dot(q, k, 1, 1) * mask
    high = scores.astype(BF16)
    low = jnp.where(same_block(), 0.0, scores - high.astype(F32)).astype(BF16)
    return high, low


def prompt_local_kernel(
    received, other, column, query_out, key_out, value_out, line_out, local_out
):
    both = in_order(received[:, 120:136, :], other[...])
    q = jnp.concatenate(both, axis=1).reshape(ROW, D).astype(BF16)
    k = received[:, 64:96, :].reshape(ROW, D).astype(BF16)
    v = rows_of_half(received[:, 96:112, :].reshape(CTX, 8, D)).astype(BF16)
    running = column[:, 0:1]
    line = column_to_row(running)
    query_out[...] = q
    key_out[...] = k
    value_out[...] = v
    line_out[...] = jnp.broadcast_to(line, (8, ROW))
    weights = prompt_weights(q, k, masking(running, line))
    local_out[...] = sum(dot(part, v, 1, 0) for part in weights)


def fold_kernel(
    rows_received, received, blocks, query, local, column, after_reply, out, start_out, factors_out
):
    del after_reply
    place = lax.axis_index("sample")
    totals = [rows_received[s, 64:65, :] for s in range(SAMPLE)]
    end = jnp.zeros((HALF, D), F32)
    start = end
    for s in range(SAMPLE):
        start = jnp.where(place == s, end, start)
        end = jnp.exp(totals[s]) * end + rows_received[s, 0:64, :]
    start_out[...] = start
    state = end
    for y in range(CHIPS):
        out[y, 0:64, :] = state
        state = jnp.exp(blocks[y : y + 1, :]) * state + received[y, 0:64, :]
    outputs = local[...] + jnp.exp(column[:, 0:1]) * dot_right(query[...], start, 1, 1)
    out[:, 64:80, :] = packed_half(outputs).reshape(CHIPS, PT, D)
    for s in range(SAMPLE):
        after = jnp.zeros((1, D), F32)
        between = after
        for other in range(s + 1, SAMPLE):
            after = after + totals[other]
            between = between + jnp.where(other < place, totals[other], 0.0)
        factors_out[s : s + 1, :] = jnp.exp(after)
        factors_out[SAMPLE + s : SAMPLE + s + 1, :] = jnp.where(place > s, jnp.exp(between), 0.0)


def spread_kernel(received, first_state, totals, mine, theirs):
    for h in range(HEADS):
        before = received[h, 0:64, :]
        after = jnp.exp(totals[h : h + 1, :]) * before + first_state[h]
        mine[h, 0:64, :], theirs[h, 0:64, :] = choose(before, after)
        mine[h, 64:72, :], theirs[h, 64:72, :] = choose(received[h, 64:72, :], received[h, 72:80, :])


def output_kernel(
    mine, other, query, weights, value, grad, growth, scale, prompt_upstream, out, output_out, prompt_out
):
    squares = jnp.zeros((T, D), F32)
    crossed = jnp.zeros((T, D), F32)
    prompt_squares = jnp.zeros((PT, D), F32)
    prompt_crossed = jnp.zeros((PT, D), F32)
    for h in range(HEADS):
        low, high = in_order(mine[h], other[h])
        state = jnp.concatenate([low[0:64], high[0:64]], axis=0)
        outputs = dot(weights[h], value[h], 1, 0) + growth[:, h : h + 1] * dot_right(query[h], state, 1, 1)
        output_out[h] = outputs
        upstream = grad[h].astype(F32) * scale[h : h + 1, :]
        squares = squares + outputs * outputs
        crossed = crossed + upstream * outputs
        outputs = unpack(low[64:72], high[64:72])
        prompt_out[h] = outputs
        prompt_squares = prompt_squares + outputs * outputs
        prompt_crossed = prompt_crossed + prompt_upstream[h] * outputs
    sums = [
        column_to_row(jnp.sum(part, axis=1, keepdims=True))
        for part in (squares, crossed, prompt_squares, prompt_crossed)
    ]
    at = iota((8, D), 0)
    tile = jnp.zeros((8, D), F32)
    for i, part in enumerate(sums):
        tile = jnp.where(at == i, part, tile)
    for x in range(HEAD_AXIS):
        out[x] = tile


def norm_terms(squares, crossed):
    inverse = lax.rsqrt(squares / FEATURES + EPSILON)
    return inverse, crossed * inverse * inverse / FEATURES


def grad_kernel(
    sums, outputs, prompt_outputs, query, grad, growth, scale, prompt_upstream, mine, theirs, grad_out
):
    total = sums[0] + sums[1] + sums[2] + sums[3]
    inverse, project = norm_terms(row_to_column(total[0:1], T), row_to_column(total[1:2], T))
    prompt_inverse, prompt_project = norm_terms(row_to_column(total[2:3], PT), row_to_column(total[3:4], PT))
    for h in range(HEADS):
        upstream = grad[h].astype(F32) * scale[h : h + 1, :]
        out_grad = ((upstream - outputs[h] * project) * inverse).astype(BF16)
        grad_out[h] = out_grad
        back = dot_right(out_grad, query[h].astype(F32) * growth[:, h : h + 1], 0, 0)
        prompt_out_grad = (prompt_upstream[h] - prompt_outputs[h] * prompt_project) * prompt_inverse
        prompt_out_grad = prompt_out_grad.astype(BF16).astype(F32)
        mine[h, 0:64, :], theirs[h, 0:64, :] = choose(back[0:64], back[64:128])
        mine[h, 64:72, :], theirs[h, 64:72, :] = choose(pack(prompt_out_grad, 0), pack(prompt_out_grad, 1))


def back_merge_kernel(mine, other, totals, after_reply, out, last_out):
    del after_reply
    for h in range(HEADS):
        first, last = in_order(mine[h], other[h])
        last_out[h] = last[0:64]
        out[h, 0:64, :] = first[0:64] + jnp.exp(totals[h : h + 1, :]) * last[0:64]
        out[h, 64:72, :] = first[64:72]
        out[h, 72:80, :] = last[64:72]


def reply_back_kernel(
    mine, other, out_grad, query, key, value, weights, decay, query_grad, key_local, value_local, to_end_out
):
    lines = running_rows(decay[0])
    columns = running_columns(decay[0])
    scales = jnp.exp(columns)
    to_end_out[...] = wide_columns(jnp.exp(columns[T - 1 : T, :] - columns))
    for h in range(HEADS):
        state = jnp.concatenate(in_order(mine[h, 0:64, :], other[h, 0:64, :]), axis=0)
        og = out_grad[h]
        mask = masking(columns[:, h : h + 1], lines[h : h + 1])
        mix = (dot(og, value[h], 1, 1) * mask).astype(BF16)
        query_grad[h] = dot(mix, key[h], 1, 0) + scales[:, h : h + 1] * dot_right(og, state, 1, 0)
        key_local[h] = dot(mix, query[h], 0, 0)
        value_local[h] = dot(weights[h], og, 0, 0)


def back_fold_kernel(received, blocks, factors, query, column, rows_out):
    adjoint = jnp.zeros((HALF, D), F32)
    for y in range(CHIPS - 1, -1, -1):
        adjoint = jnp.exp(blocks[y : y + 1, :]) * adjoint + received[y, 0:64, :]
    og = rows_of_half(received[:, 64:80, :].reshape(CTX, 8, D)).astype(BF16)
    back = dot_right(og, query[...].astype(F32) * jnp.exp(column[:, 0:1]), 0, 0)
    for s in range(SAMPLE):
        rows_out[s] = factors[s : s + 1, :] * adjoint + factors[SAMPLE + s : SAMPLE + s + 1, :] * back


def prompt_mid_kernel(
    received, blocks, start, query, key, value, column, line, reply_query, out, swap_out, reply_query_grad, rows
):
    for h in range(HEADS):
        rows[pl.ds(h, T, HEADS), :] = reply_query[h]
    reply_query_grad[0] = rows[...].reshape(T, HEADS, D).astype(BF16)
    adjoint = jnp.zeros((HALF, D), F32)
    for y in range(CHIPS - 1, -1, -1):
        out[y, 0:64, :] = adjoint
        adjoint = jnp.exp(blocks[y : y + 1, :]) * adjoint + received[y, 0:64, :]
    og = rows_of_half(received[:, 64:80, :].reshape(CTX, 8, D)).astype(BF16)
    running = column[:, 0:1]
    mask = masking(running, line[0:1, :])
    mix = split(dot(og, value[...], 1, 1) * mask)
    k, q = key[...], query[...]
    query_grad = sum(dot(part, k, 1, 0) for part in mix) + jnp.exp(running) * dot_right(og, start[...], 1, 0)
    query_grad = query_grad.reshape(CHIPS, 2 * PT, D)
    key_local = sum(dot(part, q, 0, 0) for part in mix)
    value_local = sum(dot(part, og, 0, 0) for part in prompt_weights(q, k, mask))
    out[:, 64:96, :] = key_local.reshape(CHIPS, 2 * PT, D)
    out[:, 96:112, :] = packed_half(value_local).reshape(CHIPS, PT, D)
    out[:, 112:128, :], swap_out[...] = choose(query_grad[:, 0:PT], query_grad[:, PT:])


def prompt_back_kernel(rows_received, swapped, key, value, column, message, out):
    adjoint = rows_received[0]
    for s in range(1, SAMPLE):
        adjoint = adjoint + rows_received[s]
    running = column[:, 0:1]
    to_end = jnp.exp(running[ROW - 1 : ROW] - running)
    key_grad = to_end * dot_right(value[...], adjoint, 1, 0)
    value_grad = to_end * dot_right(key[...], adjoint, 1, 1)
    out[:, 0:64, :] = message[:, 0:64, :]
    out[:, 64:96, :] = message[:, 64:96, :] + key_grad.reshape(CHIPS, 2 * PT, D)
    out[:, 96:112, :] = message[:, 96:112, :] + packed_half(value_grad).reshape(CHIPS, PT, D)
    out[:, 112:128, :] = message[:, 112:128, :] + swapped[...]


def back_spread_kernel(received, last_back, totals, mine, theirs):
    for h in range(HEADS):
        after = received[h, 0:64, :]
        before = jnp.exp(totals[HEADS + h : HEADS + h + 1, :]) * after + last_back[h]
        mine[h, 0:64, :], theirs[h, 0:64, :] = choose(before, after)
        mine[h, 64:80, :], theirs[h, 64:80, :] = choose(received[h, 64:80, :], received[h, 80:96, :])
        mine[h, 80:88, :], theirs[h, 80:88, :] = choose(received[h, 96:104, :], received[h, 104:112, :])


def end_kernel(
    received, mine, other, key, value, key_local, value_local, to_end,
    key_grad, value_grad, prompt_query_grad, prompt_key_grad, prompt_value_grad,
    rows_k, rows_v, prompt_q, prompt_k, prompt_v,
):
    for h in range(HEADS):
        low, high = in_order(mine[h], other[h])
        adjoint = jnp.concatenate([low[0:64], high[0:64]], axis=0)
        scale = to_end[:, h : h + 1]
        rows_k[pl.ds(h, T, HEADS), :] = key_local[h] + scale * dot_right(value[h], adjoint, 1, 0)
        rows_v[pl.ds(h, T, HEADS), :] = value_local[h] + scale * dot_right(key[h], adjoint, 1, 1)
        prompt_k[pl.ds(h, PT, HEADS), :] = low[64:80] + high[64:80]
        prompt_v[pl.ds(h, PT, HEADS), :] = unpack(low[80:88], high[80:88])
        prompt_q[pl.ds(h, PT, HEADS), :] = received[h, 112:128, :]
    key_grad[0] = rows_k[...].reshape(T, HEADS, D).astype(BF16)
    value_grad[0] = rows_v[...].reshape(T, HEADS, D).astype(BF16)
    prompt_query_grad[...] = prompt_q[...].reshape(PT, HEADS, D).astype(BF16)
    prompt_key_grad[...] = prompt_k[...].reshape(PT, HEADS, D).astype(BF16)
    prompt_value_grad[...] = prompt_v[...].reshape(PT, HEADS, D).astype(BF16)


VMEM = pl.BlockSpec(memory_space=pltpu.VMEM)
SMEM = pl.BlockSpec(memory_space=pltpu.SMEM)
HBM = pl.BlockSpec(memory_space=pltpu.HBM)
REPLY_ROWS = pltpu.VMEM((T * HEADS, D), F32)
PROMPT_ROWS = pltpu.VMEM((PT * HEADS, D), F32)
BY_HEAD = ((HEADS, T, D), BF16)
BY_HEAD_WIDE = ((HEADS, T, D), F32)
REPLY = ((1, T, HEADS, D), BF16)
PROMPT = ((PT, HEADS, D), BF16)


def run(kernel, outs, scratch, *operands, hbm=(), kept=(), flops=0):
    operands = [
        pltpu.with_memory_space_constraint(operand, pltpu.HBM) if i in hbm else operand
        for i, operand in enumerate(operands)
    ]
    specs = [
        SMEM if operand.dtype == jnp.int32 else HBM if i in hbm else VMEM for i, operand in enumerate(operands)
    ]
    moved = sum(operand.size * operand.dtype.itemsize for operand in operands)
    return pl.pallas_call(
        kernel,
        out_shape=[
            pltpu.VMEM(shape, kind) if i in kept else jax.ShapeDtypeStruct(shape, kind)
            for i, (shape, kind) in enumerate(outs)
        ],
        in_specs=specs,
        out_specs=[VMEM] * len(outs),
        scratch_shapes=scratch,
        compiler_params=pltpu.CompilerParams(vmem_limit_bytes=8 * 1024 * 1024),
        cost_estimate=pl.CostEstimate(flops=flops, bytes_accessed=2 * moved, transcendentals=0),
        name=kernel.__name__,
    )(*operands)


def exchange(x, axis):
    return lax.all_to_all(x, axis, 0, 0, tiled=True)


def exchange_chips(x):
    groups = [[2 * chip + core for chip in range(CHIPS)] for core in range(2)]
    return lax.all_to_all(x, "ctx", 0, 0, axis_index_groups=groups, tiled=True)


def swap_cores(x):
    return lax.ppermute(x, "ctx", [(i, i ^ 1) for i in range(CTX)])


def shards(
    prompt_query,
    prompt_key,
    prompt_value,
    prompt_grad,
    prompt_decay,
    reply_query,
    reply_key,
    reply_value,
    reply_grad,
    reply_decay,
    reply_lengths,
    norm_gain,
):
    work = 8 * 2 * T * D * D
    reply_in, prompt_in = pltpu.VMEM(*REPLY), pltpu.VMEM(*PROMPT)
    mine, theirs, own_query, key, value = run(
        send_kernel,
        [((HEADS, 96, D), F32), ((HEADS, 96, D), F32), ((HEADS, PT, D), F32), BY_HEAD, BY_HEAD],
        [reply_in, reply_in, pltpu.VMEM((1, HEADS, T), F32)]
        + [prompt_in] * 3
        + [pltpu.VMEM((HEADS, PT), F32)]
        + [REPLY_ROWS] * 2
        + [PROMPT_ROWS] * 3
        + [pltpu.SemaphoreType.DMA((7,))],
        reply_lengths,
        reply_key,
        reply_value,
        reply_decay,
        prompt_query,
        prompt_key,
        prompt_value,
        prompt_decay,
        hbm=range(1, 8),
        flops=2 * work,
        kept=(0, 2, 3, 4),
    )
    sent, first_state, block_totals = run(
        merge_kernel,
        [((HEADS, 136, D), F32), ((HEADS, HALF, D), F32), ((2 * HEADS, D), F32)],
        [],
        mine,
        swap_cores(theirs),
        own_query,
        kept=(1, 2),
    )
    first = exchange_chips(sent)
    sent, column, half_query, blocks = run(
        prompt_row_kernel,
        [((SAMPLE, 72, D), F32), ((ROW, D), F32), ((CHIPS, PT, D), F32), ((CHIPS, D), F32)],
        [],
        first,
        kept=(1, 3),
    )
    rows = exchange(sent, "sample")
    query, grad, weights, growth, scale, prompt_upstream = run(
        reply_local_kernel,
        [BY_HEAD, BY_HEAD, BY_HEAD, ((T, D), F32), ((HEADS, D), F32), ((HEADS, PT, D), F32)],
        [reply_in, reply_in, REPLY_ROWS, REPLY_ROWS, PROMPT_ROWS, pltpu.SemaphoreType.DMA((2,))],
        reply_lengths,
        reply_query,
        reply_grad,
        key,
        reply_decay,
        norm_gain,
        prompt_grad,
        hbm=(1, 2),
        flops=2 * work,
        kept=range(6),
    )
    row_query, row_key, row_value, line, row_local = run(
        prompt_local_kernel,
        [
            ((ROW, D), BF16),
            ((ROW, D), BF16),
            ((ROW, HALF), BF16),
            ((8, ROW), F32),
            ((ROW, HALF), F32),
        ],
        [],
        first,
        swap_cores(half_query),
        column,
        flops=work,
        kept=range(5),
    )
    sent, start, factors = run(
        fold_kernel,
        [((CHIPS, 80, D), F32), ((HALF, D), F32), ((2 * SAMPLE, D), F32)],
        [],
        rows,
        first,
        blocks,
        row_query,
        row_local,
        column,
        scale,
        kept=(1, 2),
    )
    mine, theirs = run(
        spread_kernel,
        [((HEADS, 72, D), F32), ((HEADS, 72, D), F32)],
        [],
        exchange_chips(sent),
        first_state,
        block_totals,
        kept=(0,),
    )
    other = swap_cores(theirs)
    sent, outputs, prompt_outputs = run(
        output_kernel,
        [((HEAD_AXIS, 8, D), F32), BY_HEAD_WIDE, ((HEADS, PT, D), F32)],
        [],
        mine,
        other,
        query,
        weights,
        value,
        grad,
        growth,
        scale,
        prompt_upstream,
        flops=2 * work,
        kept=(1, 2),
    )
    sums = exchange(sent, "head")
    back_mine, back_theirs, out_grad = run(
        grad_kernel,
        [((HEADS, 72, D), F32), ((HEADS, 72, D), F32), BY_HEAD],
        [],
        sums,
        outputs,
        prompt_outputs,
        query,
        grad,
        growth,
        scale,
        prompt_upstream,
        flops=2 * work,
        kept=(0, 2),
    )
    back_other = swap_cores(back_theirs)
    reply_query_wide, key_local, value_local, to_end = run(
        reply_back_kernel,
        [BY_HEAD_WIDE, BY_HEAD_WIDE, BY_HEAD_WIDE, ((T, D), F32)],
        [],
        mine,
        other,
        out_grad,
        query,
        key,
        value,
        weights,
        reply_decay,
        flops=6 * work,
        kept=(0, 1, 2, 3),
    )
    sent, last_back = run(
        back_merge_kernel,
        [((HEADS, 80, D), F32), ((HEADS, HALF, D), F32)],
        [],
        back_mine,
        back_other,
        block_totals,
        to_end,
        kept=(1,),
    )
    backs = exchange_chips(sent)
    (sent,) = run(
        back_fold_kernel,
        [((SAMPLE, HALF, D), F32)],
        [],
        backs,
        blocks,
        factors,
        row_query,
        column,
    )
    rows = exchange(sent, "sample")
    message, swap, reply_query_grad = run(
        prompt_mid_kernel,
        [((CHIPS, 128, D), F32), ((CHIPS, PT, D), F32), REPLY],
        [REPLY_ROWS],
        backs,
        blocks,
        start,
        row_query,
        row_key,
        row_value,
        column,
        line,
        reply_query_wide,
        flops=work,
        kept=(0,),
    )
    (sent,) = run(
        prompt_back_kernel,
        [((CHIPS, 128, D), F32)],
        [],
        rows,
        swap_cores(swap),
        row_key,
        row_value,
        column,
        message,
    )
    received = exchange_chips(sent)
    end_mine, end_theirs = run(
        back_spread_kernel,
        [((HEADS, 88, D), F32), ((HEADS, 88, D), F32)],
        [],
        received,
        last_back,
        block_totals,
        kept=(0,),
    )
    reply_key_grad, reply_value_grad, prompt_query_grad, prompt_key_grad, prompt_value_grad = run(
        end_kernel,
        [REPLY, REPLY, PROMPT, PROMPT, PROMPT],
        [REPLY_ROWS] * 2 + [PROMPT_ROWS] * 3,
        received,
        end_mine,
        swap_cores(end_theirs),
        key,
        value,
        key_local,
        value_local,
        to_end,
        flops=4 * work,
    )
    return (
        prompt_query_grad,
        prompt_key_grad,
        prompt_value_grad,
        reply_query_grad,
        reply_key_grad,
        reply_value_grad,
    )


def solution(mesh):
    prompt = P(("sample", "ctx"), "head", None)
    reply = P("sample", "ctx", "head", None)
    in_specs = (
        (prompt,) * 4
        + (P("head", ("sample", "ctx")),)
        + (reply,) * 4
        + (P("sample", "head", "ctx"), P("sample"), P("head", None))
    )
    out_specs = (prompt,) * 3 + (reply,) * 3
    return jax.shard_map(shards, mesh=mesh, in_specs=in_specs, out_specs=out_specs, check_vma=False)
```

```python
import jax
import jax.numpy as jnp
from jax import lax
from jax.experimental import pallas as pl
from jax.experimental.pallas import tpu as pltpu
from jax.sharding import PartitionSpec as P

EPSILON = 1e-05
F32 = jnp.float32
BF16 = jnp.bfloat16
HEADS = 8
D = 128
HALF = D // 2
T = 128
PT = 16
CTX = 16
CHIPS = 8
SAMPLE = 8
HEAD_AXIS = 4
ROW = CTX * PT
FEATURES = float(HEADS * HEAD_AXIS * D)


def iota(shape, axis):
    return lax.broadcasted_iota(jnp.int32, shape, axis)


def dot(a, b, ca, cb):
    return lax.dot_general(a, b, (((ca,), (cb,)), ((), ())), preferred_element_type=F32)


def split(x):
    high = x.astype(BF16)
    return high, (x - high.astype(F32)).astype(BF16)


def split3(x):
    high, rest = x.astype(BF16), None
    rest = x - high.astype(F32)
    mid = rest.astype(BF16)
    return high, mid, (rest - mid.astype(F32)).astype(BF16)


def dot_right(a, x, ca, cb):
    return sum(dot(a, part, ca, cb) for part in split(x))


def dot_left(x, b, ca, cb):
    return sum(dot(part, b, ca, cb) for part in split(x))


def low_lanes(rows):
    return iota((rows, D), 1) < HALF


def pack(x, half):
    top, bottom, low = x[0:8], x[8:16], low_lanes(8)
    if half == 0:
        return jnp.where(low, top, pltpu.roll(bottom, HALF, 1))
    return jnp.where(low, pltpu.roll(top, HALF, 1), bottom)


def unpack(first, second):
    low = low_lanes(8)
    top = jnp.where(low, first, pltpu.roll(second, HALF, 1))
    bottom = jnp.where(low, pltpu.roll(first, HALF, 1), second)
    return jnp.concatenate([top, bottom], axis=0)


def rows_of_half(x):
    both = jnp.stack([x[:, :, :HALF], x[:, :, HALF:]], axis=1)
    return both.reshape(ROW, HALF)


def packed_half(x):
    both = x.reshape(CTX, 2, 8, HALF)
    return jnp.concatenate([both[:, 0], both[:, 1]], axis=-1)


def running_rows(decay):
    upper = (iota((T, T), 0) <= iota((T, T), 1)).astype(BF16)
    return sum(dot(part, upper, 1, 0) for part in split3(decay))


def running_columns(decay):
    lower = (iota((T, T), 1) <= iota((T, T), 0)).astype(BF16)
    return sum(dot(lower, part, 1, 1) for part in split3(decay))


def masking(column, row):
    extent = row.shape[1]
    causal = iota((extent, extent), 0) >= iota((extent, extent), 1)
    return jnp.where(causal, jnp.exp(jnp.where(causal, column - row, 0.0)), 0.0)


def column_to_row(column):
    extent = column.shape[0]
    eye = iota((extent, max(extent, D)), 0) == iota((extent, max(extent, D)), 1)
    return jnp.sum(jnp.where(eye, column, 0.0), axis=0, keepdims=True)


def row_to_column(row, extent):
    eye = iota((extent, row.shape[1]), 0) == iota((extent, row.shape[1]), 1)
    return jnp.sum(jnp.where(eye, row, 0.0), axis=1, keepdims=True)


def live_tokens(lengths):
    return lax.axis_index("ctx") * T + iota((T, 1), 0) < lengths[0]


def second_core():
    return lax.axis_index("ctx") % 2 == 1


def in_order(mine, other):
    second = second_core()
    return jnp.where(second, other, mine), jnp.where(second, mine, other)


def choose(first, last):
    return in_order(first, last)


def half_lanes(x, other_core):
    x = x.astype(F32)
    own, other = choose(x[:, 0:HALF], x[:, HALF:D])
    return (other if other_core else own).astype(BF16)


def wide_columns(columns):
    return jnp.concatenate([columns, jnp.zeros((T, D - HEADS), F32)], axis=1)


def start_copies(pairs, sems):
    copies = [pltpu.make_async_copy(source, target, sems.at[i]) for i, (source, target) in enumerate(pairs)]
    for copy in copies:
        copy.start()
    return copies


def send_kernel(
    lengths, key, value, decay, prompt_query, prompt_key, prompt_value, prompt_decay,
    mine_prompt, theirs, query_out, key_out, value_out, to_end_out,
    key_in, value_in, decay_in, query_in, prompt_key_in, prompt_value_in, prompt_decay_in,
    rows_k, rows_v, prompt_q, prompt_k, prompt_v, sems,
):
    copies = start_copies(
        [
            (decay, decay_in),
            (prompt_decay, prompt_decay_in),
            (prompt_query, query_in),
            (prompt_key, prompt_key_in),
            (prompt_value, prompt_value_in),
            (value, value_in),
            (key, key_in),
        ],
        sems,
    )
    live = live_tokens(lengths)
    for copy in copies[:5]:
        copy.wait()
    columns = running_columns(decay_in[0])
    to_end = jnp.exp(columns[T - 1 : T, :] - columns)
    wide = jnp.concatenate([prompt_decay_in[...], jnp.zeros((HEADS, D - PT), F32)], axis=1)
    totals = jnp.sum(decay_in[0], axis=1, keepdims=True)
    at = iota((8, D), 0)
    prompt_q[...] = query_in[...].astype(F32).reshape(PT * HEADS, D)
    prompt_k[...] = prompt_key_in[...].astype(F32).reshape(PT * HEADS, D)
    prompt_v[...] = prompt_value_in[...].astype(F32).reshape(PT * HEADS, D)
    for h in range(HEADS):
        tail = jnp.where(at == 0, wide[h : h + 1], jnp.where(at == 1, totals[h : h + 1], 0.0))
        query_out[h] = prompt_q[pl.ds(h, PT, HEADS), :]
        k = prompt_k[pl.ds(h, PT, HEADS), :]
        v = prompt_v[pl.ds(h, PT, HEADS), :]
        own, sent = choose(pack(v, 0), pack(v, 1))
        for ref, row, half in ((mine_prompt, 0, own), (theirs, 64, sent)):
            ref[h, row : row + 16, :] = k
            ref[h, row + 16 : row + 24, :] = half
            ref[h, row + 24 : row + 32, :] = tail
    for copy in copies[5:]:
        copy.wait()
    rows_v[...] = value_in[0].astype(F32).reshape(T * HEADS, D)
    rows_k[...] = key_in[0].astype(F32).reshape(T * HEADS, D)
    for h in range(HEADS):
        k = jnp.where(live, rows_k[pl.ds(h, T, HEADS), :], 0.0)
        v = jnp.where(live, rows_v[pl.ds(h, T, HEADS), :], 0.0).astype(BF16)
        key_out[h] = k.astype(BF16)
        value_out[h] = v
        theirs[h, 0:64, :] = dot_right(half_lanes(v, other_core=True), k * to_end[:, h : h + 1], 0, 0)
    to_end_out[...] = wide_columns(to_end)


def own_half_kernel(key, value, to_end, mine):
    for h in range(HEADS):
        weighted = key[h].astype(F32) * to_end[:, h : h + 1]
        mine[h] = dot_right(half_lanes(value[h], other_core=False), weighted, 0, 0)


def reply_masks_kernel(weights, value, decay, after_fold, mask_out, local_out):
    del after_fold
    lines = running_rows(decay[0])
    columns = running_columns(decay[0])
    for h in range(HEADS):
        mask_out[h] = masking(columns[:, h : h + 1], lines[h : h + 1])
        local_out[h] = dot(weights[h], value[h], 1, 0)


def merge_kernel(mine_state, mine_prompt, other, query, out, first_out, totals_out):
    at = iota((8, D), 0)
    for h in range(HEADS):
        mine = jnp.concatenate([mine_state[h], mine_prompt[h]], axis=0)
        first, last = in_order(mine, other[h])
        totals_out[h : h + 1, :] = first[89:90]
        totals_out[HEADS + h : HEADS + h + 1, :] = last[89:90]
        first_out[h] = first[0:64]
        out[h, 0:64, :] = jnp.exp(last[89:90]) * first[0:64] + last[0:64]
        out[h, 64:80, :] = first[64:80]
        out[h, 80:96, :] = last[64:80]
        out[h, 96:104, :] = first[80:88]
        out[h, 104:112, :] = last[80:88]
        tile = jnp.where(at == 0, first[88:89], jnp.where(at == 1, first[89:90], 0.0))
        out[h, 112:120, :] = jnp.where(at == 2, last[88:89], jnp.where(at == 3, last[89:90], tile))
        out[h, 120:136, :] = query[h]


def reply_local_kernel(
    lengths, query, grad, key, decay, gain, prompt_grad,
    query_out, grad_out, weights_out, growth_out, scale_out, upstream_out,
    query_in, grad_in, rows, rows_g, prompt_rows, sems,
):
    copies = start_copies([(query, query_in), (grad, grad_in)], sems)
    live = live_tokens(lengths)
    lines = running_rows(decay[0])
    columns = running_columns(decay[0])
    growth_out[...] = wide_columns(jnp.exp(columns))
    scale = gain[...].astype(F32)
    scale_out[...] = scale
    prompt_rows[...] = prompt_grad[...].astype(F32).reshape(PT * HEADS, D)
    for h in range(HEADS):
        upstream_out[h] = prompt_rows[pl.ds(h, PT, HEADS), :] * scale[h : h + 1]
    for copy in copies:
        copy.wait()
    rows[...] = query_in[0].astype(F32).reshape(T * HEADS, D)
    rows_g[...] = grad_in[0].astype(F32).reshape(T * HEADS, D)
    for h in range(HEADS):
        q = jnp.where(live, rows[pl.ds(h, T, HEADS), :], 0.0).astype(BF16)
        query_out[h] = q
        mask = masking(columns[:, h : h + 1], lines[h : h + 1])
        weights_out[h] = (dot(q, key[h], 1, 1) * mask).astype(BF16)
        grad_out[h] = jnp.where(live, rows_g[pl.ds(h, T, HEADS), :], 0.0).astype(BF16)


def prompt_row_kernel(received, out, column_out, query_out, blocks_out):
    decay = jnp.concatenate([received[:, 112, :], received[:, 114, :]], axis=0)
    token_block, token_place = iota((ROW, CTX), 0) // PT, iota((ROW, D), 0) % PT
    at = iota((ROW, CTX), 1)
    block = jnp.where(at < CHIPS, 2 * at, 2 * (at - CHIPS) + 1)
    parts = split3(decay)
    own = sum(dot((block == token_block).astype(BF16), part, 1, 0) for part in parts)
    before = sum(dot((block < token_block).astype(BF16), part, 1, 0) for part in parts)
    running = jnp.sum(before + jnp.where(iota((ROW, D), 1) <= token_place, own, 0.0), axis=1, keepdims=True)
    last = running[ROW - 1 : ROW]
    k = received[:, 64:96, :].reshape(ROW, D)
    v = rows_of_half(received[:, 96:112, :].reshape(CTX, 8, D)).astype(BF16)
    state = dot_right(v, k * jnp.exp(last - running), 0, 0)
    total = jnp.broadcast_to(last, (8, D))
    for s in range(SAMPLE):
        out[s, 0:64, :] = state
        out[s, 64:72, :] = total
    column_out[...] = jnp.broadcast_to(running, (ROW, D))
    query_out[...] = received[:, 120:136, :]
    blocks_out[...] = received[:, 113, :] + received[:, 115, :]


def same_block():
    return iota((ROW, ROW), 0) // PT == iota((ROW, ROW), 1) // PT


def prompt_weights(q, k, mask):
    scores = dot(q, k, 1, 1) * mask
    high = scores.astype(BF16)
    low = jnp.where(same_block(), 0.0, scores - high.astype(F32)).astype(BF16)
    return high, low


def prompt_local_kernel(
    received, other, column, query_out, key_out, value_out, line_out, local_out
):
    both = in_order(received[:, 120:136, :], other[...])
    q = jnp.concatenate(both, axis=1).reshape(ROW, D).astype(BF16)
    k = received[:, 64:96, :].reshape(ROW, D).astype(BF16)
    v = rows_of_half(received[:, 96:112, :].reshape(CTX, 8, D)).astype(BF16)
    running = column[:, 0:1]
    line = column_to_row(running)
    query_out[...] = q
    key_out[...] = k
    value_out[...] = v
    line_out[...] = jnp.broadcast_to(line, (8, ROW))
    weights = prompt_weights(q, k, masking(running, line))
    local_out[...] = sum(dot(part, v, 1, 0) for part in weights)


def fold_kernel(
    rows_received, received, blocks, query, local, column, after_reply, out, start_out, factors_out
):
    del after_reply
    place = lax.axis_index("sample")
    totals = [rows_received[s, 64:65, :] for s in range(SAMPLE)]
    end = jnp.zeros((HALF, D), F32)
    start = end
    for s in range(SAMPLE):
        start = jnp.where(place == s, end, start)
        end = jnp.exp(totals[s]) * end + rows_received[s, 0:64, :]
    start_out[...] = start
    state = end
    for y in range(CHIPS):
        out[y, 0:64, :] = state
        state = jnp.exp(blocks[y : y + 1, :]) * state + received[y, 0:64, :]
    outputs = local[...] + jnp.exp(column[:, 0:1]) * dot_right(query[...], start, 1, 1)
    out[:, 64:80, :] = packed_half(outputs).reshape(CHIPS, PT, D)
    for s in range(SAMPLE):
        after = jnp.zeros((1, D), F32)
        between = after
        for other in range(s + 1, SAMPLE):
            after = after + totals[other]
            between = between + jnp.where(other < place, totals[other], 0.0)
        factors_out[s : s + 1, :] = jnp.exp(after)
        factors_out[SAMPLE + s : SAMPLE + s + 1, :] = jnp.where(place > s, jnp.exp(between), 0.0)


def spread_kernel(received, first_state, totals, mine, theirs):
    for h in range(HEADS):
        before = received[h, 0:64, :]
        after = jnp.exp(totals[h : h + 1, :]) * before + first_state[h]
        mine[h, 0:64, :], theirs[h, 0:64, :] = choose(before, after)
        mine[h, 64:72, :], theirs[h, 64:72, :] = choose(received[h, 64:72, :], received[h, 72:80, :])


def output_kernel(
    mine, other, query, local, grad, growth, scale, prompt_upstream, out, output_out, prompt_out
):
    squares = jnp.zeros((T, D), F32)
    crossed = jnp.zeros((T, D), F32)
    prompt_squares = jnp.zeros((PT, D), F32)
    prompt_crossed = jnp.zeros((PT, D), F32)
    for h in range(HEADS):
        low, high = in_order(mine[h], other[h])
        state = jnp.concatenate([low[0:64], high[0:64]], axis=0)
        outputs = local[h] + growth[:, h : h + 1] * dot_right(query[h], state, 1, 1)
        output_out[h] = outputs
        upstream = grad[h].astype(F32) * scale[h : h + 1, :]
        squares = squares + outputs * outputs
        crossed = crossed + upstream * outputs
        outputs = unpack(low[64:72], high[64:72])
        prompt_out[h] = outputs
        prompt_squares = prompt_squares + outputs * outputs
        prompt_crossed = prompt_crossed + prompt_upstream[h] * outputs
    sums = [
        column_to_row(jnp.sum(part, axis=1, keepdims=True))
        for part in (squares, crossed, prompt_squares, prompt_crossed)
    ]
    at = iota((8, D), 0)
    tile = jnp.zeros((8, D), F32)
    for i, part in enumerate(sums):
        tile = jnp.where(at == i, part, tile)
    for x in range(HEAD_AXIS):
        out[x] = tile


def norm_terms(squares, crossed):
    inverse = lax.rsqrt(squares / FEATURES + EPSILON)
    return inverse, crossed * inverse * inverse / FEATURES


def grad_kernel(
    sums, outputs, prompt_outputs, query, grad, growth, scale, prompt_upstream, mine, theirs, grad_out
):
    total = sums[0] + sums[1] + sums[2] + sums[3]
    inverse, project = norm_terms(row_to_column(total[0:1], T), row_to_column(total[1:2], T))
    prompt_inverse, prompt_project = norm_terms(row_to_column(total[2:3], PT), row_to_column(total[3:4], PT))
    for h in range(HEADS):
        upstream = grad[h].astype(F32) * scale[h : h + 1, :]
        out_grad = ((upstream - outputs[h] * project) * inverse).astype(BF16)
        grad_out[h] = out_grad
        back = dot_right(out_grad, query[h].astype(F32) * growth[:, h : h + 1], 0, 0)
        prompt_out_grad = (prompt_upstream[h] - prompt_outputs[h] * prompt_project) * prompt_inverse
        prompt_out_grad = prompt_out_grad.astype(BF16).astype(F32)
        mine[h, 0:64, :], theirs[h, 0:64, :] = choose(back[0:64], back[64:128])
        mine[h, 64:72, :], theirs[h, 64:72, :] = choose(pack(prompt_out_grad, 0), pack(prompt_out_grad, 1))


def back_merge_kernel(mine, other, totals, after_reply, out, last_out):
    del after_reply
    for h in range(HEADS):
        first, last = in_order(mine[h], other[h])
        last_out[h] = last[0:64]
        out[h, 0:64, :] = first[0:64] + jnp.exp(totals[h : h + 1, :]) * last[0:64]
        out[h, 64:72, :] = first[64:72]
        out[h, 72:80, :] = last[64:72]


def reply_back_kernel(
    mine, other, out_grad, query, key, value, weights, masks, growth, query_grad, key_local, value_local
):
    for h in range(HEADS):
        state = jnp.concatenate(in_order(mine[h, 0:64, :], other[h, 0:64, :]), axis=0)
        og = out_grad[h]
        mix = (dot(og, value[h], 1, 1) * masks[h]).astype(BF16)
        query_grad[h] = dot(mix, key[h], 1, 0) + growth[:, h : h + 1] * dot_right(og, state, 1, 0)
        key_local[h] = dot(mix, query[h], 0, 0)
        value_local[h] = dot(weights[h], og, 0, 0)


def back_fold_kernel(received, blocks, factors, query, column, rows_out):
    adjoint = jnp.zeros((HALF, D), F32)
    for y in range(CHIPS - 1, -1, -1):
        adjoint = jnp.exp(blocks[y : y + 1, :]) * adjoint + received[y, 0:64, :]
    og = rows_of_half(received[:, 64:80, :].reshape(CTX, 8, D)).astype(BF16)
    back = dot_right(og, query[...].astype(F32) * jnp.exp(column[:, 0:1]), 0, 0)
    for s in range(SAMPLE):
        rows_out[s] = factors[s : s + 1, :] * adjoint + factors[SAMPLE + s : SAMPLE + s + 1, :] * back


def prompt_mid_kernel(
    received, blocks, start, query, key, value, column, line, reply_query, out, swap_out, reply_query_grad, rows
):
    for h in range(HEADS):
        rows[pl.ds(h, T, HEADS), :] = reply_query[h]
    reply_query_grad[0] = rows[...].reshape(T, HEADS, D).astype(BF16)
    adjoint = jnp.zeros((HALF, D), F32)
    for y in range(CHIPS - 1, -1, -1):
        out[y, 0:64, :] = adjoint
        adjoint = jnp.exp(blocks[y : y + 1, :]) * adjoint + received[y, 0:64, :]
    og = rows_of_half(received[:, 64:80, :].reshape(CTX, 8, D)).astype(BF16)
    running = column[:, 0:1]
    mask = masking(running, line[0:1, :])
    mix = split(dot(og, value[...], 1, 1) * mask)
    k, q = key[...], query[...]
    query_grad = sum(dot(part, k, 1, 0) for part in mix) + jnp.exp(running) * dot_right(og, start[...], 1, 0)
    query_grad = query_grad.reshape(CHIPS, 2 * PT, D)
    key_local = sum(dot(part, q, 0, 0) for part in mix)
    value_local = sum(dot(part, og, 0, 0) for part in prompt_weights(q, k, mask))
    out[:, 64:96, :] = key_local.reshape(CHIPS, 2 * PT, D)
    out[:, 96:112, :] = packed_half(value_local).reshape(CHIPS, PT, D)
    out[:, 112:128, :], swap_out[...] = choose(query_grad[:, 0:PT], query_grad[:, PT:])


def prompt_back_kernel(rows_received, swapped, key, value, column, message, out):
    adjoint = rows_received[0]
    for s in range(1, SAMPLE):
        adjoint = adjoint + rows_received[s]
    running = column[:, 0:1]
    to_end = jnp.exp(running[ROW - 1 : ROW] - running)
    key_grad = to_end * dot_right(value[...], adjoint, 1, 0)
    value_grad = to_end * dot_right(key[...], adjoint, 1, 1)
    out[:, 0:64, :] = message[:, 0:64, :]
    out[:, 64:96, :] = message[:, 64:96, :] + key_grad.reshape(CHIPS, 2 * PT, D)
    out[:, 96:112, :] = message[:, 96:112, :] + packed_half(value_grad).reshape(CHIPS, PT, D)
    out[:, 112:128, :] = message[:, 112:128, :] + swapped[...]


def back_spread_kernel(received, last_back, totals, mine, theirs):
    for h in range(HEADS):
        after = received[h, 0:64, :]
        before = jnp.exp(totals[HEADS + h : HEADS + h + 1, :]) * after + last_back[h]
        mine[h, 0:64, :], theirs[h, 0:64, :] = choose(before, after)
        mine[h, 64:80, :], theirs[h, 64:80, :] = choose(received[h, 64:80, :], received[h, 80:96, :])
        mine[h, 80:88, :], theirs[h, 80:88, :] = choose(received[h, 96:104, :], received[h, 104:112, :])


def end_kernel(
    received, mine, other, key, value, key_local, value_local, to_end,
    key_grad, value_grad, prompt_query_grad, prompt_key_grad, prompt_value_grad,
    rows_k, rows_v, prompt_q, prompt_k, prompt_v,
):
    for h in range(HEADS):
        low, high = in_order(mine[h], other[h])
        adjoint = jnp.concatenate([low[0:64], high[0:64]], axis=0)
        scale = to_end[:, h : h + 1]
        rows_k[pl.ds(h, T, HEADS), :] = key_local[h] + scale * dot_right(value[h], adjoint, 1, 0)
        rows_v[pl.ds(h, T, HEADS), :] = value_local[h] + scale * dot_right(key[h], adjoint, 1, 1)
        prompt_k[pl.ds(h, PT, HEADS), :] = low[64:80] + high[64:80]
        prompt_v[pl.ds(h, PT, HEADS), :] = unpack(low[80:88], high[80:88])
        prompt_q[pl.ds(h, PT, HEADS), :] = received[h, 112:128, :]
    key_grad[0] = rows_k[...].reshape(T, HEADS, D).astype(BF16)
    value_grad[0] = rows_v[...].reshape(T, HEADS, D).astype(BF16)
    prompt_query_grad[...] = prompt_q[...].reshape(PT, HEADS, D).astype(BF16)
    prompt_key_grad[...] = prompt_k[...].reshape(PT, HEADS, D).astype(BF16)
    prompt_value_grad[...] = prompt_v[...].reshape(PT, HEADS, D).astype(BF16)


VMEM = pl.BlockSpec(memory_space=pltpu.VMEM)
SMEM = pl.BlockSpec(memory_space=pltpu.SMEM)
HBM = pl.BlockSpec(memory_space=pltpu.HBM)
REPLY_ROWS = pltpu.VMEM((T * HEADS, D), F32)
PROMPT_ROWS = pltpu.VMEM((PT * HEADS, D), F32)
BY_HEAD = ((HEADS, T, D), BF16)
BY_HEAD_WIDE = ((HEADS, T, D), F32)
REPLY = ((1, T, HEADS, D), BF16)
PROMPT = ((PT, HEADS, D), BF16)


def run(kernel, outs, scratch, *operands, hbm=(), kept=(), flops=0):
    operands = [
        pltpu.with_memory_space_constraint(operand, pltpu.HBM) if i in hbm else operand
        for i, operand in enumerate(operands)
    ]
    specs = [
        SMEM if operand.dtype == jnp.int32 else HBM if i in hbm else VMEM for i, operand in enumerate(operands)
    ]
    moved = sum(operand.size * operand.dtype.itemsize for operand in operands)
    return pl.pallas_call(
        kernel,
        out_shape=[
            pltpu.VMEM(shape, kind) if i in kept else jax.ShapeDtypeStruct(shape, kind)
            for i, (shape, kind) in enumerate(outs)
        ],
        in_specs=specs,
        out_specs=[VMEM] * len(outs),
        scratch_shapes=scratch,
        compiler_params=pltpu.CompilerParams(vmem_limit_bytes=8 * 1024 * 1024),
        cost_estimate=pl.CostEstimate(flops=flops, bytes_accessed=2 * moved, transcendentals=0),
        name=kernel.__name__,
    )(*operands)


def exchange(x, axis):
    return lax.all_to_all(x, axis, 0, 0, tiled=True)


def exchange_chips(x):
    groups = [[2 * chip + core for chip in range(CHIPS)] for core in range(2)]
    return lax.all_to_all(x, "ctx", 0, 0, axis_index_groups=groups, tiled=True)


def swap_cores(x):
    return lax.ppermute(x, "ctx", [(i, i ^ 1) for i in range(CTX)])


def shards(
    prompt_query,
    prompt_key,
    prompt_value,
    prompt_grad,
    prompt_decay,
    reply_query,
    reply_key,
    reply_value,
    reply_grad,
    reply_decay,
    reply_lengths,
    norm_gain,
):
    work = 8 * 2 * T * D * D
    reply_in, prompt_in = pltpu.VMEM(*REPLY), pltpu.VMEM(*PROMPT)
    own_prompt, theirs, own_query, key, value, to_end = run(
        send_kernel,
        [
            ((HEADS, 32, D), F32),
            ((HEADS, 96, D), F32),
            ((HEADS, PT, D), F32),
            BY_HEAD,
            BY_HEAD,
            ((T, D), F32),
        ],
        [reply_in, reply_in, pltpu.VMEM((1, HEADS, T), F32)]
        + [prompt_in] * 3
        + [pltpu.VMEM((HEADS, PT), F32)]
        + [REPLY_ROWS] * 2
        + [PROMPT_ROWS] * 3
        + [pltpu.SemaphoreType.DMA((7,))],
        reply_lengths,
        reply_key,
        reply_value,
        reply_decay,
        prompt_query,
        prompt_key,
        prompt_value,
        prompt_decay,
        hbm=range(1, 8),
        flops=2 * work,
        kept=(0, 2, 3, 4, 5),
    )
    other = swap_cores(theirs)
    (own_state,) = run(
        own_half_kernel, [((HEADS, HALF, D), F32)], [], key, value, to_end, flops=work, kept=(0,)
    )
    sent, first_state, block_totals = run(
        merge_kernel,
        [((HEADS, 136, D), F32), ((HEADS, HALF, D), F32), ((2 * HEADS, D), F32)],
        [],
        own_state,
        own_prompt,
        other,
        own_query,
        kept=(1, 2),
    )
    first = exchange_chips(sent)
    sent, column, half_query, blocks = run(
        prompt_row_kernel,
        [((SAMPLE, 72, D), F32), ((ROW, D), F32), ((CHIPS, PT, D), F32), ((CHIPS, D), F32)],
        [],
        first,
        kept=(1, 3),
    )
    rows = exchange(sent, "sample")
    query, grad, weights, growth, scale, prompt_upstream = run(
        reply_local_kernel,
        [BY_HEAD, BY_HEAD, BY_HEAD, ((T, D), F32), ((HEADS, D), F32), ((HEADS, PT, D), F32)],
        [reply_in, reply_in, REPLY_ROWS, REPLY_ROWS, PROMPT_ROWS, pltpu.SemaphoreType.DMA((2,))],
        reply_lengths,
        reply_query,
        reply_grad,
        key,
        reply_decay,
        norm_gain,
        prompt_grad,
        hbm=(1, 2),
        flops=2 * work,
        kept=range(6),
    )
    row_query, row_key, row_value, line, row_local = run(
        prompt_local_kernel,
        [
            ((ROW, D), BF16),
            ((ROW, D), BF16),
            ((ROW, HALF), BF16),
            ((8, ROW), F32),
            ((ROW, HALF), F32),
        ],
        [],
        first,
        swap_cores(half_query),
        column,
        flops=work,
        kept=range(5),
    )
    sent, start, factors = run(
        fold_kernel,
        [((CHIPS, 80, D), F32), ((HALF, D), F32), ((2 * SAMPLE, D), F32)],
        [],
        rows,
        first,
        blocks,
        row_query,
        row_local,
        column,
        scale,
        kept=(1, 2),
    )
    mine, theirs = run(
        spread_kernel,
        [((HEADS, 72, D), F32), ((HEADS, 72, D), F32)],
        [],
        exchange_chips(sent),
        first_state,
        block_totals,
        kept=(0,),
    )
    other = swap_cores(theirs)
    masks, local = run(
        reply_masks_kernel,
        [BY_HEAD_WIDE, BY_HEAD_WIDE],
        [],
        weights,
        value,
        reply_decay,
        mine,
        flops=work,
        kept=(0, 1),
    )
    sent, outputs, prompt_outputs = run(
        output_kernel,
        [((HEAD_AXIS, 8, D), F32), BY_HEAD_WIDE, ((HEADS, PT, D), F32)],
        [],
        mine,
        other,
        query,
        local,
        grad,
        growth,
        scale,
        prompt_upstream,
        flops=2 * work,
        kept=(1, 2),
    )
    sums = exchange(sent, "head")
    back_mine, back_theirs, out_grad = run(
        grad_kernel,
        [((HEADS, 72, D), F32), ((HEADS, 72, D), F32), BY_HEAD],
        [],
        sums,
        outputs,
        prompt_outputs,
        query,
        grad,
        growth,
        scale,
        prompt_upstream,
        flops=2 * work,
        kept=(0, 2),
    )
    back_other = swap_cores(back_theirs)
    reply_query_wide, key_local, value_local = run(
        reply_back_kernel,
        [BY_HEAD_WIDE, BY_HEAD_WIDE, BY_HEAD_WIDE],
        [],
        mine,
        other,
        out_grad,
        query,
        key,
        value,
        weights,
        masks,
        growth,
        flops=6 * work,
        kept=(0, 1, 2),
    )
    sent, last_back = run(
        back_merge_kernel,
        [((HEADS, 80, D), F32), ((HEADS, HALF, D), F32)],
        [],
        back_mine,
        back_other,
        block_totals,
        reply_query_wide,
        kept=(1,),
    )
    backs = exchange_chips(sent)
    (sent,) = run(
        back_fold_kernel,
        [((SAMPLE, HALF, D), F32)],
        [],
        backs,
        blocks,
        factors,
        row_query,
        column,
    )
    rows = exchange(sent, "sample")
    message, swap, reply_query_grad = run(
        prompt_mid_kernel,
        [((CHIPS, 128, D), F32), ((CHIPS, PT, D), F32), REPLY],
        [REPLY_ROWS],
        backs,
        blocks,
        start,
        row_query,
        row_key,
        row_value,
        column,
        line,
        reply_query_wide,
        flops=work,
        kept=(0,),
    )
    (sent,) = run(
        prompt_back_kernel,
        [((CHIPS, 128, D), F32)],
        [],
        rows,
        swap_cores(swap),
        row_key,
        row_value,
        column,
        message,
    )
    received = exchange_chips(sent)
    end_mine, end_theirs = run(
        back_spread_kernel,
        [((HEADS, 88, D), F32), ((HEADS, 88, D), F32)],
        [],
        received,
        last_back,
        block_totals,
        kept=(0,),
    )
    reply_key_grad, reply_value_grad, prompt_query_grad, prompt_key_grad, prompt_value_grad = run(
        end_kernel,
        [REPLY, REPLY, PROMPT, PROMPT, PROMPT],
        [REPLY_ROWS] * 2 + [PROMPT_ROWS] * 3,
        received,
        end_mine,
        swap_cores(end_theirs),
        key,
        value,
        key_local,
        value_local,
        to_end,
        flops=4 * work,
    )
    return (
        prompt_query_grad,
        prompt_key_grad,
        prompt_value_grad,
        reply_query_grad,
        reply_key_grad,
        reply_value_grad,
    )


def solution(mesh):
    prompt = P(("sample", "ctx"), "head", None)
    reply = P("sample", "ctx", "head", None)
    in_specs = (
        (prompt,) * 4
        + (P("head", ("sample", "ctx")),)
        + (reply,) * 4
        + (P("sample", "head", "ctx"), P("sample"), P("head", None))
    )
    out_specs = (prompt,) * 3 + (reply,) * 3
    return jax.shard_map(shards, mesh=mesh, in_specs=in_specs, out_specs=out_specs, check_vma=False)
```

```python
import jax
import jax.numpy as jnp
from jax import lax
from jax.experimental import pallas as pl
from jax.experimental.pallas import tpu as pltpu
from jax.sharding import PartitionSpec as P

EPSILON = 1e-05
F32 = jnp.float32
BF16 = jnp.bfloat16
HEADS = 8
D = 128
HALF = D // 2
T = 128
PT = 16
CTX = 16
CHIPS = 8
SAMPLE = 8
HEAD_AXIS = 4
ROW = CTX * PT
FEATURES = float(HEADS * HEAD_AXIS * D)


def iota(shape, axis):
    return lax.broadcasted_iota(jnp.int32, shape, axis)


def dot(a, b, ca, cb):
    return lax.dot_general(a, b, (((ca,), (cb,)), ((), ())), preferred_element_type=F32)


def split(x):
    high = x.astype(BF16)
    return high, (x - high.astype(F32)).astype(BF16)


def split3(x):
    high, rest = x.astype(BF16), None
    rest = x - high.astype(F32)
    mid = rest.astype(BF16)
    return high, mid, (rest - mid.astype(F32)).astype(BF16)


def dot_right(a, x, ca, cb):
    return sum(dot(a, part, ca, cb) for part in split(x))


def dot_left(x, b, ca, cb):
    return sum(dot(part, b, ca, cb) for part in split(x))


def low_lanes(rows):
    return iota((rows, D), 1) < HALF


def pack(x, half):
    top, bottom, low = x[0:8], x[8:16], low_lanes(8)
    if half == 0:
        return jnp.where(low, top, pltpu.roll(bottom, HALF, 1))
    return jnp.where(low, pltpu.roll(top, HALF, 1), bottom)


def unpack(first, second):
    low = low_lanes(8)
    top = jnp.where(low, first, pltpu.roll(second, HALF, 1))
    bottom = jnp.where(low, pltpu.roll(first, HALF, 1), second)
    return jnp.concatenate([top, bottom], axis=0)


def rows_of_half(x):
    both = jnp.stack([x[:, :, :HALF], x[:, :, HALF:]], axis=1)
    return both.reshape(ROW, HALF)


def packed_half(x):
    both = x.reshape(CTX, 2, 8, HALF)
    return jnp.concatenate([both[:, 0], both[:, 1]], axis=-1)


def running_rows(decay):
    upper = (iota((T, T), 0) <= iota((T, T), 1)).astype(BF16)
    return sum(dot(part, upper, 1, 0) for part in split3(decay))


def running_columns(decay):
    lower = (iota((T, T), 1) <= iota((T, T), 0)).astype(BF16)
    return sum(dot(lower, part, 1, 1) for part in split3(decay))


def masking(column, row):
    extent = row.shape[1]
    causal = iota((extent, extent), 0) >= iota((extent, extent), 1)
    return jnp.where(causal, jnp.exp(jnp.where(causal, column - row, 0.0)), 0.0)


def column_to_row(column):
    extent = column.shape[0]
    eye = iota((extent, max(extent, D)), 0) == iota((extent, max(extent, D)), 1)
    return jnp.sum(jnp.where(eye, column, 0.0), axis=0, keepdims=True)


def row_to_column(row, extent):
    eye = iota((extent, row.shape[1]), 0) == iota((extent, row.shape[1]), 1)
    return jnp.sum(jnp.where(eye, row, 0.0), axis=1, keepdims=True)


def live_tokens(lengths):
    return lax.axis_index("ctx") * T + iota((T, 1), 0) < lengths[0]


def second_core():
    return lax.axis_index("ctx") % 2 == 1


def in_order(mine, other):
    second = second_core()
    return jnp.where(second, other, mine), jnp.where(second, mine, other)


def choose(first, last):
    return in_order(first, last)


def start_copies(pairs, sems):
    copies = [pltpu.make_async_copy(source, target, sems.at[i]) for i, (source, target) in enumerate(pairs)]
    for copy in copies:
        copy.start()
    return copies


def send_kernel(
    lengths, key, value, decay, prompt_query, prompt_key, prompt_value, prompt_decay,
    mine, theirs, query_out, key_out, value_out,
    key_in, value_in, decay_in, query_in, prompt_key_in, prompt_value_in, prompt_decay_in,
    rows_k, rows_v, prompt_q, prompt_k, prompt_v, sems,
):
    copies = start_copies(
        [
            (decay, decay_in),
            (prompt_decay, prompt_decay_in),
            (prompt_query, query_in),
            (prompt_key, prompt_key_in),
            (prompt_value, prompt_value_in),
            (value, value_in),
            (key, key_in),
        ],
        sems,
    )
    live = live_tokens(lengths)
    for copy in copies[:5]:
        copy.wait()
    columns = running_columns(decay_in[0])
    to_end = jnp.exp(columns[T - 1 : T, :] - columns)
    wide = jnp.concatenate([prompt_decay_in[...], jnp.zeros((HEADS, D - PT), F32)], axis=1)
    totals = jnp.sum(decay_in[0], axis=1, keepdims=True)
    at = iota((8, D), 0)
    prompt_q[...] = query_in[...].astype(F32).reshape(PT * HEADS, D)
    prompt_k[...] = prompt_key_in[...].astype(F32).reshape(PT * HEADS, D)
    prompt_v[...] = prompt_value_in[...].astype(F32).reshape(PT * HEADS, D)
    for h in range(HEADS):
        tail = jnp.where(at == 0, wide[h : h + 1], jnp.where(at == 1, totals[h : h + 1], 0.0))
        query_out[h] = prompt_q[pl.ds(h, PT, HEADS), :]
        k = prompt_k[pl.ds(h, PT, HEADS), :]
        v = prompt_v[pl.ds(h, PT, HEADS), :]
        for ref, half in zip((mine, theirs), choose(pack(v, 0), pack(v, 1))):
            ref[h, 64:80, :] = k
            ref[h, 80:88, :] = half
            ref[h, 88:96, :] = tail
    for copy in copies[5:]:
        copy.wait()
    rows_v[...] = value_in[0].astype(F32).reshape(T * HEADS, D)
    rows_k[...] = key_in[0].astype(F32).reshape(T * HEADS, D)
    for h in range(HEADS):
        k = jnp.where(live, rows_k[pl.ds(h, T, HEADS), :], 0.0)
        v = jnp.where(live, rows_v[pl.ds(h, T, HEADS), :], 0.0).astype(BF16)
        key_out[h] = k.astype(BF16)
        value_out[h] = v
        state = dot_right(v, k * to_end[:, h : h + 1], 0, 0)
        for ref, half in zip((mine, theirs), choose(state[0:64], state[64:128])):
            ref[h, 0:64, :] = half


def reply_masks_kernel(weights, value, decay, after_fold, mask_out, local_out):
    del after_fold
    lines = running_rows(decay[0])
    columns = running_columns(decay[0])
    for h in range(HEADS):
        mask_out[h] = masking(columns[:, h : h + 1], lines[h : h + 1])
        local_out[h] = dot(weights[h], value[h], 1, 0)


def merge_kernel(mine, other, query, out, first_out, totals_out):
    at = iota((8, D), 0)
    for h in range(HEADS):
        first, last = in_order(mine[h], other[h])
        totals_out[h : h + 1, :] = first[89:90]
        totals_out[HEADS + h : HEADS + h + 1, :] = last[89:90]
        first_out[h] = first[0:64]
        out[h, 0:64, :] = jnp.exp(last[89:90]) * first[0:64] + last[0:64]
        out[h, 64:80, :] = first[64:80]
        out[h, 80:96, :] = last[64:80]
        out[h, 96:104, :] = first[80:88]
        out[h, 104:112, :] = last[80:88]
        tile = jnp.where(at == 0, first[88:89], jnp.where(at == 1, first[89:90], 0.0))
        out[h, 112:120, :] = jnp.where(at == 2, last[88:89], jnp.where(at == 3, last[89:90], tile))
        out[h, 120:136, :] = query[h]


def wide_columns(columns):
    return jnp.concatenate([columns, jnp.zeros((T, D - HEADS), F32)], axis=1)


def reply_local_kernel(
    lengths, query, grad, key, decay, gain, prompt_grad,
    query_out, grad_out, weights_out, growth_out, scale_out, upstream_out,
    query_in, grad_in, rows, rows_g, prompt_rows, sems,
):
    copies = start_copies([(query, query_in), (grad, grad_in)], sems)
    live = live_tokens(lengths)
    lines = running_rows(decay[0])
    columns = running_columns(decay[0])
    growth_out[...] = wide_columns(jnp.exp(columns))
    scale = gain[...].astype(F32)
    scale_out[...] = scale
    prompt_rows[...] = prompt_grad[...].astype(F32).reshape(PT * HEADS, D)
    for h in range(HEADS):
        upstream_out[h] = prompt_rows[pl.ds(h, PT, HEADS), :] * scale[h : h + 1]
    for copy in copies:
        copy.wait()
    rows[...] = query_in[0].astype(F32).reshape(T * HEADS, D)
    rows_g[...] = grad_in[0].astype(F32).reshape(T * HEADS, D)
    for h in range(HEADS):
        q = jnp.where(live, rows[pl.ds(h, T, HEADS), :], 0.0).astype(BF16)
        query_out[h] = q
        mask = masking(columns[:, h : h + 1], lines[h : h + 1])
        weights_out[h] = (dot(q, key[h], 1, 1) * mask).astype(BF16)
        grad_out[h] = jnp.where(live, rows_g[pl.ds(h, T, HEADS), :], 0.0).astype(BF16)


def prompt_row_kernel(received, out, column_out, query_out, blocks_out):
    decay = jnp.concatenate([received[:, 112, :], received[:, 114, :]], axis=0)
    token_block, token_place = iota((ROW, CTX), 0) // PT, iota((ROW, D), 0) % PT
    at = iota((ROW, CTX), 1)
    block = jnp.where(at < CHIPS, 2 * at, 2 * (at - CHIPS) + 1)
    parts = split3(decay)
    own = sum(dot((block == token_block).astype(BF16), part, 1, 0) for part in parts)
    before = sum(dot((block < token_block).astype(BF16), part, 1, 0) for part in parts)
    running = jnp.sum(before + jnp.where(iota((ROW, D), 1) <= token_place, own, 0.0), axis=1, keepdims=True)
    last = running[ROW - 1 : ROW]
    k = received[:, 64:96, :].reshape(ROW, D)
    v = rows_of_half(received[:, 96:112, :].reshape(CTX, 8, D)).astype(BF16)
    state = dot_right(v, k * jnp.exp(last - running), 0, 0)
    total = jnp.broadcast_to(last, (8, D))
    for s in range(SAMPLE):
        out[s, 0:64, :] = state
        out[s, 64:72, :] = total
    column_out[...] = jnp.broadcast_to(running, (ROW, D))
    query_out[...] = received[:, 120:136, :]
    blocks_out[...] = received[:, 113, :] + received[:, 115, :]


def same_block():
    return iota((ROW, ROW), 0) // PT == iota((ROW, ROW), 1) // PT


def prompt_weights(q, k, mask):
    scores = dot(q, k, 1, 1) * mask
    high = scores.astype(BF16)
    low = jnp.where(same_block(), 0.0, scores - high.astype(F32)).astype(BF16)
    return high, low


def prompt_local_kernel(
    received, other, column, query_out, key_out, value_out, line_out, local_out
):
    both = in_order(received[:, 120:136, :], other[...])
    q = jnp.concatenate(both, axis=1).reshape(ROW, D).astype(BF16)
    k = received[:, 64:96, :].reshape(ROW, D).astype(BF16)
    v = rows_of_half(received[:, 96:112, :].reshape(CTX, 8, D)).astype(BF16)
    running = column[:, 0:1]
    line = column_to_row(running)
    query_out[...] = q
    key_out[...] = k
    value_out[...] = v
    line_out[...] = jnp.broadcast_to(line, (8, ROW))
    weights = prompt_weights(q, k, masking(running, line))
    local_out[...] = sum(dot(part, v, 1, 0) for part in weights)


def fold_kernel(
    rows_received, received, blocks, query, local, column, after_reply, out, start_out, factors_out
):
    del after_reply
    place = lax.axis_index("sample")
    totals = [rows_received[s, 64:65, :] for s in range(SAMPLE)]
    end = jnp.zeros((HALF, D), F32)
    start = end
    for s in range(SAMPLE):
        start = jnp.where(place == s, end, start)
        end = jnp.exp(totals[s]) * end + rows_received[s, 0:64, :]
    start_out[...] = start
    state = end
    for y in range(CHIPS):
        out[y, 0:64, :] = state
        state = jnp.exp(blocks[y : y + 1, :]) * state + received[y, 0:64, :]
    outputs = local[...] + jnp.exp(column[:, 0:1]) * dot_right(query[...], start, 1, 1)
    out[:, 64:80, :] = packed_half(outputs).reshape(CHIPS, PT, D)
    for s in range(SAMPLE):
        after = jnp.zeros((1, D), F32)
        between = after
        for other in range(s + 1, SAMPLE):
            after = after + totals[other]
            between = between + jnp.where(other < place, totals[other], 0.0)
        factors_out[s : s + 1, :] = jnp.exp(after)
        factors_out[SAMPLE + s : SAMPLE + s + 1, :] = jnp.where(place > s, jnp.exp(between), 0.0)


def spread_kernel(received, first_state, totals, mine, theirs):
    for h in range(HEADS):
        before = received[h, 0:64, :]
        after = jnp.exp(totals[h : h + 1, :]) * before + first_state[h]
        mine[h, 0:64, :], theirs[h, 0:64, :] = choose(before, after)
        mine[h, 64:72, :], theirs[h, 64:72, :] = choose(received[h, 64:72, :], received[h, 72:80, :])


def output_kernel(
    mine, other, query, local, grad, growth, scale, prompt_upstream, out, output_out, prompt_out
):
    squares = jnp.zeros((T, D), F32)
    crossed = jnp.zeros((T, D), F32)
    prompt_squares = jnp.zeros((PT, D), F32)
    prompt_crossed = jnp.zeros((PT, D), F32)
    for h in range(HEADS):
        low, high = in_order(mine[h], other[h])
        state = jnp.concatenate([low[0:64], high[0:64]], axis=0)
        outputs = local[h] + growth[:, h : h + 1] * dot_right(query[h], state, 1, 1)
        output_out[h] = outputs
        upstream = grad[h].astype(F32) * scale[h : h + 1, :]
        squares = squares + outputs * outputs
        crossed = crossed + upstream * outputs
        outputs = unpack(low[64:72], high[64:72])
        prompt_out[h] = outputs
        prompt_squares = prompt_squares + outputs * outputs
        prompt_crossed = prompt_crossed + prompt_upstream[h] * outputs
    sums = [
        column_to_row(jnp.sum(part, axis=1, keepdims=True))
        for part in (squares, crossed, prompt_squares, prompt_crossed)
    ]
    at = iota((8, D), 0)
    tile = jnp.zeros((8, D), F32)
    for i, part in enumerate(sums):
        tile = jnp.where(at == i, part, tile)
    for x in range(HEAD_AXIS):
        out[x] = tile


def norm_terms(squares, crossed):
    inverse = lax.rsqrt(squares / FEATURES + EPSILON)
    return inverse, crossed * inverse * inverse / FEATURES


def grad_kernel(
    sums, outputs, prompt_outputs, query, grad, growth, scale, prompt_upstream, mine, theirs, grad_out
):
    total = sums[0] + sums[1] + sums[2] + sums[3]
    inverse, project = norm_terms(row_to_column(total[0:1], T), row_to_column(total[1:2], T))
    prompt_inverse, prompt_project = norm_terms(row_to_column(total[2:3], PT), row_to_column(total[3:4], PT))
    for h in range(HEADS):
        upstream = grad[h].astype(F32) * scale[h : h + 1, :]
        out_grad = ((upstream - outputs[h] * project) * inverse).astype(BF16)
        grad_out[h] = out_grad
        back = dot_right(out_grad, query[h].astype(F32) * growth[:, h : h + 1], 0, 0)
        prompt_out_grad = (prompt_upstream[h] - prompt_outputs[h] * prompt_project) * prompt_inverse
        prompt_out_grad = prompt_out_grad.astype(BF16).astype(F32)
        mine[h, 0:64, :], theirs[h, 0:64, :] = choose(back[0:64], back[64:128])
        mine[h, 64:72, :], theirs[h, 64:72, :] = choose(pack(prompt_out_grad, 0), pack(prompt_out_grad, 1))


def back_merge_kernel(mine, other, totals, after_reply, out, last_out):
    del after_reply
    for h in range(HEADS):
        first, last = in_order(mine[h], other[h])
        last_out[h] = last[0:64]
        out[h, 0:64, :] = first[0:64] + jnp.exp(totals[h : h + 1, :]) * last[0:64]
        out[h, 64:72, :] = first[64:72]
        out[h, 72:80, :] = last[64:72]


def reply_back_kernel(
    mine, other, out_grad, query, key, value, weights, masks, growth, decay,
    query_grad, key_local, value_local, to_end_out,
):
    columns = running_columns(decay[0])
    to_end_out[...] = wide_columns(jnp.exp(columns[T - 1 : T, :] - columns))
    for h in range(HEADS):
        state = jnp.concatenate(in_order(mine[h, 0:64, :], other[h, 0:64, :]), axis=0)
        og = out_grad[h]
        mix = (dot(og, value[h], 1, 1) * masks[h]).astype(BF16)
        query_grad[h] = dot(mix, key[h], 1, 0) + growth[:, h : h + 1] * dot_right(og, state, 1, 0)
        key_local[h] = dot(mix, query[h], 0, 0)
        value_local[h] = dot(weights[h], og, 0, 0)


def back_fold_kernel(received, blocks, factors, query, column, rows_out):
    adjoint = jnp.zeros((HALF, D), F32)
    for y in range(CHIPS - 1, -1, -1):
        adjoint = jnp.exp(blocks[y : y + 1, :]) * adjoint + received[y, 0:64, :]
    og = rows_of_half(received[:, 64:80, :].reshape(CTX, 8, D)).astype(BF16)
    back = dot_right(og, query[...].astype(F32) * jnp.exp(column[:, 0:1]), 0, 0)
    for s in range(SAMPLE):
        rows_out[s] = factors[s : s + 1, :] * adjoint + factors[SAMPLE + s : SAMPLE + s + 1, :] * back


def prompt_mid_kernel(
    received, blocks, start, query, key, value, column, line, reply_query, out, swap_out, reply_query_grad, rows
):
    for h in range(HEADS):
        rows[pl.ds(h, T, HEADS), :] = reply_query[h]
    reply_query_grad[0] = rows[...].reshape(T, HEADS, D).astype(BF16)
    adjoint = jnp.zeros((HALF, D), F32)
    for y in range(CHIPS - 1, -1, -1):
        out[y, 0:64, :] = adjoint
        adjoint = jnp.exp(blocks[y : y + 1, :]) * adjoint + received[y, 0:64, :]
    og = rows_of_half(received[:, 64:80, :].reshape(CTX, 8, D)).astype(BF16)
    running = column[:, 0:1]
    mask = masking(running, line[0:1, :])
    mix = split(dot(og, value[...], 1, 1) * mask)
    k, q = key[...], query[...]
    query_grad = sum(dot(part, k, 1, 0) for part in mix) + jnp.exp(running) * dot_right(og, start[...], 1, 0)
    query_grad = query_grad.reshape(CHIPS, 2 * PT, D)
    key_local = sum(dot(part, q, 0, 0) for part in mix)
    value_local = sum(dot(part, og, 0, 0) for part in prompt_weights(q, k, mask))
    out[:, 64:96, :] = key_local.reshape(CHIPS, 2 * PT, D)
    out[:, 96:112, :] = packed_half(value_local).reshape(CHIPS, PT, D)
    out[:, 112:128, :], swap_out[...] = choose(query_grad[:, 0:PT], query_grad[:, PT:])


def prompt_back_kernel(rows_received, swapped, key, value, column, message, out):
    adjoint = rows_received[0]
    for s in range(1, SAMPLE):
        adjoint = adjoint + rows_received[s]
    running = column[:, 0:1]
    to_end = jnp.exp(running[ROW - 1 : ROW] - running)
    key_grad = to_end * dot_right(value[...], adjoint, 1, 0)
    value_grad = to_end * dot_right(key[...], adjoint, 1, 1)
    out[:, 0:64, :] = message[:, 0:64, :]
    out[:, 64:96, :] = message[:, 64:96, :] + key_grad.reshape(CHIPS, 2 * PT, D)
    out[:, 96:112, :] = message[:, 96:112, :] + packed_half(value_grad).reshape(CHIPS, PT, D)
    out[:, 112:128, :] = message[:, 112:128, :] + swapped[...]


def back_spread_kernel(received, last_back, totals, mine, theirs):
    for h in range(HEADS):
        after = received[h, 0:64, :]
        before = jnp.exp(totals[HEADS + h : HEADS + h + 1, :]) * after + last_back[h]
        mine[h, 0:64, :], theirs[h, 0:64, :] = choose(before, after)
        mine[h, 64:80, :], theirs[h, 64:80, :] = choose(received[h, 64:80, :], received[h, 80:96, :])
        mine[h, 80:88, :], theirs[h, 80:88, :] = choose(received[h, 96:104, :], received[h, 104:112, :])


def end_kernel(
    received, mine, other, key, value, key_local, value_local, to_end,
    key_grad, value_grad, prompt_query_grad, prompt_key_grad, prompt_value_grad,
    rows_k, rows_v, prompt_q, prompt_k, prompt_v,
):
    for h in range(HEADS):
        low, high = in_order(mine[h], other[h])
        adjoint = jnp.concatenate([low[0:64], high[0:64]], axis=0)
        scale = to_end[:, h : h + 1]
        rows_k[pl.ds(h, T, HEADS), :] = key_local[h] + scale * dot_right(value[h], adjoint, 1, 0)
        rows_v[pl.ds(h, T, HEADS), :] = value_local[h] + scale * dot_right(key[h], adjoint, 1, 1)
        prompt_k[pl.ds(h, PT, HEADS), :] = low[64:80] + high[64:80]
        prompt_v[pl.ds(h, PT, HEADS), :] = unpack(low[80:88], high[80:88])
        prompt_q[pl.ds(h, PT, HEADS), :] = received[h, 112:128, :]
    key_grad[0] = rows_k[...].reshape(T, HEADS, D).astype(BF16)
    value_grad[0] = rows_v[...].reshape(T, HEADS, D).astype(BF16)
    prompt_query_grad[...] = prompt_q[...].reshape(PT, HEADS, D).astype(BF16)
    prompt_key_grad[...] = prompt_k[...].reshape(PT, HEADS, D).astype(BF16)
    prompt_value_grad[...] = prompt_v[...].reshape(PT, HEADS, D).astype(BF16)


VMEM = pl.BlockSpec(memory_space=pltpu.VMEM)
SMEM = pl.BlockSpec(memory_space=pltpu.SMEM)
HBM = pl.BlockSpec(memory_space=pltpu.HBM)
REPLY_ROWS = pltpu.VMEM((T * HEADS, D), F32)
PROMPT_ROWS = pltpu.VMEM((PT * HEADS, D), F32)
BY_HEAD = ((HEADS, T, D), BF16)
BY_HEAD_WIDE = ((HEADS, T, D), F32)
REPLY = ((1, T, HEADS, D), BF16)
PROMPT = ((PT, HEADS, D), BF16)


def run(kernel, outs, scratch, *operands, hbm=(), kept=(), flops=0):
    operands = [
        pltpu.with_memory_space_constraint(operand, pltpu.HBM) if i in hbm else operand
        for i, operand in enumerate(operands)
    ]
    specs = [
        SMEM if operand.dtype == jnp.int32 else HBM if i in hbm else VMEM for i, operand in enumerate(operands)
    ]
    moved = sum(operand.size * operand.dtype.itemsize for operand in operands)
    return pl.pallas_call(
        kernel,
        out_shape=[
            pltpu.VMEM(shape, kind) if i in kept else jax.ShapeDtypeStruct(shape, kind)
            for i, (shape, kind) in enumerate(outs)
        ],
        in_specs=specs,
        out_specs=[VMEM] * len(outs),
        scratch_shapes=scratch,
        compiler_params=pltpu.CompilerParams(vmem_limit_bytes=8 * 1024 * 1024),
        cost_estimate=pl.CostEstimate(flops=flops, bytes_accessed=2 * moved, transcendentals=0),
        name=kernel.__name__,
    )(*operands)


def exchange(x, axis):
    return lax.all_to_all(x, axis, 0, 0, tiled=True)


def exchange_chips(x):
    groups = [[2 * chip + core for chip in range(CHIPS)] for core in range(2)]
    return lax.all_to_all(x, "ctx", 0, 0, axis_index_groups=groups, tiled=True)


def swap_cores(x):
    return lax.ppermute(x, "ctx", [(i, i ^ 1) for i in range(CTX)])


def shards(
    prompt_query,
    prompt_key,
    prompt_value,
    prompt_grad,
    prompt_decay,
    reply_query,
    reply_key,
    reply_value,
    reply_grad,
    reply_decay,
    reply_lengths,
    norm_gain,
):
    work = 8 * 2 * T * D * D
    reply_in, prompt_in = pltpu.VMEM(*REPLY), pltpu.VMEM(*PROMPT)
    mine, theirs, own_query, key, value = run(
        send_kernel,
        [((HEADS, 96, D), F32), ((HEADS, 96, D), F32), ((HEADS, PT, D), F32), BY_HEAD, BY_HEAD],
        [reply_in, reply_in, pltpu.VMEM((1, HEADS, T), F32)]
        + [prompt_in] * 3
        + [pltpu.VMEM((HEADS, PT), F32)]
        + [REPLY_ROWS] * 2
        + [PROMPT_ROWS] * 3
        + [pltpu.SemaphoreType.DMA((7,))],
        reply_lengths,
        reply_key,
        reply_value,
        reply_decay,
        prompt_query,
        prompt_key,
        prompt_value,
        prompt_decay,
        hbm=range(1, 8),
        flops=2 * work,
        kept=(0, 2, 3, 4),
    )
    sent, first_state, block_totals = run(
        merge_kernel,
        [((HEADS, 136, D), F32), ((HEADS, HALF, D), F32), ((2 * HEADS, D), F32)],
        [],
        mine,
        swap_cores(theirs),
        own_query,
        kept=(1, 2),
    )
    first = exchange_chips(sent)
    sent, column, half_query, blocks = run(
        prompt_row_kernel,
        [((SAMPLE, 72, D), F32), ((ROW, D), F32), ((CHIPS, PT, D), F32), ((CHIPS, D), F32)],
        [],
        first,
        kept=(1, 3),
    )
    rows = exchange(sent, "sample")
    query, grad, weights, growth, scale, prompt_upstream = run(
        reply_local_kernel,
        [BY_HEAD, BY_HEAD, BY_HEAD, ((T, D), F32), ((HEADS, D), F32), ((HEADS, PT, D), F32)],
        [reply_in, reply_in, REPLY_ROWS, REPLY_ROWS, PROMPT_ROWS, pltpu.SemaphoreType.DMA((2,))],
        reply_lengths,
        reply_query,
        reply_grad,
        key,
        reply_decay,
        norm_gain,
        prompt_grad,
        hbm=(1, 2),
        flops=2 * work,
        kept=range(6),
    )
    row_query, row_key, row_value, line, row_local = run(
        prompt_local_kernel,
        [
            ((ROW, D), BF16),
            ((ROW, D), BF16),
            ((ROW, HALF), BF16),
            ((8, ROW), F32),
            ((ROW, HALF), F32),
        ],
        [],
        first,
        swap_cores(half_query),
        column,
        flops=work,
        kept=range(5),
    )
    sent, start, factors = run(
        fold_kernel,
        [((CHIPS, 80, D), F32), ((HALF, D), F32), ((2 * SAMPLE, D), F32)],
        [],
        rows,
        first,
        blocks,
        row_query,
        row_local,
        column,
        scale,
        kept=(1, 2),
    )
    mine, theirs = run(
        spread_kernel,
        [((HEADS, 72, D), F32), ((HEADS, 72, D), F32)],
        [],
        exchange_chips(sent),
        first_state,
        block_totals,
        kept=(0,),
    )
    other = swap_cores(theirs)
    masks, local = run(
        reply_masks_kernel,
        [BY_HEAD_WIDE, BY_HEAD_WIDE],
        [],
        weights,
        value,
        reply_decay,
        mine,
        flops=work,
        kept=(0, 1),
    )
    sent, outputs, prompt_outputs = run(
        output_kernel,
        [((HEAD_AXIS, 8, D), F32), BY_HEAD_WIDE, ((HEADS, PT, D), F32)],
        [],
        mine,
        other,
        query,
        local,
        grad,
        growth,
        scale,
        prompt_upstream,
        flops=2 * work,
        kept=(1, 2),
    )
    sums = exchange(sent, "head")
    back_mine, back_theirs, out_grad = run(
        grad_kernel,
        [((HEADS, 72, D), F32), ((HEADS, 72, D), F32), BY_HEAD],
        [],
        sums,
        outputs,
        prompt_outputs,
        query,
        grad,
        growth,
        scale,
        prompt_upstream,
        flops=2 * work,
        kept=(0, 2),
    )
    back_other = swap_cores(back_theirs)
    reply_query_wide, key_local, value_local, to_end = run(
        reply_back_kernel,
        [BY_HEAD_WIDE, BY_HEAD_WIDE, BY_HEAD_WIDE, ((T, D), F32)],
        [],
        mine,
        other,
        out_grad,
        query,
        key,
        value,
        weights,
        masks,
        growth,
        reply_decay,
        flops=6 * work,
        kept=(0, 1, 2, 3),
    )
    sent, last_back = run(
        back_merge_kernel,
        [((HEADS, 80, D), F32), ((HEADS, HALF, D), F32)],
        [],
        back_mine,
        back_other,
        block_totals,
        to_end,
        kept=(1,),
    )
    backs = exchange_chips(sent)
    (sent,) = run(
        back_fold_kernel,
        [((SAMPLE, HALF, D), F32)],
        [],
        backs,
        blocks,
        factors,
        row_query,
        column,
    )
    rows = exchange(sent, "sample")
    message, swap, reply_query_grad = run(
        prompt_mid_kernel,
        [((CHIPS, 128, D), F32), ((CHIPS, PT, D), F32), REPLY],
        [REPLY_ROWS],
        backs,
        blocks,
        start,
        row_query,
        row_key,
        row_value,
        column,
        line,
        reply_query_wide,
        flops=work,
        kept=(0,),
    )
    (sent,) = run(
        prompt_back_kernel,
        [((CHIPS, 128, D), F32)],
        [],
        rows,
        swap_cores(swap),
        row_key,
        row_value,
        column,
        message,
    )
    received = exchange_chips(sent)
    end_mine, end_theirs = run(
        back_spread_kernel,
        [((HEADS, 88, D), F32), ((HEADS, 88, D), F32)],
        [],
        received,
        last_back,
        block_totals,
        kept=(0,),
    )
    reply_key_grad, reply_value_grad, prompt_query_grad, prompt_key_grad, prompt_value_grad = run(
        end_kernel,
        [REPLY, REPLY, PROMPT, PROMPT, PROMPT],
        [REPLY_ROWS] * 2 + [PROMPT_ROWS] * 3,
        received,
        end_mine,
        swap_cores(end_theirs),
        key,
        value,
        key_local,
        value_local,
        to_end,
        flops=4 * work,
    )
    return (
        prompt_query_grad,
        prompt_key_grad,
        prompt_value_grad,
        reply_query_grad,
        reply_key_grad,
        reply_value_grad,
    )


def solution(mesh):
    prompt = P(("sample", "ctx"), "head", None)
    reply = P("sample", "ctx", "head", None)
    in_specs = (
        (prompt,) * 4
        + (P("head", ("sample", "ctx")),)
        + (reply,) * 4
        + (P("sample", "head", "ctx"), P("sample"), P("head", None))
    )
    out_specs = (prompt,) * 3 + (reply,) * 3
    return jax.shard_map(shards, mesh=mesh, in_specs=in_specs, out_specs=out_specs, check_vma=False)
```

```python
import jax
import jax.numpy as jnp
from jax import lax
from jax.experimental import pallas as pl
from jax.experimental.pallas import tpu as pltpu
from jax.sharding import PartitionSpec as P

EPSILON = 1e-05
F32 = jnp.float32
BF16 = jnp.bfloat16
HEADS = 8
D = 128
HALF = D // 2
T = 128
PT = 16
CTX = 16
CHIPS = 8
SAMPLE = 8
HEAD_AXIS = 4
ROW = CTX * PT
FEATURES = float(HEADS * HEAD_AXIS * D)


def iota(shape, axis):
    return lax.broadcasted_iota(jnp.int32, shape, axis)


def dot(a, b, ca, cb):
    return lax.dot_general(a, b, (((ca,), (cb,)), ((), ())), preferred_element_type=F32)


def split(x):
    high = x.astype(BF16)
    return high, (x - high.astype(F32)).astype(BF16)


def split3(x):
    high, rest = x.astype(BF16), None
    rest = x - high.astype(F32)
    mid = rest.astype(BF16)
    return high, mid, (rest - mid.astype(F32)).astype(BF16)


def dot_right(a, x, ca, cb):
    return sum(dot(a, part, ca, cb) for part in split(x))


def dot_left(x, b, ca, cb):
    return sum(dot(part, b, ca, cb) for part in split(x))


def low_lanes(rows):
    return iota((rows, D), 1) < HALF


def pack(x, half):
    top, bottom, low = x[0:8], x[8:16], low_lanes(8)
    if half == 0:
        return jnp.where(low, top, pltpu.roll(bottom, HALF, 1))
    return jnp.where(low, pltpu.roll(top, HALF, 1), bottom)


def unpack(first, second):
    low = low_lanes(8)
    top = jnp.where(low, first, pltpu.roll(second, HALF, 1))
    bottom = jnp.where(low, pltpu.roll(first, HALF, 1), second)
    return jnp.concatenate([top, bottom], axis=0)


def rows_of_half(x):
    both = jnp.stack([x[:, :, :HALF], x[:, :, HALF:]], axis=1)
    return both.reshape(ROW, HALF)


def packed_half(x):
    both = x.reshape(CTX, 2, 8, HALF)
    return jnp.concatenate([both[:, 0], both[:, 1]], axis=-1)


def running_rows(decay):
    upper = (iota((T, T), 0) <= iota((T, T), 1)).astype(BF16)
    return sum(dot(part, upper, 1, 0) for part in split3(decay))


def running_columns(decay):
    lower = (iota((T, T), 1) <= iota((T, T), 0)).astype(BF16)
    return sum(dot(lower, part, 1, 1) for part in split3(decay))


def masking(column, row):
    extent = row.shape[1]
    causal = iota((extent, extent), 0) >= iota((extent, extent), 1)
    return jnp.where(causal, jnp.exp(jnp.where(causal, column - row, 0.0)), 0.0)


def column_to_row(column):
    extent = column.shape[0]
    eye = iota((extent, max(extent, D)), 0) == iota((extent, max(extent, D)), 1)
    return jnp.sum(jnp.where(eye, column, 0.0), axis=0, keepdims=True)


def row_to_column(row, extent):
    eye = iota((extent, row.shape[1]), 0) == iota((extent, row.shape[1]), 1)
    return jnp.sum(jnp.where(eye, row, 0.0), axis=1, keepdims=True)


def live_tokens(lengths):
    return lax.axis_index("ctx") * T + iota((T, 1), 0) < lengths[0]


def second_core():
    return lax.axis_index("ctx") % 2 == 1


def in_order(mine, other):
    second = second_core()
    return jnp.where(second, other, mine), jnp.where(second, mine, other)


def choose(first, last):
    return in_order(first, last)


def start_copies(pairs, sems):
    copies = [pltpu.make_async_copy(source, target, sems.at[i]) for i, (source, target) in enumerate(pairs)]
    for copy in copies:
        copy.start()
    return copies


def send_kernel(
    lengths, key, value, decay, prompt_query, prompt_key, prompt_value, prompt_decay,
    mine, theirs, query_out, key_out, value_out,
    key_in, value_in, decay_in, query_in, prompt_key_in, prompt_value_in, prompt_decay_in,
    rows_k, rows_v, prompt_q, prompt_k, prompt_v, sems,
):
    copies = start_copies(
        [
            (decay, decay_in),
            (prompt_decay, prompt_decay_in),
            (prompt_query, query_in),
            (prompt_key, prompt_key_in),
            (prompt_value, prompt_value_in),
            (value, value_in),
            (key, key_in),
        ],
        sems,
    )
    live = live_tokens(lengths)
    for copy in copies[:5]:
        copy.wait()
    columns = running_columns(decay_in[0])
    to_end = jnp.exp(columns[T - 1 : T, :] - columns)
    wide = jnp.concatenate([prompt_decay_in[...], jnp.zeros((HEADS, D - PT), F32)], axis=1)
    totals = jnp.sum(decay_in[0], axis=1, keepdims=True)
    at = iota((8, D), 0)
    prompt_q[...] = query_in[...].astype(F32).reshape(PT * HEADS, D)
    prompt_k[...] = prompt_key_in[...].astype(F32).reshape(PT * HEADS, D)
    prompt_v[...] = prompt_value_in[...].astype(F32).reshape(PT * HEADS, D)
    for h in range(HEADS):
        tail = jnp.where(at == 0, wide[h : h + 1], jnp.where(at == 1, totals[h : h + 1], 0.0))
        query_out[h] = prompt_q[pl.ds(h, PT, HEADS), :]
        k = prompt_k[pl.ds(h, PT, HEADS), :]
        v = prompt_v[pl.ds(h, PT, HEADS), :]
        for ref, half in zip((mine, theirs), choose(pack(v, 0), pack(v, 1))):
            ref[h, 64:80, :] = k
            ref[h, 80:88, :] = half
            ref[h, 88:96, :] = tail
    for copy in copies[5:]:
        copy.wait()
    rows_v[...] = value_in[0].astype(F32).reshape(T * HEADS, D)
    rows_k[...] = key_in[0].astype(F32).reshape(T * HEADS, D)
    for h in range(HEADS):
        k = jnp.where(live, rows_k[pl.ds(h, T, HEADS), :], 0.0)
        v = jnp.where(live, rows_v[pl.ds(h, T, HEADS), :], 0.0).astype(BF16)
        key_out[h] = k.astype(BF16)
        value_out[h] = v
        state = dot_right(v, k * to_end[:, h : h + 1], 0, 0)
        for ref, half in zip((mine, theirs), choose(state[0:64], state[64:128])):
            ref[h, 0:64, :] = half


def reply_masks_kernel(weights, value, decay, after_fold, mask_out, local_out, to_end_out):
    del after_fold
    lines = running_rows(decay[0])
    columns = running_columns(decay[0])
    to_end_out[...] = wide_columns(jnp.exp(columns[T - 1 : T, :] - columns))
    for h in range(HEADS):
        mask_out[h] = masking(columns[:, h : h + 1], lines[h : h + 1])
        local_out[h] = dot(weights[h], value[h], 1, 0)


def merge_kernel(mine, other, query, out, first_out, totals_out):
    at = iota((8, D), 0)
    for h in range(HEADS):
        first, last = in_order(mine[h], other[h])
        totals_out[h : h + 1, :] = first[89:90]
        totals_out[HEADS + h : HEADS + h + 1, :] = last[89:90]
        first_out[h] = first[0:64]
        out[h, 0:64, :] = jnp.exp(last[89:90]) * first[0:64] + last[0:64]
        out[h, 64:80, :] = first[64:80]
        out[h, 80:96, :] = last[64:80]
        out[h, 96:104, :] = first[80:88]
        out[h, 104:112, :] = last[80:88]
        tile = jnp.where(at == 0, first[88:89], jnp.where(at == 1, first[89:90], 0.0))
        out[h, 112:120, :] = jnp.where(at == 2, last[88:89], jnp.where(at == 3, last[89:90], tile))
        out[h, 120:136, :] = query[h]


def wide_columns(columns):
    return jnp.concatenate([columns, jnp.zeros((T, D - HEADS), F32)], axis=1)


def reply_local_kernel(
    lengths, query, grad, key, decay, gain, prompt_grad,
    query_out, grad_out, weights_out, growth_out, scale_out, upstream_out,
    query_in, grad_in, rows, rows_g, prompt_rows, sems,
):
    copies = start_copies([(query, query_in), (grad, grad_in)], sems)
    live = live_tokens(lengths)
    lines = running_rows(decay[0])
    columns = running_columns(decay[0])
    growth_out[...] = wide_columns(jnp.exp(columns))
    scale = gain[...].astype(F32)
    scale_out[...] = scale
    prompt_rows[...] = prompt_grad[...].astype(F32).reshape(PT * HEADS, D)
    for h in range(HEADS):
        upstream_out[h] = prompt_rows[pl.ds(h, PT, HEADS), :] * scale[h : h + 1]
    for copy in copies:
        copy.wait()
    rows[...] = query_in[0].astype(F32).reshape(T * HEADS, D)
    rows_g[...] = grad_in[0].astype(F32).reshape(T * HEADS, D)
    for h in range(HEADS):
        q = jnp.where(live, rows[pl.ds(h, T, HEADS), :], 0.0).astype(BF16)
        query_out[h] = q
        mask = masking(columns[:, h : h + 1], lines[h : h + 1])
        weights_out[h] = (dot(q, key[h], 1, 1) * mask).astype(BF16)
        grad_out[h] = jnp.where(live, rows_g[pl.ds(h, T, HEADS), :], 0.0).astype(BF16)


def prompt_row_kernel(received, out, column_out, query_out, blocks_out):
    decay = jnp.concatenate([received[:, 112, :], received[:, 114, :]], axis=0)
    token_block, token_place = iota((ROW, CTX), 0) // PT, iota((ROW, D), 0) % PT
    at = iota((ROW, CTX), 1)
    block = jnp.where(at < CHIPS, 2 * at, 2 * (at - CHIPS) + 1)
    parts = split3(decay)
    own = sum(dot((block == token_block).astype(BF16), part, 1, 0) for part in parts)
    before = sum(dot((block < token_block).astype(BF16), part, 1, 0) for part in parts)
    running = jnp.sum(before + jnp.where(iota((ROW, D), 1) <= token_place, own, 0.0), axis=1, keepdims=True)
    last = running[ROW - 1 : ROW]
    k = received[:, 64:96, :].reshape(ROW, D)
    v = rows_of_half(received[:, 96:112, :].reshape(CTX, 8, D)).astype(BF16)
    state = dot_right(v, k * jnp.exp(last - running), 0, 0)
    total = jnp.broadcast_to(last, (8, D))
    for s in range(SAMPLE):
        out[s, 0:64, :] = state
        out[s, 64:72, :] = total
    column_out[...] = jnp.broadcast_to(running, (ROW, D))
    query_out[...] = received[:, 120:136, :]
    blocks_out[...] = received[:, 113, :] + received[:, 115, :]


def same_block():
    return iota((ROW, ROW), 0) // PT == iota((ROW, ROW), 1) // PT


def prompt_weights(q, k, mask):
    scores = dot(q, k, 1, 1) * mask
    high = scores.astype(BF16)
    low = jnp.where(same_block(), 0.0, scores - high.astype(F32)).astype(BF16)
    return high, low


def prompt_local_kernel(
    received, other, column, query_out, key_out, value_out, line_out, local_out
):
    both = in_order(received[:, 120:136, :], other[...])
    q = jnp.concatenate(both, axis=1).reshape(ROW, D).astype(BF16)
    k = received[:, 64:96, :].reshape(ROW, D).astype(BF16)
    v = rows_of_half(received[:, 96:112, :].reshape(CTX, 8, D)).astype(BF16)
    running = column[:, 0:1]
    line = column_to_row(running)
    query_out[...] = q
    key_out[...] = k
    value_out[...] = v
    line_out[...] = jnp.broadcast_to(line, (8, ROW))
    weights = prompt_weights(q, k, masking(running, line))
    local_out[...] = sum(dot(part, v, 1, 0) for part in weights)


def fold_kernel(
    rows_received, received, blocks, query, local, column, after_reply, out, start_out, factors_out
):
    del after_reply
    place = lax.axis_index("sample")
    totals = [rows_received[s, 64:65, :] for s in range(SAMPLE)]
    end = jnp.zeros((HALF, D), F32)
    start = end
    for s in range(SAMPLE):
        start = jnp.where(place == s, end, start)
        end = jnp.exp(totals[s]) * end + rows_received[s, 0:64, :]
    start_out[...] = start
    state = end
    for y in range(CHIPS):
        out[y, 0:64, :] = state
        state = jnp.exp(blocks[y : y + 1, :]) * state + received[y, 0:64, :]
    outputs = local[...] + jnp.exp(column[:, 0:1]) * dot_right(query[...], start, 1, 1)
    out[:, 64:80, :] = packed_half(outputs).reshape(CHIPS, PT, D)
    for s in range(SAMPLE):
        after = jnp.zeros((1, D), F32)
        between = after
        for other in range(s + 1, SAMPLE):
            after = after + totals[other]
            between = between + jnp.where(other < place, totals[other], 0.0)
        factors_out[s : s + 1, :] = jnp.exp(after)
        factors_out[SAMPLE + s : SAMPLE + s + 1, :] = jnp.where(place > s, jnp.exp(between), 0.0)


def spread_kernel(received, first_state, totals, mine, theirs):
    for h in range(HEADS):
        before = received[h, 0:64, :]
        after = jnp.exp(totals[h : h + 1, :]) * before + first_state[h]
        mine[h, 0:64, :], theirs[h, 0:64, :] = choose(before, after)
        mine[h, 64:72, :], theirs[h, 64:72, :] = choose(received[h, 64:72, :], received[h, 72:80, :])


def output_kernel(
    mine, other, query, local, grad, growth, scale, prompt_upstream, out, output_out, prompt_out
):
    squares = jnp.zeros((T, D), F32)
    crossed = jnp.zeros((T, D), F32)
    prompt_squares = jnp.zeros((PT, D), F32)
    prompt_crossed = jnp.zeros((PT, D), F32)
    for h in range(HEADS):
        low, high = in_order(mine[h], other[h])
        state = jnp.concatenate([low[0:64], high[0:64]], axis=0)
        outputs = local[h] + growth[:, h : h + 1] * dot_right(query[h], state, 1, 1)
        output_out[h] = outputs
        upstream = grad[h].astype(F32) * scale[h : h + 1, :]
        squares = squares + outputs * outputs
        crossed = crossed + upstream * outputs
        outputs = unpack(low[64:72], high[64:72])
        prompt_out[h] = outputs
        prompt_squares = prompt_squares + outputs * outputs
        prompt_crossed = prompt_crossed + prompt_upstream[h] * outputs
    sums = [
        column_to_row(jnp.sum(part, axis=1, keepdims=True))
        for part in (squares, crossed, prompt_squares, prompt_crossed)
    ]
    at = iota((8, D), 0)
    tile = jnp.zeros((8, D), F32)
    for i, part in enumerate(sums):
        tile = jnp.where(at == i, part, tile)
    for x in range(HEAD_AXIS):
        out[x] = tile


def norm_terms(squares, crossed):
    inverse = lax.rsqrt(squares / FEATURES + EPSILON)
    return inverse, crossed * inverse * inverse / FEATURES


def grad_kernel(
    sums, outputs, prompt_outputs, query, grad, growth, scale, prompt_upstream, mine, theirs, grad_out
):
    total = sums[0] + sums[1] + sums[2] + sums[3]
    inverse, project = norm_terms(row_to_column(total[0:1], T), row_to_column(total[1:2], T))
    prompt_inverse, prompt_project = norm_terms(row_to_column(total[2:3], PT), row_to_column(total[3:4], PT))
    for h in range(HEADS):
        upstream = grad[h].astype(F32) * scale[h : h + 1, :]
        out_grad = ((upstream - outputs[h] * project) * inverse).astype(BF16)
        grad_out[h] = out_grad
        back = dot_right(out_grad, query[h].astype(F32) * growth[:, h : h + 1], 0, 0)
        prompt_out_grad = (prompt_upstream[h] - prompt_outputs[h] * prompt_project) * prompt_inverse
        prompt_out_grad = prompt_out_grad.astype(BF16).astype(F32)
        mine[h, 0:64, :], theirs[h, 0:64, :] = choose(back[0:64], back[64:128])
        mine[h, 64:72, :], theirs[h, 64:72, :] = choose(pack(prompt_out_grad, 0), pack(prompt_out_grad, 1))


def back_merge_kernel(mine, other, totals, after_reply, out, last_out):
    del after_reply
    for h in range(HEADS):
        first, last = in_order(mine[h], other[h])
        last_out[h] = last[0:64]
        out[h, 0:64, :] = first[0:64] + jnp.exp(totals[h : h + 1, :]) * last[0:64]
        out[h, 64:72, :] = first[64:72]
        out[h, 72:80, :] = last[64:72]


def reply_back_kernel(
    mine, other, out_grad, query, key, value, weights, masks, growth, query_grad, key_local, value_local
):
    for h in range(HEADS):
        state = jnp.concatenate(in_order(mine[h, 0:64, :], other[h, 0:64, :]), axis=0)
        og = out_grad[h]
        mix = (dot(og, value[h], 1, 1) * masks[h]).astype(BF16)
        query_grad[h] = dot(mix, key[h], 1, 0) + growth[:, h : h + 1] * dot_right(og, state, 1, 0)
        key_local[h] = dot(mix, query[h], 0, 0)
        value_local[h] = dot(weights[h], og, 0, 0)


def back_fold_kernel(received, blocks, factors, query, column, rows_out):
    adjoint = jnp.zeros((HALF, D), F32)
    for y in range(CHIPS - 1, -1, -1):
        adjoint = jnp.exp(blocks[y : y + 1, :]) * adjoint + received[y, 0:64, :]
    og = rows_of_half(received[:, 64:80, :].reshape(CTX, 8, D)).astype(BF16)
    back = dot_right(og, query[...].astype(F32) * jnp.exp(column[:, 0:1]), 0, 0)
    for s in range(SAMPLE):
        rows_out[s] = factors[s : s + 1, :] * adjoint + factors[SAMPLE + s : SAMPLE + s + 1, :] * back


def prompt_mid_kernel(
    received, blocks, start, query, key, value, column, line, reply_query, out, swap_out, reply_query_grad, rows
):
    for h in range(HEADS):
        rows[pl.ds(h, T, HEADS), :] = reply_query[h]
    reply_query_grad[0] = rows[...].reshape(T, HEADS, D).astype(BF16)
    adjoint = jnp.zeros((HALF, D), F32)
    for y in range(CHIPS - 1, -1, -1):
        out[y, 0:64, :] = adjoint
        adjoint = jnp.exp(blocks[y : y + 1, :]) * adjoint + received[y, 0:64, :]
    og = rows_of_half(received[:, 64:80, :].reshape(CTX, 8, D)).astype(BF16)
    running = column[:, 0:1]
    mask = masking(running, line[0:1, :])
    mix = split(dot(og, value[...], 1, 1) * mask)
    k, q = key[...], query[...]
    query_grad = sum(dot(part, k, 1, 0) for part in mix) + jnp.exp(running) * dot_right(og, start[...], 1, 0)
    query_grad = query_grad.reshape(CHIPS, 2 * PT, D)
    key_local = sum(dot(part, q, 0, 0) for part in mix)
    value_local = sum(dot(part, og, 0, 0) for part in prompt_weights(q, k, mask))
    out[:, 64:96, :] = key_local.reshape(CHIPS, 2 * PT, D)
    out[:, 96:112, :] = packed_half(value_local).reshape(CHIPS, PT, D)
    out[:, 112:128, :], swap_out[...] = choose(query_grad[:, 0:PT], query_grad[:, PT:])


def prompt_back_kernel(rows_received, swapped, key, value, column, message, out):
    adjoint = rows_received[0]
    for s in range(1, SAMPLE):
        adjoint = adjoint + rows_received[s]
    running = column[:, 0:1]
    to_end = jnp.exp(running[ROW - 1 : ROW] - running)
    key_grad = to_end * dot_right(value[...], adjoint, 1, 0)
    value_grad = to_end * dot_right(key[...], adjoint, 1, 1)
    out[:, 0:64, :] = message[:, 0:64, :]
    out[:, 64:96, :] = message[:, 64:96, :] + key_grad.reshape(CHIPS, 2 * PT, D)
    out[:, 96:112, :] = message[:, 96:112, :] + packed_half(value_grad).reshape(CHIPS, PT, D)
    out[:, 112:128, :] = message[:, 112:128, :] + swapped[...]


def back_spread_kernel(received, last_back, totals, mine, theirs):
    for h in range(HEADS):
        after = received[h, 0:64, :]
        before = jnp.exp(totals[HEADS + h : HEADS + h + 1, :]) * after + last_back[h]
        mine[h, 0:64, :], theirs[h, 0:64, :] = choose(before, after)
        mine[h, 64:80, :], theirs[h, 64:80, :] = choose(received[h, 64:80, :], received[h, 80:96, :])
        mine[h, 80:88, :], theirs[h, 80:88, :] = choose(received[h, 96:104, :], received[h, 104:112, :])


def end_kernel(
    received, mine, other, key, value, key_local, value_local, to_end,
    key_grad, value_grad, prompt_query_grad, prompt_key_grad, prompt_value_grad,
    rows_k, rows_v, prompt_q, prompt_k, prompt_v,
):
    for h in range(HEADS):
        low, high = in_order(mine[h], other[h])
        adjoint = jnp.concatenate([low[0:64], high[0:64]], axis=0)
        scale = to_end[:, h : h + 1]
        rows_k[pl.ds(h, T, HEADS), :] = key_local[h] + scale * dot_right(value[h], adjoint, 1, 0)
        rows_v[pl.ds(h, T, HEADS), :] = value_local[h] + scale * dot_right(key[h], adjoint, 1, 1)
        prompt_k[pl.ds(h, PT, HEADS), :] = low[64:80] + high[64:80]
        prompt_v[pl.ds(h, PT, HEADS), :] = unpack(low[80:88], high[80:88])
        prompt_q[pl.ds(h, PT, HEADS), :] = received[h, 112:128, :]
    key_grad[0] = rows_k[...].reshape(T, HEADS, D).astype(BF16)
    value_grad[0] = rows_v[...].reshape(T, HEADS, D).astype(BF16)
    prompt_query_grad[...] = prompt_q[...].reshape(PT, HEADS, D).astype(BF16)
    prompt_key_grad[...] = prompt_k[...].reshape(PT, HEADS, D).astype(BF16)
    prompt_value_grad[...] = prompt_v[...].reshape(PT, HEADS, D).astype(BF16)


VMEM = pl.BlockSpec(memory_space=pltpu.VMEM)
SMEM = pl.BlockSpec(memory_space=pltpu.SMEM)
HBM = pl.BlockSpec(memory_space=pltpu.HBM)
REPLY_ROWS = pltpu.VMEM((T * HEADS, D), F32)
PROMPT_ROWS = pltpu.VMEM((PT * HEADS, D), F32)
BY_HEAD = ((HEADS, T, D), BF16)
BY_HEAD_WIDE = ((HEADS, T, D), F32)
REPLY = ((1, T, HEADS, D), BF16)
PROMPT = ((PT, HEADS, D), BF16)


def run(kernel, outs, scratch, *operands, hbm=(), kept=(), flops=0):
    operands = [
        pltpu.with_memory_space_constraint(operand, pltpu.HBM) if i in hbm else operand
        for i, operand in enumerate(operands)
    ]
    specs = [
        SMEM if operand.dtype == jnp.int32 else HBM if i in hbm else VMEM for i, operand in enumerate(operands)
    ]
    moved = sum(operand.size * operand.dtype.itemsize for operand in operands)
    return pl.pallas_call(
        kernel,
        out_shape=[
            pltpu.VMEM(shape, kind) if i in kept else jax.ShapeDtypeStruct(shape, kind)
            for i, (shape, kind) in enumerate(outs)
        ],
        in_specs=specs,
        out_specs=[VMEM] * len(outs),
        scratch_shapes=scratch,
        compiler_params=pltpu.CompilerParams(vmem_limit_bytes=8 * 1024 * 1024),
        cost_estimate=pl.CostEstimate(flops=flops, bytes_accessed=2 * moved, transcendentals=0),
        name=kernel.__name__,
    )(*operands)


def exchange(x, axis):
    return lax.all_to_all(x, axis, 0, 0, tiled=True)


def exchange_chips(x):
    groups = [[2 * chip + core for chip in range(CHIPS)] for core in range(2)]
    return lax.all_to_all(x, "ctx", 0, 0, axis_index_groups=groups, tiled=True)


def swap_cores(x):
    return lax.ppermute(x, "ctx", [(i, i ^ 1) for i in range(CTX)])


def shards(
    prompt_query,
    prompt_key,
    prompt_value,
    prompt_grad,
    prompt_decay,
    reply_query,
    reply_key,
    reply_value,
    reply_grad,
    reply_decay,
    reply_lengths,
    norm_gain,
):
    work = 8 * 2 * T * D * D
    reply_in, prompt_in = pltpu.VMEM(*REPLY), pltpu.VMEM(*PROMPT)
    mine, theirs, own_query, key, value = run(
        send_kernel,
        [((HEADS, 96, D), F32), ((HEADS, 96, D), F32), ((HEADS, PT, D), F32), BY_HEAD, BY_HEAD],
        [reply_in, reply_in, pltpu.VMEM((1, HEADS, T), F32)]
        + [prompt_in] * 3
        + [pltpu.VMEM((HEADS, PT), F32)]
        + [REPLY_ROWS] * 2
        + [PROMPT_ROWS] * 3
        + [pltpu.SemaphoreType.DMA((7,))],
        reply_lengths,
        reply_key,
        reply_value,
        reply_decay,
        prompt_query,
        prompt_key,
        prompt_value,
        prompt_decay,
        hbm=range(1, 8),
        flops=2 * work,
        kept=(0, 2, 3, 4),
    )
    sent, first_state, block_totals = run(
        merge_kernel,
        [((HEADS, 136, D), F32), ((HEADS, HALF, D), F32), ((2 * HEADS, D), F32)],
        [],
        mine,
        swap_cores(theirs),
        own_query,
        kept=(1, 2),
    )
    first = exchange_chips(sent)
    sent, column, half_query, blocks = run(
        prompt_row_kernel,
        [((SAMPLE, 72, D), F32), ((ROW, D), F32), ((CHIPS, PT, D), F32), ((CHIPS, D), F32)],
        [],
        first,
        kept=(1, 3),
    )
    rows = exchange(sent, "sample")
    query, grad, weights, growth, scale, prompt_upstream = run(
        reply_local_kernel,
        [BY_HEAD, BY_HEAD, BY_HEAD, ((T, D), F32), ((HEADS, D), F32), ((HEADS, PT, D), F32)],
        [reply_in, reply_in, REPLY_ROWS, REPLY_ROWS, PROMPT_ROWS, pltpu.SemaphoreType.DMA((2,))],
        reply_lengths,
        reply_query,
        reply_grad,
        key,
        reply_decay,
        norm_gain,
        prompt_grad,
        hbm=(1, 2),
        flops=2 * work,
        kept=range(6),
    )
    row_query, row_key, row_value, line, row_local = run(
        prompt_local_kernel,
        [
            ((ROW, D), BF16),
            ((ROW, D), BF16),
            ((ROW, HALF), BF16),
            ((8, ROW), F32),
            ((ROW, HALF), F32),
        ],
        [],
        first,
        swap_cores(half_query),
        column,
        flops=work,
        kept=range(5),
    )
    sent, start, factors = run(
        fold_kernel,
        [((CHIPS, 80, D), F32), ((HALF, D), F32), ((2 * SAMPLE, D), F32)],
        [],
        rows,
        first,
        blocks,
        row_query,
        row_local,
        column,
        scale,
        kept=(1, 2),
    )
    mine, theirs = run(
        spread_kernel,
        [((HEADS, 72, D), F32), ((HEADS, 72, D), F32)],
        [],
        exchange_chips(sent),
        first_state,
        block_totals,
        kept=(0,),
    )
    other = swap_cores(theirs)
    masks, local, to_end = run(
        reply_masks_kernel,
        [BY_HEAD_WIDE, BY_HEAD_WIDE, ((T, D), F32)],
        [],
        weights,
        value,
        reply_decay,
        mine,
        flops=work,
        kept=(0, 1, 2),
    )
    sent, outputs, prompt_outputs = run(
        output_kernel,
        [((HEAD_AXIS, 8, D), F32), BY_HEAD_WIDE, ((HEADS, PT, D), F32)],
        [],
        mine,
        other,
        query,
        local,
        grad,
        growth,
        scale,
        prompt_upstream,
        flops=2 * work,
        kept=(1, 2),
    )
    sums = exchange(sent, "head")
    back_mine, back_theirs, out_grad = run(
        grad_kernel,
        [((HEADS, 72, D), F32), ((HEADS, 72, D), F32), BY_HEAD],
        [],
        sums,
        outputs,
        prompt_outputs,
        query,
        grad,
        growth,
        scale,
        prompt_upstream,
        flops=2 * work,
        kept=(0, 2),
    )
    back_other = swap_cores(back_theirs)
    reply_query_wide, key_local, value_local = run(
        reply_back_kernel,
        [BY_HEAD_WIDE, BY_HEAD_WIDE, BY_HEAD_WIDE],
        [],
        mine,
        other,
        out_grad,
        query,
        key,
        value,
        weights,
        masks,
        growth,
        flops=6 * work,
        kept=(0, 1, 2),
    )
    sent, last_back = run(
        back_merge_kernel,
        [((HEADS, 80, D), F32), ((HEADS, HALF, D), F32)],
        [],
        back_mine,
        back_other,
        block_totals,
        reply_query_wide,
        kept=(1,),
    )
    backs = exchange_chips(sent)
    (sent,) = run(
        back_fold_kernel,
        [((SAMPLE, HALF, D), F32)],
        [],
        backs,
        blocks,
        factors,
        row_query,
        column,
    )
    rows = exchange(sent, "sample")
    message, swap, reply_query_grad = run(
        prompt_mid_kernel,
        [((CHIPS, 128, D), F32), ((CHIPS, PT, D), F32), REPLY],
        [REPLY_ROWS],
        backs,
        blocks,
        start,
        row_query,
        row_key,
        row_value,
        column,
        line,
        reply_query_wide,
        flops=work,
        kept=(0,),
    )
    (sent,) = run(
        prompt_back_kernel,
        [((CHIPS, 128, D), F32)],
        [],
        rows,
        swap_cores(swap),
        row_key,
        row_value,
        column,
        message,
    )
    received = exchange_chips(sent)
    end_mine, end_theirs = run(
        back_spread_kernel,
        [((HEADS, 88, D), F32), ((HEADS, 88, D), F32)],
        [],
        received,
        last_back,
        block_totals,
        kept=(0,),
    )
    reply_key_grad, reply_value_grad, prompt_query_grad, prompt_key_grad, prompt_value_grad = run(
        end_kernel,
        [REPLY, REPLY, PROMPT, PROMPT, PROMPT],
        [REPLY_ROWS] * 2 + [PROMPT_ROWS] * 3,
        received,
        end_mine,
        swap_cores(end_theirs),
        key,
        value,
        key_local,
        value_local,
        to_end,
        flops=4 * work,
    )
    return (
        prompt_query_grad,
        prompt_key_grad,
        prompt_value_grad,
        reply_query_grad,
        reply_key_grad,
        reply_value_grad,
    )


def solution(mesh):
    prompt = P(("sample", "ctx"), "head", None)
    reply = P("sample", "ctx", "head", None)
    in_specs = (
        (prompt,) * 4
        + (P("head", ("sample", "ctx")),)
        + (reply,) * 4
        + (P("sample", "head", "ctx"), P("sample"), P("head", None))
    )
    out_specs = (prompt,) * 3 + (reply,) * 3
    return jax.shard_map(shards, mesh=mesh, in_specs=in_specs, out_specs=out_specs, check_vma=False)
```
